128 devices in a mesh: tx: 8 (over y_lo, x), ty: 16 (over y_hi, z, core).
Axes of the slice: x: 4, y: 4 (y_hi: 2, y_lo: 2; y = y_hi * 2 + y_lo), z: 4, core: 2. Of those that a mesh axis runs over, the one named last changes fastest.
Arguments:
- far_adjoint: bfloat16 [2, 4096, 8192], P(None, 'tx', 'ty'), may hold values from -6 to 6
- pillar: float32 [4096, 8192], P('tx', 'ty'), may hold values from -1 to 1
- green_blocks: bfloat16 [8, 2, 256, 256], replicated, may hold values from -0.09375 to 0.09375
- pair_src: int32 [8, 16, 24576], P('tx', 'ty'), may hold values from 0 to 1023, as said below
- pair_dst: int32 [8, 16, 24576], P('tx', 'ty'), may hold values from 0 to 3135, as said below
- group_end: int32 [8, 16, 8], P('tx', 'ty'), may hold values from 0 to 24576, as said below
- w_in: float32 [64, 9], replicated, may hold values from -2 to 2
- b_in: float32 [64], replicated, may hold values from -3 to 3
- w_out: float32 [2, 64], replicated, may hold values from -0.75 to 0.75
Outputs:
- grad_pillar: float32 [4096, 8192], P('tx', 'ty')
- grad_w_in: float32 [64, 9], replicated
- grad_b_in: float32 [64], replicated
- grad_w_out: float32 [2, 64], replicated
The draws below stay inside these ranges and needn't reach their ends.
Inputs may be any that keep to these rules, and one draw needn't show every extreme that they name: `pair_src`: the source block of each slot, numbered row by row over the tile's 32 x 32 blocks. `pair_dst`: the target block of each slot, numbered row by row over the tile's blocks extended by 12 blocks on every side (56 to a row); it lies at most 12 blocks from the slot's source block along each dimension. `group_end`: per tile, nondecreasing ends of the runs of slots that use Green's blocks 0 to 7 in order; the last is the tile's number of live pairs, 3072 or more, and some tile has all 24576 slots live.
All inputs are finite; a program needn't handle non-finite values.
Results may differ from the reference program's by a relative error of at most 0.0003.
Values may be sent and summed in bfloat16 or wider, within the bound.
A program may use at most 128 MiB of HBM per device.

```python
import jax
import jax.numpy as jnp
from jax import lax

CX = 512
CY = 512
SLOTS = 24576
BLK = 16
BB = 256
CONE = 12
NG = 8
HID = 64
NBX = 32
NBY = 32
NX = 4096
NY = 8192
N_TX = 8
N_TY = 16


def slot_pairs(key):
    key_src, key_off, key_pick = jax.random.split(jax.random.fold_in(key, 21), 3)
    slot_shape = (N_TX, N_TY, SLOTS)
    sources = jax.random.randint(key_src, slot_shape, 0, NBX * NBY)
    shift_x = jax.random.randint(jax.random.fold_in(key_off, 1), slot_shape, -CONE, CONE + 1)
    shift_y = jax.random.randint(jax.random.fold_in(key_off, 2), slot_shape, -CONE, CONE + 1)
    chosen = jax.random.randint(key_pick, (N_TX, N_TY, 1), 0, SLOTS // 8)
    partner = (chosen + 1) % (SLOTS // 8)
    slot_ids = jnp.arange(SLOTS, dtype=jnp.int32)[None, None, :]
    at_high = slot_ids == chosen
    at_low = slot_ids == partner
    sources = jnp.where(at_high, NBX * NBY - 1, jnp.where(at_low, 0, sources))
    shift_x = jnp.where(at_high, CONE, jnp.where(at_low, -CONE, shift_x))
    shift_y = jnp.where(at_high, CONE, jnp.where(at_low, -CONE, shift_y))
    block_x = sources // NBY
    block_y = sources % NBY
    targets = (block_x + CONE + shift_x) * (NBY + 2 * CONE) + block_y + CONE + shift_y
    return (sources.astype(jnp.int32), targets.astype(jnp.int32))


def draw_pair_src(key, part):
    return slot_pairs(key)[0]


def draw_pair_dst(key, part):
    return slot_pairs(key)[1]


def draw_group_end(key, part):
    key = jax.random.fold_in(key, 7)
    key_x, key_y, key_jit, key_wts = jax.random.split(key, 4)
    centre_x = jax.random.randint(key_x, (), 0, N_TX)
    centre_y = jax.random.randint(key_y, (), 0, N_TY)
    tile_x = jnp.arange(N_TX, dtype=jnp.int32)[:, None]
    tile_y = jnp.arange(N_TY, dtype=jnp.int32)[None, :]
    distance = jnp.maximum(jnp.abs(tile_x - centre_x), jnp.abs(tile_y - centre_y))
    capped = jnp.minimum(distance, 4)
    jitter = jax.random.randint(key_jit, (N_TX, N_TY), 0, SLOTS // 16 + 1)
    jitter = jnp.where(distance > 0, jitter, 0)
    live_count = SLOTS - 3 * SLOTS // 4 * capped // 4 - jitter
    weights = jax.random.randint(key_wts, (N_TX, N_TY, NG), 1, 9)
    running = jnp.cumsum(weights, axis=2)
    return (live_count[:, :, None] * running // running[:, :, -1:]).astype(jnp.int32)


def level_of(own_key, extent, cuts, low, top_value):
    loudness, own = 1.0, jax.random.fold_in(own_key, 6)
    for position, blocks in cuts:
        draws = jnp.exp(jax.random.uniform(jax.random.fold_in(own, position), (blocks,), jnp.float32, low / len(cuts), top_value / len(cuts)))
        loudness = loudness * jnp.repeat(draws, extent[position] // blocks).reshape([-1 if axis == position else 1 for axis in range(len(extent))])
    return loudness


def noise(key, dims, scale, bound, cuts=(), kind=jnp.bfloat16):
    values = jax.random.normal(key, dims, jnp.float32) * scale
    if len(cuts) > 0:
        values = level_of(key, dims, cuts, -0.22, 0.18) * values
    return jnp.clip(values, min=-bound, max=bound).astype(kind)


def setup_inputs(seed: int = 0) -> dict:
    key_list = jax.random.split(jax.random.key(seed), 10)
    far_adjoint = noise(key_list[0], (2, NX, NY), 1.0, 6.0, ((1, 8), (2, 16)))
    pillar = jnp.clip(jax.random.uniform(key_list[1], (NX, NY), jnp.float32, -1.0, 1.0) * level_of(key_list[1], (NX, NY), ((0, 8), (1, 16)), -0.4, 0.0), -1.0, 1.0)
    green_blocks = noise(key_list[2], (NG, 2, BB, BB), (16 * BB) ** -0.5, 0.09375)
    pair_src = draw_pair_src(jax.random.fold_in(key_list[9], 71), 0)
    pair_dst = draw_pair_dst(jax.random.fold_in(key_list[9], 71), 0)
    group_end = draw_group_end(jax.random.fold_in(key_list[9], 71), 0)
    w_in = noise(key_list[6], (HID, 9), 9 ** -0.5, 2.0, (), jnp.float32)
    b_in = noise(key_list[7], (HID,), 0.5, 3.0, (), jnp.float32)
    w_out = noise(key_list[8], (2, HID), HID ** -0.5, 0.75, (), jnp.float32)
    return dict(far_adjoint=far_adjoint, pillar=pillar, green_blocks=green_blocks, pair_src=pair_src, pair_dst=pair_dst, group_end=group_end, w_in=w_in, b_in=b_in, w_out=w_out)


highest = lax.Precision.HIGHEST


def green_stack(green_table):
    real_part = green_table[:, 0]
    imag_part = green_table[:, 1]
    upper_half = jnp.concatenate([real_part, -imag_part], axis=2)
    lower_half = jnp.concatenate([imag_part, real_part], axis=2)
    return jnp.concatenate([upper_half, lower_half], axis=1)


def to_blocks(grid_data, block_side):
    channels, extent_x, extent_y = grid_data.shape
    reshaped = grid_data.reshape(channels, extent_x // block_side, block_side, extent_y // block_side, block_side)
    reshaped = reshaped.transpose(1, 3, 0, 2, 4)
    return reshaped.reshape((extent_x // block_side) * (extent_y // block_side), channels * block_side * block_side)


def from_blocks(blocks, extent_x, extent_y, block_side):
    reshaped = blocks.reshape(extent_x // block_side, extent_y // block_side, 2, block_side, block_side)
    return reshaped.transpose(2, 0, 3, 1, 4).reshape(2, extent_x, extent_y)


def grouped_adjoint(ext_blocks, sources, targets, run_ends, lower_slot, upper_slot, stacks, block_count):
    piece_rows = min(768, sources.shape[0])
    filler = jnp.zeros((piece_rows,), jnp.int32)
    padded_src = jnp.concatenate([sources, filler])
    padded_dst = jnp.concatenate([targets, filler])
    run_starts = jnp.concatenate([jnp.zeros((1,), jnp.int32), run_ends[:-1]])
    offsets = jnp.arange(piece_rows, dtype=jnp.int32)
    summed = jnp.zeros((block_count, stacks.shape[2]), jnp.float32)
    for group_index in range(stacks.shape[0]):
        first_row = jnp.clip(run_starts[group_index], lower_slot, upper_slot)
        stop_row = jnp.clip(run_ends[group_index], lower_slot, upper_slot)
        piece_count = (stop_row - first_row + piece_rows - 1) // piece_rows

        def one_piece(piece_index, running, group_index=group_index, first_row=first_row, stop_row=stop_row):
            start_row = first_row + piece_index * piece_rows
            piece_src = lax.dynamic_slice_in_dim(padded_src, start_row, piece_rows)
            piece_dst = lax.dynamic_slice_in_dim(padded_dst, start_row, piece_rows)
            live_rows = (start_row + offsets) < stop_row
            gathered = jnp.where(live_rows[:, None], ext_blocks[piece_dst], jnp.zeros((), ext_blocks.dtype))
            product = jnp.dot(gathered.astype(jnp.float32), stacks[group_index].astype(jnp.float32),
                              precision=highest, preferred_element_type=jnp.float32)
            return running.at[piece_src].add(product)

        summed = lax.fori_loop(0, piece_count, one_piece, summed)
    return summed


def cell_pass(pillar_band, near_band, w_in, b_in, w_out):
    band_x = near_band.shape[1]
    band_y = near_band.shape[2]
    feats = jnp.stack([pillar_band[1 + shift_x:1 + shift_x + band_x, 1 + shift_y:1 + shift_y + band_y]
                       for shift_x in (-1, 0, 1) for shift_y in (-1, 0, 1)])
    hidden = jnp.tanh(jnp.einsum("ks,sij->kij", w_in, feats, precision=highest) + b_in[:, None, None])
    pulled = jnp.einsum("ck,cij->kij", w_out, near_band, precision=highest)
    slope_hidden = pulled * (1.0 - hidden * hidden)
    slopes = jnp.einsum("ks,kij->sij", w_in, slope_hidden, precision=highest)
    return feats, hidden, slope_hidden, slopes


def region_sums(feats, hidden, slope_hidden, near_band, margin):
    end_x = near_band.shape[1] - margin
    end_y = near_band.shape[2] - margin
    feats_cut = feats[:, margin:end_x, margin:end_y]
    hidden_cut = hidden[:, margin:end_x, margin:end_y]
    slope_cut = slope_hidden[:, margin:end_x, margin:end_y]
    near_cut = near_band[:, margin:end_x, margin:end_y]
    grad_in = jnp.einsum("kij,sij->ks", slope_cut, feats_cut, precision=highest)
    grad_bias = jnp.sum(slope_cut, axis=(1, 2))
    grad_out = jnp.einsum("cij,kij->ck", near_cut, hidden_cut, precision=highest)
    return grad_in, grad_bias, grad_out


def combine_slopes(slopes):
    band_x = slopes.shape[1] - 2
    band_y = slopes.shape[2] - 2
    summed = jnp.zeros((band_x, band_y), jnp.float32)
    for shift_x in (-1, 0, 1):
        for shift_y in (-1, 0, 1):
            index = 3 * (shift_x + 1) + (shift_y + 1)
            summed = summed + slopes[index, 1 - shift_x:1 - shift_x + band_x, 1 - shift_y:1 - shift_y + band_y]
    return summed


def reference(far_adjoint, pillar, green_blocks, pair_src, pair_dst, group_end, w_in, b_in, w_out):
    rim_cells = CONE * BLK
    stacks = green_stack(green_blocks)
    padded_far = jnp.pad(far_adjoint, ((0, 0), (rim_cells, rim_cells), (rim_cells, rim_cells)))
    tile_total = N_TX * N_TY
    block_count = (CX // BLK) * (CY // BLK)

    def tile_work(packed):
        tile_index, sources, targets, run_ends = packed
        start_x = (tile_index // N_TY) * CX
        start_y = (tile_index % N_TY) * CY
        extended = lax.dynamic_slice(padded_far, (jnp.int32(0), start_x.astype(jnp.int32), start_y.astype(jnp.int32)),
                                     (2, CX + 2 * rim_cells, CY + 2 * rim_cells))
        ext_blocks = to_blocks(extended, BLK)
        summed = grouped_adjoint(ext_blocks, sources, targets, run_ends, 0, SLOTS, stacks, block_count)
        return from_blocks(summed, CX, CY, BLK)

    near_tiles = lax.map(tile_work, (jnp.arange(tile_total, dtype=jnp.int32),
                                     pair_src.reshape(tile_total, SLOTS),
                                     pair_dst.reshape(tile_total, SLOTS),
                                     group_end.reshape(tile_total, NG)))
    near = near_tiles.reshape(N_TX, N_TY, 2, CX, CY).transpose(2, 0, 3, 1, 4).reshape(2, NX, NY)

    band_rows = min(32, CX)
    padded_pillar = jnp.pad(pillar, 2)
    padded_near = jnp.pad(near, ((0, 0), (1, 1), (1, 1)))

    def band_work(band_index):
        start_x = (band_index * band_rows).astype(jnp.int32)
        pillar_band = lax.dynamic_slice(padded_pillar, (start_x, jnp.int32(0)), (band_rows + 4, NY + 4))
        near_band = lax.dynamic_slice(padded_near, (jnp.int32(0), start_x, jnp.int32(0)), (2, band_rows + 2, NY + 2))
        feats, hidden, slope_hidden, slopes = cell_pass(pillar_band, near_band, w_in, b_in, w_out)
        return combine_slopes(slopes), region_sums(feats, hidden, slope_hidden, near_band, 1)

    grad_rows, band_sums = lax.map(band_work, jnp.arange(NX // band_rows, dtype=jnp.int32))
    grad_pillar = grad_rows.reshape(NX, NY)
    scale = float(NX * NY) ** -0.5
    grad_w_in = jnp.sum(band_sums[0], axis=0) * scale
    grad_b_in = jnp.sum(band_sums[1], axis=0) * scale
    grad_w_out = jnp.sum(band_sums[2], axis=0) * scale
    return (grad_pillar, grad_w_in, grad_b_in, grad_w_out)
```

```python
import functools

import jax
import jax.numpy as jnp
from jax import lax
from jax.experimental import pallas as pl
from jax.experimental.pallas import tpu as pltpu
from jax.sharding import PartitionSpec as P

BLK = 16
CONE = 12
SIDE = 512
NB = SIDE // BLK
EXT = NB + 2 * CONE
GROUPS = 8
CHUNK = 512
UNROLL = 32
HIDDEN = 64
PADROWS = 16
SROWS = 24
VMEM_BYTES = 60 * 1024 * 1024

f32 = jnp.float32
bf16 = jnp.bfloat16


def swap_pieces(v):
    sub = lax.broadcasted_iota(jnp.int32, (8, 128), 0)
    lane = lax.broadcasted_iota(jnp.int32, (8, 128), 1) // 16
    for d in (1, 2, 4):
        low_s = (sub & d) == 0
        low_l = (lane & d) == 0
        up = pltpu.roll(pltpu.roll(v, 8 - d, 0), 16 * d, 1)
        if d == 4:
            down = up
        else:
            down = pltpu.roll(pltpu.roll(v, d, 0), 128 - 16 * d, 1)
        v = jnp.where(low_s == low_l, v, jnp.where(low_s, up, down))
    return v


def block_kernel(far_ref, out_ref, flat):
    def row(r, carry):
        for c in range(2):
            strip = far_ref[c, pl.ds(pl.multiple_of(r * BLK, BLK), BLK), :].astype(f32)
            for xh in range(2):
                for t in range(SIDE // 128):
                    v = swap_pieces(strip[8 * xh : 8 * xh + 8, 128 * t : 128 * t + 128])
                    flat[pl.ds(32 * t + 2 * c + xh, 8, stride=4), :] = v
        out_ref[pl.ds(pl.multiple_of(r * 128, 128), 128), :] = flat[...].astype(bf16)
        return carry

    lax.fori_loop(0, NB, row, 0)


def to_block_table(far):
    return pl.pallas_call(
        block_kernel,
        out_shape=jax.ShapeDtypeStruct((NB * NB * 4, 128), bf16),
        in_specs=[pl.BlockSpec(memory_space=pltpu.VMEM)],
        out_specs=pl.BlockSpec(memory_space=pltpu.VMEM),
        scratch_shapes=[pltpu.VMEM((128, 128), f32)],
        compiler_params=pltpu.CompilerParams(vmem_limit_bytes=VMEM_BYTES),
        name="to_blocks",
    )(far)


def sparse_kernel(
    dst_ref, ends_ref, src_ref, ext_ref, green_ref, near_ref, table, rows, rows16, seg, acc
):
    def widen(i, carry):
        at = pl.ds(pl.multiple_of(i * 128, 128), 128)
        table[at, :] = ext_ref[at, :].astype(f32)
        return carry

    lax.fori_loop(0, EXT * EXT * 4 // 128, widen, 0)
    acc[...] = jnp.zeros_like(acc)

    def group(k, carry):
        start = jnp.where(k == 0, 0, ends_ref[jnp.maximum(k - 1, 0)])
        stop = ends_ref[k]
        seg[...] = jnp.zeros_like(seg)

        def chunk(c, inner):
            base = c * CHUNK

            def gather(i, deep):
                for j in range(UNROLL):
                    q = i * UNROLL + j
                    d = pl.multiple_of(dst_ref[base + q], 4)
                    rows[pl.ds(pl.multiple_of(q * 4, 4), 4), :] = table[pl.ds(d, 4), :]
                return deep

            lax.fori_loop(0, CHUNK // UNROLL, gather, 0)
            for j in range(4):
                rows16[:, 128 * j : 128 * j + 128] = rows[
                    pl.ds(j, CHUNK, stride=4), :
                ].astype(bf16)
            slot = base + lax.broadcasted_iota(jnp.int32, (1, CHUNK), 1)
            live = (slot >= start) & (slot < stop)
            source = jnp.where(live, src_ref[c], -1)
            for m in range(4):
                ids = lax.broadcasted_iota(jnp.int32, (256, CHUNK), 0) + 256 * m
                hot = jnp.where(ids == source, 1.0, 0.0).astype(bf16)
                seg[256 * m : 256 * m + 256, :] += jnp.dot(
                    hot, rows16[...], preferred_element_type=f32
                )
            return inner

        lax.fori_loop(start // CHUNK, (stop + CHUNK - 1) // CHUNK, chunk, 0)

        def apply(m, inner):
            at = pl.ds(pl.multiple_of(m * 256, 256), 256)
            value = seg[at, :]
            high = value.astype(bf16)
            low = (value - high.astype(f32)).astype(bf16)
            acc[at, :] += jnp.dot(high, green_ref[k], preferred_element_type=f32) + jnp.dot(
                low, green_ref[k], preferred_element_type=f32
            )
            return inner

        lax.fori_loop(0, 4, apply, 0)
        return carry

    lax.fori_loop(0, GROUPS, group, 0)

    def lay(r, carry):
        for t in range(SIDE // 128):
            for c in range(2):
                for xh in range(2):
                    j = 2 * c + xh
                    v = acc[
                        pl.ds(pl.multiple_of(r * 32 + 8 * t, 8), 8), 128 * j : 128 * j + 128
                    ]
                    near_ref[
                        c,
                        pl.ds(pl.multiple_of(r * 16 + 8 * xh + PADROWS, 8), 8),
                        128 * t : 128 * t + 128,
                    ] = swap_pieces(v)
        return carry

    lax.fori_loop(0, NB, lay, 0)
    for c in range(2):
        near_ref[c, 0:PADROWS, :] = jnp.zeros((PADROWS, SIDE), f32)
        near_ref[c, PADROWS + SIDE : 2 * PADROWS + SIDE, :] = jnp.zeros((PADROWS, SIDE), f32)


def sparse_near(targets, ends, sources, ext, stacks):
    slots = targets.shape[0]
    return pl.pallas_call(
        sparse_kernel,
        out_shape=jax.ShapeDtypeStruct((2, SIDE + 2 * PADROWS, SIDE), f32),
        in_specs=[
            pl.BlockSpec(memory_space=pltpu.SMEM),
            pl.BlockSpec(memory_space=pltpu.SMEM),
            pl.BlockSpec(memory_space=pltpu.VMEM),
            pl.BlockSpec(memory_space=pltpu.VMEM),
            pl.BlockSpec(memory_space=pltpu.VMEM),
        ],
        out_specs=pl.BlockSpec(memory_space=pltpu.VMEM),
        scratch_shapes=[
            pltpu.VMEM((EXT * EXT * 4, 128), f32),
            pltpu.VMEM((CHUNK * 4, 128), f32),
            pltpu.VMEM((CHUNK, 512), bf16),
            pltpu.VMEM((NB * NB, 512), f32),
            pltpu.VMEM((NB * NB, 512), f32),
        ],
        compiler_params=pltpu.CompilerParams(vmem_limit_bytes=VMEM_BYTES),
        name="sparse_near",
    )(targets * 4, ends, sources.reshape(slots // CHUNK, 1, CHUNK), ext, stacks)


def split2(value):
    high = value.astype(bf16).astype(f32)
    return high, value - high


def put(ref, start, stride, value):
    for t in range(SIDE // 128):
        ref[t, pl.ds(start, 8, stride=stride), :] = value[:, 128 * t : 128 * t + 128]


def take(ref, start, stride):
    tiles = [ref[t, pl.ds(start, 8, stride=stride), :] for t in range(SIDE // 128)]
    return jnp.concatenate(tiles, 1)


def cell_kernel(
    p3_ref, near_ref, w1_ref, v_ref, grad_ref, west_ref, east_ref, sums_ref, q32, qs, gs, ps, total
):
    width = SIDE

    def build(i, carry):
        r0 = pl.multiple_of(i * 8, 8)
        for b in range(3):
            x = p3_ref[b, pl.ds(r0, 8), :]
            x1, rest = split2(x)
            x2, x3 = split2(rest)
            for n, piece in enumerate((x1, x1, x2, x2, x3)):
                put(q32, b * 5 + n, 16, piece)
        put(q32, 15, 16, jnp.ones((8, width), f32))
        for t in range(4):
            qs[pl.ds(r0, 8), :, 128 * t : 128 * t + 128] = (
                q32[t].astype(bf16).reshape(8, 16, 128)
            )
        return carry

    lax.fori_loop(0, (SIDE + 8) // 8, build, 0)
    total[...] = jnp.zeros_like(total)
    gs[...] = jnp.zeros_like(gs)
    zero_rows = jnp.zeros((PADROWS * SROWS, 128), f32)
    for t in range(4):
        ps[t, 0 : PADROWS * SROWS, :] = zero_rows
        ps[t, (PADROWS + SIDE) * SROWS : (2 * PADROWS + SIDE) * SROWS, :] = zero_rows

    def strip(i, carry):
        r0 = pl.multiple_of(i * 8, 8)
        n = [near_ref[c, pl.ds(pl.multiple_of(r0 + PADROWS, 8), 8), :] for c in range(2)]
        deep = [p3_ref[b, pl.ds(r0, 16), :] for b in range(3)]
        for a in range(3):
            for b in range(3):
                feat = deep[b][a : a + 8]
                for c in range(2):
                    put(gs, 10 * c + 3 * a + b, SROWS, n[c] * feat)
        for c in range(2):
            put(gs, 10 * c + 9, SROWS, n[c])
        for half in range(2):
            left, right = [], []
            for j in range(4 * half, 4 * half + 4):
                feats = qs[pl.ds(r0 + j, 3)].reshape(48, width)
                h = jnp.tanh(jnp.dot(w1_ref[...], feats, preferred_element_type=f32))
                u = 1.0 - h * h
                u1 = u.astype(bf16)
                u2 = (u - u1.astype(f32)).astype(bf16)
                h1 = h.astype(bf16)
                h2 = (h - h1.astype(f32)).astype(bf16)
                slope = jnp.dot(
                    v_ref[...], jnp.concatenate([u1, u2, u1], 0), preferred_element_type=f32
                )
                at = pl.ds(pl.multiple_of((r0 + PADROWS + j) * SROWS, 8), SROWS)
                for t in range(4):
                    ps[t, at, :] = slope[:SROWS, 128 * t : 128 * t + 128]
                g = jnp.concatenate(
                    [gs[t, SROWS * j : SROWS * j + SROWS, :] for t in range(4)], 1
                )
                g1, g2 = split2(g)
                left.append(jnp.concatenate([u1, u2, h1, h2], 0))
                right.append(jnp.concatenate([g1, g2], 0).astype(bf16))
            total[...] += lax.dot_general(
                jnp.concatenate(left, 1),
                jnp.concatenate(right, 1),
                (((1,), (1,)), ((), ())),
                preferred_element_type=f32,
            )
        return carry

    lax.fori_loop(0, SIDE // 8, strip, 0)
    sums_ref[...] = total[...]

    lane = lax.broadcasted_iota(jnp.int32, (8, width), 1)

    def combine(i, carry):
        parts = []
        deep = [near_ref[c, pl.ds(pl.multiple_of(i * 8, 8), 24), :] for c in range(2)]
        for b in range(3):
            acc = None
            for a in range(3):
                x0 = i * 8 + 9 - a
                for c in range(2):
                    term = deep[c][9 - a : 17 - a] * take(
                        ps, x0 * SROWS + 9 * c + 3 * a + b, SROWS
                    )
                    acc = term if acc is None else acc + term
            parts.append(acc)
        low = jnp.where(lane == width - 1, 0.0, pltpu.roll(parts[0], width - 1, 1))
        high = jnp.where(lane == 0, 0.0, pltpu.roll(parts[2], 1, 1))
        at = pl.ds(pl.multiple_of(i * 8, 8), 8)
        grad_ref[at, :] = parts[1] + low + high
        west_ref[at, :] = parts[0][:, 0:128]
        east_ref[at, :] = parts[2][:, width - 128 : width]
        return carry

    lax.fori_loop(0, SIDE // 8 + 2, combine, 0)


def cell_model(p3, near, first, back):
    rows = SIDE + 16
    return pl.pallas_call(
        cell_kernel,
        out_shape=[
            jax.ShapeDtypeStruct((rows, SIDE), f32),
            jax.ShapeDtypeStruct((rows, 128), f32),
            jax.ShapeDtypeStruct((rows, 128), f32),
            jax.ShapeDtypeStruct((4 * HIDDEN, 2 * SROWS), f32),
        ],
        in_specs=[pl.BlockSpec(memory_space=pltpu.VMEM)] * 4,
        out_specs=[pl.BlockSpec(memory_space=pltpu.VMEM)] * 4,
        scratch_shapes=[
            pltpu.VMEM((4, 128, 128), f32),
            pltpu.VMEM((SIDE + 8, 16, SIDE), bf16),
            pltpu.VMEM((4, 8 * SROWS, 128), f32),
            pltpu.VMEM((4, (SIDE + 2 * PADROWS) * SROWS, 128), f32),
            pltpu.VMEM((4 * HIDDEN, 2 * SROWS), f32),
        ],
        compiler_params=pltpu.CompilerParams(vmem_limit_bytes=VMEM_BYTES),
        name="cell_model",
    )(p3, near, first, back)


def neighbours(axis):
    count = lax.axis_size(axis)
    up = [(i, i + 1) for i in range(count - 1)]
    return up, [(j, i) for i, j in up]


def with_halo(shard, sides):
    for axis, dim, size in sides:
        up, down = neighbours(axis)
        length = shard.shape[dim]
        before = lax.ppermute(
            lax.slice_in_dim(shard, length - size, length, axis=dim), axis, up
        )
        after = lax.ppermute(lax.slice_in_dim(shard, 0, size, axis=dim), axis, down)
        shard = jnp.concatenate([before, shard, after], axis=dim)
    return shard


def green_stack(green_table):
    real_part = green_table[:, 0]
    imag_part = green_table[:, 1]
    upper_half = jnp.concatenate([real_part, -imag_part], axis=2)
    lower_half = jnp.concatenate([imag_part, real_part], axis=2)
    return jnp.concatenate([upper_half, lower_half], axis=1)


def rounded(value):
    return lax.reduce_precision(value, 8, 7)


def first_weights(w_in, b_in):
    w = w_in.reshape(HIDDEN, 3, 3)
    w1 = rounded(w)
    w2 = rounded(w - w1)
    b1 = rounded(b_in)
    b2 = rounded(b_in - b1)
    b3 = b_in - b1 - b2
    cells = jnp.stack([w1, w2, w1, w2, w1], 3).reshape(HIDDEN, 3, 15)
    bias = jnp.stack([b1, b2, b3], 1)[:, :, None]
    return jnp.concatenate([cells, bias], 2).reshape(HIDDEN, 48).astype(bf16)


def back_weights(w_in, w_out):
    v = (w_in.T[None] * w_out[:, None, :]).reshape(18, HIDDEN)
    v1 = rounded(v)
    v2 = v - v1
    both = jnp.concatenate([v1, v1, v2], 1)
    return jnp.pad(both, ((0, 14), (0, 0))).astype(bf16)


def local(far_adjoint, pillar, green_blocks, pair_src, pair_dst, group_end, w_in, b_in, w_out):
    own = to_block_table(far_adjoint).reshape(NB, NB // 4, 16, 128)
    ext = with_halo(own, (("tx", 0, CONE), ("ty", 1, CONE // 4)))
    ext = ext.reshape(EXT * EXT * 4, 128)
    near = sparse_near(
        pair_dst.reshape(-1), group_end.reshape(-1), pair_src.reshape(-1), ext,
        green_stack(green_blocks),
    )
    wide = with_halo(pillar, (("tx", 0, 1), ("ty", 1, 1)))
    wide = jnp.pad(wide, ((0, 6), (0, 0)))
    p3 = jnp.stack([wide[:, b : b + SIDE] for b in range(3)])
    grad, west, east, sums = cell_model(
        p3, near, first_weights(w_in, b_in), back_weights(w_in, w_out)
    )
    grad = exchange_edges(grad, west, east)
    both = sums.reshape(2, 2, HIDDEN, 2, SROWS).sum((1, 3))
    back = both[0]
    grad_in = w_out[0][:, None] * back[:, 0:10] + w_out[1][:, None] * back[:, 10:20]
    packed = jnp.concatenate([grad_in, both[1][:, 9:10], both[1][:, 19:20]], 1)
    count = lax.axis_size("tx") * lax.axis_size("ty")
    scale = float(SIDE * SIDE * count) ** (-0.5)
    packed = lax.psum(packed, ("tx", "ty")) * scale
    return grad, packed[:, 0:9], packed[:, 9], packed[:, 10:12].T


def exchange_edges(grad, west, east):
    up, down = neighbours("tx")
    def line(row):
        return jnp.concatenate([west[row, 0:1], grad[row], east[row, 127:128]])
    from_below = lax.ppermute(line(7), "tx", down)
    from_above = lax.ppermute(line(SIDE + 8), "tx", up)
    core = grad[8 : SIDE + 8]
    core = core.at[SIDE - 1].add(from_below[1 : SIDE + 1]).at[0].add(from_above[1 : SIDE + 1])
    left = west[8 : SIDE + 8, 0]
    left = left.at[SIDE - 1].add(from_below[0]).at[0].add(from_above[0])
    right = east[8 : SIDE + 8, 127]
    right = right.at[SIDE - 1].add(from_below[SIDE + 1]).at[0].add(from_above[SIDE + 1])
    up, down = neighbours("ty")
    from_right = lax.ppermute(left, "ty", down)
    from_left = lax.ppermute(right, "ty", up)
    return core.at[:, SIDE - 1].add(from_right).at[:, 0].add(from_left)


def solution(mesh):
    return jax.shard_map(
        local,
        mesh=mesh,
        in_specs=(
            P(None, "tx", "ty"),
            P("tx", "ty"),
            P(),
            P("tx", "ty", None),
            P("tx", "ty", None),
            P("tx", "ty", None),
            P(),
            P(),
            P(),
        ),
        out_specs=(P("tx", "ty"), P(), P(), P()),
        check_vma=False,
    )
```

```python
import functools

import jax
import jax.numpy as jnp
from jax import lax
from jax.experimental import pallas as pl
from jax.experimental.pallas import tpu as pltpu
from jax.sharding import PartitionSpec as P

BLK = 16
CONE = 12
SIDE = 512
NB = SIDE // BLK
EXT = NB + 2 * CONE
GROUPS = 8
CHUNK = 512
UNROLL = 32
HIDDEN = 64
PADROWS = 16
SROWS = 24
VMEM_BYTES = 60 * 1024 * 1024

f32 = jnp.float32
bf16 = jnp.bfloat16
MESH = pl.DeviceIdType.MESH


def swap_pieces(v):
    sub = lax.broadcasted_iota(jnp.int32, (8, 128), 0)
    lane = lax.broadcasted_iota(jnp.int32, (8, 128), 1) // 16
    for d in (1, 2, 4):
        low_s = (sub & d) == 0
        low_l = (lane & d) == 0
        up = pltpu.roll(pltpu.roll(v, 8 - d, 0), 16 * d, 1)
        if d == 4:
            down = up
        else:
            down = pltpu.roll(pltpu.roll(v, d, 0), 128 - 16 * d, 1)
        v = jnp.where(low_s == low_l, v, jnp.where(low_s, up, down))
    return v


def block_kernel(far_ref, out_ref, flat):
    def row(r, carry):
        for c in range(2):
            strip = far_ref[c, pl.ds(pl.multiple_of(r * BLK, BLK), BLK), :].astype(f32)
            for xh in range(2):
                for t in range(SIDE // 128):
                    v = swap_pieces(strip[8 * xh : 8 * xh + 8, 128 * t : 128 * t + 128])
                    flat[pl.ds(32 * t + 2 * c + xh, 8, stride=4), :] = v
        out_ref[pl.ds(pl.multiple_of(r * 128, 128), 128), :] = flat[...].astype(bf16)
        return carry

    lax.fori_loop(0, NB, row, 0)


def to_block_table(far):
    return pl.pallas_call(
        block_kernel,
        out_shape=jax.ShapeDtypeStruct((NB * NB * 4, 128), bf16),
        in_specs=[pl.BlockSpec(memory_space=pltpu.VMEM)],
        out_specs=pl.BlockSpec(memory_space=pltpu.VMEM),
        scratch_shapes=[pltpu.VMEM((128, 128), f32)],
        compiler_params=pltpu.CompilerParams(vmem_limit_bytes=VMEM_BYTES),
        name="to_blocks",
    )(far)


def sparse_kernel(
    dst_ref, ends_ref, src_ref, ext_ref, green_ref, near_ref, table, rows, rows16, seg, acc
):
    def widen(i, carry):
        at = pl.ds(pl.multiple_of(i * 128, 128), 128)
        table[at, :] = ext_ref[at, :].astype(f32)
        return carry

    lax.fori_loop(0, EXT * EXT * 4 // 128, widen, 0)
    acc[...] = jnp.zeros_like(acc)

    def group(k, carry):
        start = jnp.where(k == 0, 0, ends_ref[jnp.maximum(k - 1, 0)])
        stop = ends_ref[k]
        seg[...] = jnp.zeros_like(seg)

        def chunk(c, inner):
            base = c * CHUNK

            def gather(i, deep):
                for j in range(UNROLL):
                    q = i * UNROLL + j
                    d = pl.multiple_of(dst_ref[base + q], 4)
                    rows[pl.ds(pl.multiple_of(q * 4, 4), 4), :] = table[pl.ds(d, 4), :]
                return deep

            lax.fori_loop(0, CHUNK // UNROLL, gather, 0)
            for j in range(4):
                rows16[:, 128 * j : 128 * j + 128] = rows[
                    pl.ds(j, CHUNK, stride=4), :
                ].astype(bf16)
            slot = base + lax.broadcasted_iota(jnp.int32, (1, CHUNK), 1)
            live = (slot >= start) & (slot < stop)
            source = jnp.where(live, src_ref[c], -1)
            for m in range(4):
                ids = lax.broadcasted_iota(jnp.int32, (256, CHUNK), 0) + 256 * m
                hot = jnp.where(ids == source, 1.0, 0.0).astype(bf16)
                seg[256 * m : 256 * m + 256, :] += jnp.dot(
                    hot, rows16[...], preferred_element_type=f32
                )
            return inner

        lax.fori_loop(start // CHUNK, (stop + CHUNK - 1) // CHUNK, chunk, 0)

        def apply(m, inner):
            at = pl.ds(pl.multiple_of(m * 256, 256), 256)
            value = seg[at, :]
            high = value.astype(bf16)
            low = (value - high.astype(f32)).astype(bf16)
            acc[at, :] += jnp.dot(high, green_ref[k], preferred_element_type=f32) + jnp.dot(
                low, green_ref[k], preferred_element_type=f32
            )
            return inner

        lax.fori_loop(0, 4, apply, 0)
        return carry

    lax.fori_loop(0, GROUPS, group, 0)

    def lay(r, carry):
        for t in range(SIDE // 128):
            for c in range(2):
                for xh in range(2):
                    j = 2 * c + xh
                    v = acc[
                        pl.ds(pl.multiple_of(r * 32 + 8 * t, 8), 8), 128 * j : 128 * j + 128
                    ]
                    near_ref[
                        c,
                        pl.ds(pl.multiple_of(r * 16 + 8 * xh + PADROWS, 8), 8),
                        128 * t : 128 * t + 128,
                    ] = swap_pieces(v)
        return carry

    lax.fori_loop(0, NB, lay, 0)
    for c in range(2):
        near_ref[c, 0:PADROWS, :] = jnp.zeros((PADROWS, SIDE), f32)
        near_ref[c, PADROWS + SIDE : 2 * PADROWS + SIDE, :] = jnp.zeros((PADROWS, SIDE), f32)


def sparse_near(targets, ends, sources, ext, stacks):
    slots = targets.shape[0]
    return pl.pallas_call(
        sparse_kernel,
        out_shape=jax.ShapeDtypeStruct((2, SIDE + 2 * PADROWS, SIDE), f32),
        in_specs=[
            pl.BlockSpec(memory_space=pltpu.SMEM),
            pl.BlockSpec(memory_space=pltpu.SMEM),
            pl.BlockSpec(memory_space=pltpu.VMEM),
            pl.BlockSpec(memory_space=pltpu.VMEM),
            pl.BlockSpec(memory_space=pltpu.VMEM),
        ],
        out_specs=pl.BlockSpec(memory_space=pltpu.VMEM),
        scratch_shapes=[
            pltpu.VMEM((EXT * EXT * 4, 128), f32),
            pltpu.VMEM((CHUNK * 4, 128), f32),
            pltpu.VMEM((CHUNK, 512), bf16),
            pltpu.VMEM((NB * NB, 512), f32),
            pltpu.VMEM((NB * NB, 512), f32),
        ],
        compiler_params=pltpu.CompilerParams(vmem_limit_bytes=VMEM_BYTES),
        name="sparse_near",
    )(targets * 4, ends, sources.reshape(slots // CHUNK, 1, CHUNK), ext, stacks)


def split2(value):
    high = value.astype(bf16).astype(f32)
    return high, value - high


def put(ref, start, stride, value):
    for t in range(SIDE // 128):
        ref[t, pl.ds(start, 8, stride=stride), :] = value[:, 128 * t : 128 * t + 128]


def take(ref, start, stride):
    tiles = [ref[t, pl.ds(start, 8, stride=stride), :] for t in range(SIDE // 128)]
    return jnp.concatenate(tiles, 1)


def cell_kernel(
    p3_ref,
    near_ref,
    w1_ref,
    v_ref,
    wout_ref,
    grad_ref,
    west_ref,
    east_ref,
    sums_ref,
    q32,
    qs,
    gs,
    ps,
    total,
    nh,
):
    width = SIDE

    def build(i, carry):
        r0 = pl.multiple_of(i * 8, 8)
        for b in range(3):
            x = p3_ref[b, pl.ds(r0, 8), :]
            x1, rest = split2(x)
            x2, x3 = split2(rest)
            for n, piece in enumerate((x1, x1, x2, x2, x3)):
                put(q32, b * 5 + n, 16, piece)
        put(q32, 15, 16, jnp.ones((8, width), f32))
        for t in range(4):
            qs[pl.ds(r0, 8), :, 128 * t : 128 * t + 128] = (
                q32[t].astype(bf16).reshape(8, 16, 128)
            )
        return carry

    lax.fori_loop(0, (SIDE + 8) // 8, build, 0)
    total[...] = jnp.zeros_like(total)
    nh[...] = jnp.zeros_like(nh)
    gs[...] = jnp.zeros_like(gs)
    zero_rows = jnp.zeros((PADROWS * SROWS, 128), f32)
    for t in range(4):
        ps[t, 0 : PADROWS * SROWS, :] = zero_rows
        ps[t, (PADROWS + SIDE) * SROWS : (2 * PADROWS + SIDE) * SROWS, :] = zero_rows

    def strip(i, carry):
        r0 = pl.multiple_of(i * 8, 8)
        n = [near_ref[c, pl.ds(pl.multiple_of(r0 + PADROWS, 8), 8), :] for c in range(2)]
        deep = [p3_ref[b, pl.ds(r0, 16), :] for b in range(3)]
        for a in range(3):
            for b in range(3):
                feat = deep[b][a : a + 8]
                for c in range(2):
                    put(gs, 10 * c + 3 * a + b, SROWS, n[c] * feat)
        for c in range(2):
            put(gs, 10 * c + 9, SROWS, n[c])
        for half in range(2):
            left, right = [], []
            partial = [None, None]
            feats = qs[pl.ds(r0 + 4 * half, 6)].reshape(96, width)
            h = jnp.tanh(jnp.dot(w1_ref[...], feats, preferred_element_type=f32))
            for pair in range(2):
                pieces = []
                for r in range(2 * pair, 2 * pair + 2):
                    j = 4 * half + r
                    hr = h[HIDDEN * r : HIDDEN * r + HIDDEN]
                    u = 1.0 - hr * hr
                    u1 = u.astype(bf16)
                    u2 = (u - u1.astype(f32)).astype(bf16)
                    pieces += [u1, u2]
                    for c in range(2):
                        for t in range(4):
                            tile = slice(128 * t, 128 * t + 128)
                            term = n[c][j : j + 1, tile] * hr[:, tile]
                            partial[c] = term if partial[c] is None else partial[c] + term
                    g = jnp.concatenate(
                        [gs[t, SROWS * j : SROWS * j + SROWS, :] for t in range(4)], 1
                    )
                    g1, g2 = split2(g)
                    left.append(jnp.concatenate([u1, u2], 0))
                    right.append(jnp.concatenate([g1, g2], 0).astype(bf16))
                slope = jnp.dot(
                    v_ref[...], jnp.concatenate(pieces, 0), preferred_element_type=f32
                )
                for r in range(2):
                    j = 4 * half + 2 * pair + r
                    one = (
                        slope[2 * SROWS * r : 2 * SROWS * r + SROWS]
                        + slope[2 * SROWS * r + SROWS : 2 * SROWS * r + 2 * SROWS]
                    )
                    at = pl.ds(pl.multiple_of((r0 + PADROWS + j) * SROWS, 8), SROWS)
                    for t in range(4):
                        ps[t, at, :] = one[:, 128 * t : 128 * t + 128]
            total[:, 0 : 2 * SROWS] += lax.dot_general(
                jnp.concatenate(left, 1),
                jnp.concatenate(right, 1),
                (((1,), (1,)), ((), ())),
                preferred_element_type=f32,
            )
            for c in range(2):
                nh[HIDDEN * c : HIDDEN * c + HIDDEN, :] += partial[c]
        return carry

    lax.fori_loop(0, SIDE // 8, strip, 0)
    turned = total[...].T
    turned = turned + pltpu.roll(turned, HIDDEN, 1)
    pulled = turned[0:SROWS] + turned[SROWS : 2 * SROWS]
    first = wout_ref[0:1, :] * pulled[0:10] + wout_ref[1:2, :] * pulled[10:20]
    second = jnp.sum(nh[...].T, axis=0, keepdims=True)
    sums_ref[...] = jnp.zeros_like(sums_ref)
    sums_ref[0:10, :] = first
    sums_ref[10:11, :] = second

    lane = lax.broadcasted_iota(jnp.int32, (8, width), 1)

    def combine(i, carry):
        parts = []
        deep = [near_ref[c, pl.ds(pl.multiple_of(i * 8, 8), 24), :] for c in range(2)]
        for b in range(3):
            acc = None
            for a in range(3):
                x0 = i * 8 + 9 - a
                for c in range(2):
                    term = deep[c][9 - a : 17 - a] * take(
                        ps, x0 * SROWS + 9 * c + 3 * a + b, SROWS
                    )
                    acc = term if acc is None else acc + term
            parts.append(acc)
        low = jnp.where(lane == width - 1, 0.0, pltpu.roll(parts[0], width - 1, 1))
        high = jnp.where(lane == 0, 0.0, pltpu.roll(parts[2], 1, 1))
        at = pl.ds(pl.multiple_of(i * 8, 8), 8)
        grad_ref[at, :] = parts[1] + low + high
        west_ref[at, :] = parts[0][:, 0:128]
        east_ref[at, :] = parts[2][:, width - 128 : width]
        return carry

    lax.fori_loop(0, SIDE // 8 + 2, combine, 0)


def cell_model(p3, near, first, back, out_weights):
    rows = SIDE + 16
    return pl.pallas_call(
        cell_kernel,
        out_shape=[
            jax.ShapeDtypeStruct((rows, SIDE), f32),
            jax.ShapeDtypeStruct((rows, 128), f32),
            jax.ShapeDtypeStruct((rows, 128), f32),
            jax.ShapeDtypeStruct((16, 128), f32),
        ],
        in_specs=[pl.BlockSpec(memory_space=pltpu.VMEM)] * 5,
        out_specs=[pl.BlockSpec(memory_space=pltpu.VMEM)] * 4,
        scratch_shapes=[
            pltpu.VMEM((4, 128, 128), f32),
            pltpu.VMEM((SIDE + 8, 16, SIDE), bf16),
            pltpu.VMEM((4, 8 * SROWS, 128), f32),
            pltpu.VMEM((4, (SIDE + 2 * PADROWS) * SROWS, 128), f32),
            pltpu.VMEM((128, 128), f32),
            pltpu.VMEM((128, 128), f32),
        ],
        compiler_params=pltpu.CompilerParams(vmem_limit_bytes=VMEM_BYTES),
        name="cell_model",
    )(p3, near, first, back, out_weights)


def neighbours(axis):
    count = lax.axis_size(axis)
    up = [(i, i + 1) for i in range(count - 1)]
    return up, [(j, i) for i, j in up]


def with_halo(shard, sides):
    for axis, dim, size in sides:
        up, down = neighbours(axis)
        length = shard.shape[dim]
        before = lax.ppermute(
            lax.slice_in_dim(shard, length - size, length, axis=dim), axis, up
        )
        after = lax.ppermute(lax.slice_in_dim(shard, 0, size, axis=dim), axis, down)
        shard = jnp.concatenate([before, shard, after], axis=dim)
    return shard


def green_stack(green_table):
    real_part = green_table[:, 0]
    imag_part = green_table[:, 1]
    upper_half = jnp.concatenate([real_part, -imag_part], axis=2)
    lower_half = jnp.concatenate([imag_part, real_part], axis=2)
    return jnp.concatenate([upper_half, lower_half], axis=1)


def rounded(value):
    return lax.reduce_precision(value, 8, 7)


def first_weights(w_in, b_in):
    w = w_in.reshape(HIDDEN, 3, 3)
    w1 = rounded(w)
    w2 = rounded(w - w1)
    b1 = rounded(b_in)
    b2 = rounded(b_in - b1)
    b3 = b_in - b1 - b2
    cells = jnp.stack([w1, w2, w1, w2, w1], 3).reshape(HIDDEN, 3, 15)
    bias = jnp.stack([b1, b2, b3], 1)[:, :, None]
    one = jnp.concatenate([cells, bias], 2).reshape(HIDDEN, 48)
    return jnp.concatenate(
        [jnp.pad(one, ((0, 0), (16 * r, 48 - 16 * r))) for r in range(4)], 0
    ).astype(bf16)


def back_weights(w_in, w_out):
    v = (w_in.T[None] * w_out[:, None, :]).reshape(18, HIDDEN)
    v1 = rounded(v)
    v2 = v - v1
    wide = jnp.concatenate(
        [
            jnp.pad(jnp.concatenate([v1, v1], 1), ((0, 6), (0, 0))),
            jnp.pad(v2, ((0, 6), (0, HIDDEN))),
        ],
        0,
    )
    upper = jnp.pad(wide, ((0, 0), (0, 2 * HIDDEN)))
    lower = jnp.pad(wide, ((0, 0), (2 * HIDDEN, 0)))
    return jnp.concatenate([upper, lower], 0).astype(bf16)


def local(far_adjoint, pillar, green_blocks, pair_src, pair_dst, group_end, w_in, b_in, w_out):
    own = to_block_table(far_adjoint).reshape(NB, NB // 4, 16, 128)
    ext = with_halo(own, (("tx", 0, CONE), ("ty", 1, CONE // 4)))
    ext = ext.reshape(EXT * EXT * 4, 128)
    near = sparse_near(
        pair_dst.reshape(-1), group_end.reshape(-1), pair_src.reshape(-1), ext,
        green_stack(green_blocks),
    )
    wide = with_halo(pillar, (("tx", 0, 1), ("ty", 1, 1)))
    wide = jnp.pad(wide, ((0, 6), (0, 0)))
    p3 = jnp.stack([wide[:, b : b + SIDE] for b in range(3)])
    grad, west, east, sums = cell_model(
        p3,
        near,
        first_weights(w_in, b_in),
        back_weights(w_in, w_out),
        jnp.pad(w_out, ((0, 6), (0, HIDDEN))),
    )
    grad, sums = finish(grad, west, east, sums)
    return (
        grad,
        sums[0:9, 0:HIDDEN].T,
        sums[9, 0:HIDDEN],
        sums[10].reshape(2, HIDDEN),
    )


def finish_kernel(
    shape,
    grad_ref,
    west_ref,
    east_ref,
    msg_ref,
    out_ref,
    sums_ref,
    row_out,
    row_in,
    col_out,
    col_in,
    cols,
    buf_a,
    buf_b,
    row_send,
    row_recv,
    col_send,
    col_recv,
    send_a,
    recv_a,
    send_b,
    recv_b,
):
    nx, ny = shape
    tx = lax.axis_index("tx")
    ty = lax.axis_index("ty")

    barrier = pltpu.get_barrier_semaphore()
    for d in range(1, nx):
        pl.semaphore_signal(
            barrier, inc=1, device_id=(lax.rem(tx + d, nx), ty), device_id_type=MESH
        )
    for d in range(1, ny):
        pl.semaphore_signal(
            barrier, inc=1, device_id=(tx, lax.rem(ty + d, ny)), device_id_type=MESH
        )
    if nx + ny > 2:
        pl.semaphore_wait(barrier, nx + ny - 2)

    def line(side, which):
        out, into, send, recv, axis = which
        at = (tx, ty)[axis] + 2 * side - 1
        device = (at, ty) if axis == 0 else (tx, at)
        return pltpu.make_async_remote_copy(
            src_ref=out.at[side],
            dst_ref=into.at[side],
            send_sem=send.at[side],
            recv_sem=recv.at[side],
            device_id=device,
            device_id_type=MESH,
        )

    rows = (row_out, row_in, row_send, row_recv, 0)
    columns = (col_out, col_in, col_send, col_recv, 1)

    def has(side, index, count):
        return index > 0 if side == 0 else index < count - 1

    row_out[0, :, 0:128] = west_ref[0:8, :]
    row_out[0, :, 128 : 128 + SIDE] = grad_ref[0:8, :]
    row_out[0, :, 128 + SIDE : 256 + SIDE] = east_ref[0:8, :]
    row_out[1, :, 0:128] = west_ref[SIDE + 8 : SIDE + 16, :]
    row_out[1, :, 128 : 128 + SIDE] = grad_ref[SIDE + 8 : SIDE + 16, :]
    row_out[1, :, 128 + SIDE : 256 + SIDE] = east_ref[SIDE + 8 : SIDE + 16, :]
    for side in range(2):
        pl.when(has(side, tx, nx))(lambda side=side: line(side, rows).start())

    def sums_copy(d, buf, send, recv, index, count, axis):
        other = lax.rem(index + d, count)
        return pltpu.make_async_remote_copy(
            src_ref=buf.at[index],
            dst_ref=buf.at[index],
            send_sem=send.at[d],
            recv_sem=recv.at[index],
            device_id=(other, ty) if axis == 0 else (tx, other),
            device_id_type=MESH,
        )

    def sums_wait(d, buf, send, recv, index, count, axis):
        sender = lax.rem(index + d, count)
        pltpu.make_async_remote_copy(
            src_ref=buf.at[sender],
            dst_ref=buf.at[sender],
            send_sem=send.at[d],
            recv_sem=recv.at[sender],
            device_id=(sender, ty) if axis == 0 else (tx, sender),
            device_id_type=MESH,
        ).wait_recv()

    along_x = (buf_a, send_a, recv_a, tx, nx, 0)
    along_y = (buf_b, send_b, recv_b, ty, ny, 1)
    buf_a[tx] = msg_ref[...]
    for d in range(1, nx):
        sums_copy(d, *along_x).start()

    def copy(i, carry):
        at = pl.multiple_of(i * 8, 8)
        out_ref[pl.ds(at, 8), :] = grad_ref[pl.ds(at + 8, 8), :]
        cols[0, pl.ds(at, 8), :] = west_ref[pl.ds(at + 8, 8), :]
        cols[1, pl.ds(at, 8), :] = east_ref[pl.ds(at + 8, 8), :]
        return carry

    lax.fori_loop(0, SIDE // 8, copy, 0)
    for side, row, first in ((0, 7, SIDE - 8), (1, 0, 0)):

        @pl.when(has(1 - side, tx, nx))
        def _(side=side, row=row, first=first):
            line(side, rows).wait_recv()
            got = row_in[side]
            got = jnp.where(
                lax.broadcasted_iota(jnp.int32, got.shape, 0) == row, got, 0.0
            )
            out_ref[first : first + 8, :] += got[:, 128 : 128 + SIDE]
            cols[0, first : first + 8, :] += got[:, 0:128]
            cols[1, first : first + 8, :] += got[:, 128 + SIDE : 256 + SIDE]

    for q in range(4):
        tile = slice(128 * q, 128 * q + 128)
        col_out[0, :, tile] = cols[0, tile, :].T[0:8]
        col_out[1, :, tile] = cols[1, tile, :].T[120:128]
    for side in range(2):
        pl.when(has(side, ty, ny))(lambda side=side: line(side, columns).start())

    for d in range(1, nx):
        sums_wait(d, *along_x)
    value = buf_a[0]
    for d in range(1, nx):
        value = value + buf_a[d]
    buf_b[ty] = value
    for d in range(1, ny):
        sums_copy(d, *along_y).start()

    lane = lax.broadcasted_iota(jnp.int32, (128, 128), 1)
    for side, row, first, spot in ((0, 0, SIDE - 128, 127), (1, 7, 0, 0)):

        @pl.when(has(1 - side, ty, ny))
        def _(side=side, row=row, first=first, spot=spot):
            line(side, columns).wait_recv()
            for q in range(4):
                tile = slice(128 * q, 128 * q + 128)
                got = jnp.broadcast_to(col_in[side, row : row + 1, tile], (128, 128)).T
                out_ref[tile, first : first + 128] += jnp.where(lane == spot, got, 0.0)

    for d in range(1, ny):
        sums_wait(d, *along_y)
    value = buf_b[0]
    for d in range(1, ny):
        value = value + buf_b[d]
    sums_ref[...] = value * (float(SIDE * SIDE * nx * ny) ** (-0.5))
    for side in range(2):
        pl.when(has(side, tx, nx))(lambda side=side: line(side, rows).wait_send())
        pl.when(has(side, ty, ny))(lambda side=side: line(side, columns).wait_send())
    for d in range(1, nx):
        sums_copy(d, *along_x).wait_send()
    for d in range(1, ny):
        sums_copy(d, *along_y).wait_send()


def finish(grad, west, east, sums):
    nx, ny = lax.axis_size("tx"), lax.axis_size("ty")
    dma = pltpu.SemaphoreType.DMA
    return pl.pallas_call(
        functools.partial(finish_kernel, (nx, ny)),
        out_shape=[
            jax.ShapeDtypeStruct((SIDE, SIDE), f32),
            jax.ShapeDtypeStruct((16, 128), f32),
        ],
        in_specs=[pl.BlockSpec(memory_space=pltpu.VMEM)] * 4,
        out_specs=[pl.BlockSpec(memory_space=pltpu.VMEM)] * 2,
        scratch_shapes=[
            pltpu.VMEM((2, 8, SIDE + 256), f32),
            pltpu.VMEM((2, 8, SIDE + 256), f32),
            pltpu.VMEM((2, 8, SIDE), f32),
            pltpu.VMEM((2, 8, SIDE), f32),
            pltpu.VMEM((2, SIDE, 128), f32),
            pltpu.VMEM((nx, 16, 128), f32),
            pltpu.VMEM((ny, 16, 128), f32),
            dma((2,)),
            dma((2,)),
            dma((2,)),
            dma((2,)),
            dma((nx,)),
            dma((nx,)),
            dma((ny,)),
            dma((ny,)),
        ],
        compiler_params=pltpu.CompilerParams(
            vmem_limit_bytes=VMEM_BYTES, collective_id=0, has_side_effects=True
        ),
        name="finish",
    )(grad, west, east, sums)


def solution(mesh):
    return jax.shard_map(
        local,
        mesh=mesh,
        in_specs=(
            P(None, "tx", "ty"),
            P("tx", "ty"),
            P(),
            P("tx", "ty", None),
            P("tx", "ty", None),
            P("tx", "ty", None),
            P(),
            P(),
            P(),
        ),
        out_specs=(P("tx", "ty"), P(), P(), P()),
        check_vma=False,
    )
```

```python
import functools

import jax
import jax.numpy as jnp
from jax import lax
from jax.experimental import pallas as pl
from jax.experimental.pallas import tpu as pltpu
from jax.sharding import PartitionSpec as P

BLK = 16
CONE = 12
SIDE = 512
NB = SIDE // BLK
EXT = NB + 2 * CONE
GROUPS = 8
CHUNK = 512
PARTS = 1
HIDDEN = 64
PADROWS = 16
SROWS = 24
VMEM_BYTES = 60 * 1024 * 1024

f32 = jnp.float32
bf16 = jnp.bfloat16
MESH = pl.DeviceIdType.MESH


def swap_pieces(vectors):
    lane = lax.broadcasted_iota(jnp.int32, (8, 128), 1) // 16
    for d in (1, 2, 4):
        mixed = []
        for x in range(8):
            if x & d:
                moved = pltpu.roll(vectors[x ^ d], 128 - 16 * d, 1)
                mixed.append(jnp.where((lane & d) == 0, moved, vectors[x]))
            else:
                moved = pltpu.roll(vectors[x ^ d], 16 * d, 1)
                mixed.append(jnp.where((lane & d) == 0, vectors[x], moved))
        vectors = mixed
    return vectors


def sparse_kernel(
    dst_ref, ends_ref, src_ref, ext_ref, green_ref, near_ref, table, rows, rows16, stack, seg, acc
):
    chunks = dst_ref.shape[0] // CHUNK

    def widen(i, carry):
        at = pl.ds(pl.multiple_of(i * 128, 128), 128)
        table[at, :] = ext_ref[at, :].astype(f32)
        return carry

    lax.fori_loop(0, EXT * EXT * 4 // 128, widen, 0)
    acc[...] = jnp.zeros_like(acc)

    def gather(base, first, count):
        for q in range(first, first + count):
            d = pl.multiple_of(dst_ref[base + q], 4)
            rows[4 * q : 4 * q + 4, :] = table[pl.ds(d, 4), :]

    def narrow():
        for j in range(4):
            rows16[:, 128 * j : 128 * j + 128] = rows[
                pl.ds(j, CHUNK, stride=4), :
            ].astype(bf16)

    gather(0, 0, CHUNK)
    narrow()

    def group(k, carry):
        start = jnp.where(k == 0, 0, ends_ref[jnp.maximum(k - 1, 0)])
        stop = ends_ref[k]
        seg[...] = jnp.zeros_like(seg)

        def chunk(c, inner):
            ahead = jnp.minimum(c + 1, chunks - 1) * CHUNK
            slot = c * CHUNK + lax.broadcasted_iota(jnp.int32, (1, CHUNK), 1)
            live = (slot >= start) & (slot < stop)
            source = jnp.where(live, src_ref[c], -1)
            for m in range(PARTS):
                size = NB * NB // PARTS
                ids = lax.broadcasted_iota(jnp.int32, (size, CHUNK), 0) + size * m
                hot = jnp.where(ids == source, 1.0, 0.0).astype(bf16)
                gather(ahead, CHUNK // PARTS * m, CHUNK // PARTS)
                seg[size * m : size * m + size, :] += jnp.dot(
                    hot, rows16[...], preferred_element_type=f32
                )
            pl.when((c + 1) * CHUNK <= stop)(narrow)
            return inner

        lax.fori_loop(start // CHUNK, (stop + CHUNK - 1) // CHUNK, chunk, 0)

        half = BLK * BLK
        real = green_ref[k, 0]
        imag = green_ref[k, 1]
        stack[0:half, 0:half] = real
        stack[0:half, half : 2 * half] = -imag
        stack[half : 2 * half, 0:half] = imag
        stack[half : 2 * half, half : 2 * half] = real

        def apply(m, inner):
            at = pl.ds(pl.multiple_of(m * 512, 512), 512)
            value = seg[at, :]
            high = value.astype(bf16)
            low = (value - high.astype(f32)).astype(bf16)
            near = jnp.dot(high, stack[...], preferred_element_type=f32) + jnp.dot(
                low, stack[...], preferred_element_type=f32
            )
            for j in range(4):
                acc[j, at, :] += near[:, 128 * j : 128 * j + 128]
            return inner

        lax.fori_loop(0, 2, apply, 0)
        return carry

    lax.fori_loop(0, GROUPS, group, 0)

    def lay(i, carry):
        for j in range(4):
            for t in range(SIDE // 128):
                vectors = [
                    acc[j, pl.ds(i * 256 + 8 * t + b, 8, stride=NB), :] for b in range(8)
                ]
                for x, v in enumerate(swap_pieces(vectors)):
                    at = pl.ds(PADROWS + i * 128 + 8 * (j % 2) + x, 8, stride=BLK)
                    near_ref[j // 2, t, at, :] = v
        return carry

    lax.fori_loop(0, NB // 8, lay, 0)
    for c in range(2):
        for t in range(4):
            near_ref[c, t, 0:PADROWS, :] = jnp.zeros((PADROWS, 128), f32)
            near_ref[c, t, PADROWS + SIDE : 2 * PADROWS + SIDE, :] = jnp.zeros(
                (PADROWS, 128), f32
            )


def sparse_near(targets, ends, sources, ext, green):
    slots = targets.shape[0]
    return pl.pallas_call(
        sparse_kernel,
        out_shape=jax.ShapeDtypeStruct((2, 4, SIDE + 2 * PADROWS, 128), f32),
        in_specs=[
            pl.BlockSpec(memory_space=pltpu.SMEM),
            pl.BlockSpec(memory_space=pltpu.SMEM),
            pl.BlockSpec(memory_space=pltpu.VMEM),
            pl.BlockSpec(memory_space=pltpu.VMEM),
            pl.BlockSpec(memory_space=pltpu.VMEM),
        ],
        out_specs=pl.BlockSpec(memory_space=pltpu.VMEM),
        scratch_shapes=[
            pltpu.VMEM((EXT * EXT * 4, 128), f32),
            pltpu.VMEM((CHUNK * 4, 128), f32),
            pltpu.VMEM((CHUNK, 512), bf16),
            pltpu.VMEM((512, 512), bf16),
            pltpu.VMEM((NB * NB, 512), f32),
            pltpu.VMEM((4, NB * NB, 128), f32),
        ],
        compiler_params=pltpu.CompilerParams(vmem_limit_bytes=VMEM_BYTES),
        name="sparse_near",
    )(
        jnp.clip(targets, 0, EXT * EXT - 1) * 4,
        ends,
        sources.reshape(slots // CHUNK, 1, CHUNK),
        ext,
        green,
    )


def split2(value):
    high = value.astype(bf16).astype(f32)
    return high, value - high


def put(ref, start, stride, value):
    for t in range(SIDE // 128):
        ref[t, pl.ds(start, 8, stride=stride), :] = value[:, 128 * t : 128 * t + 128]


def take(ref, start, stride):
    tiles = [ref[t, pl.ds(start, 8, stride=stride), :] for t in range(SIDE // 128)]
    return jnp.concatenate(tiles, 1)


def cell_kernel(
    p3_ref,
    near_ref,
    w1_ref,
    v_ref,
    wout_ref,
    grad_ref,
    west_ref,
    east_ref,
    sums_ref,
    q32,
    qs,
    gs,
    ps,
    total,
    nh,
):
    width = SIDE

    def near_rows(c, first, count):
        at = pl.ds(pl.multiple_of(first, 8), count)
        return jnp.concatenate([near_ref[c, t, at, :] for t in range(4)], 1)

    def build(i, carry):
        r0 = pl.multiple_of(i * 8, 8)
        for b in range(3):
            x = p3_ref[b, pl.ds(r0, 8), :]
            x1, rest = split2(x)
            x2, x3 = split2(rest)
            for n, piece in enumerate((x1, x1, x2, x2, x3)):
                put(q32, b * 5 + n, 16, piece)
        put(q32, 15, 16, jnp.ones((8, width), f32))
        for t in range(4):
            qs[pl.ds(r0, 8), :, 128 * t : 128 * t + 128] = (
                q32[t].astype(bf16).reshape(8, 16, 128)
            )
        return carry

    lax.fori_loop(0, (SIDE + 16) // 8, build, 0)
    total[...] = jnp.zeros_like(total)
    nh[...] = jnp.zeros_like(nh)
    gs[...] = jnp.zeros_like(gs)
    zero_rows = jnp.zeros((PADROWS * SROWS, 128), f32)
    for t in range(4):
        ps[t, 0 : PADROWS * SROWS, :] = zero_rows
        ps[t, (PADROWS + SIDE) * SROWS : (2 * PADROWS + SIDE) * SROWS, :] = zero_rows

    def strip(i, carry):
        r0 = pl.multiple_of(i * 8, 8)
        n = [near_rows(c, r0 + PADROWS, 8) for c in range(2)]
        deep = [p3_ref[b, pl.ds(r0, 24), :] for b in range(3)]
        for a in range(3):
            for b in range(3):
                feat = deep[b][7 + a : 15 + a]
                for c in range(2):
                    put(gs, 10 * c + 3 * a + b, SROWS, n[c] * feat)
        for c in range(2):
            put(gs, 10 * c + 9, SROWS, n[c])
        for half in range(2):
            left, right = [], []
            partial = [None, None]
            feats = qs[pl.ds(r0 + 4 * half + 7, 6)].reshape(96, width)
            h = jnp.tanh(jnp.dot(w1_ref[...], feats, preferred_element_type=f32))
            for pair in range(2):
                pieces = []
                for r in range(2 * pair, 2 * pair + 2):
                    j = 4 * half + r
                    hr = h[HIDDEN * r : HIDDEN * r + HIDDEN]
                    u = 1.0 - hr * hr
                    u1 = u.astype(bf16)
                    u2 = (u - u1.astype(f32)).astype(bf16)
                    pieces += [u1, u2]
                    for c in range(2):
                        for t in range(4):
                            tile = slice(128 * t, 128 * t + 128)
                            term = n[c][j : j + 1, tile] * hr[:, tile]
                            partial[c] = term if partial[c] is None else partial[c] + term
                    g = jnp.concatenate(
                        [gs[t, SROWS * j : SROWS * j + SROWS, :] for t in range(4)], 1
                    )
                    g1, g2 = split2(g)
                    left.append(jnp.concatenate([u1, u2], 0))
                    right.append(jnp.concatenate([g1, g2], 0).astype(bf16))
                slope = jnp.dot(
                    v_ref[...], jnp.concatenate(pieces, 0), preferred_element_type=f32
                )
                for r in range(2):
                    j = 4 * half + 2 * pair + r
                    one = (
                        slope[2 * SROWS * r : 2 * SROWS * r + SROWS]
                        + slope[2 * SROWS * r + SROWS : 2 * SROWS * r + 2 * SROWS]
                    )
                    at = pl.ds(pl.multiple_of((r0 + PADROWS + j) * SROWS, 8), SROWS)
                    for t in range(4):
                        ps[t, at, :] = one[:, 128 * t : 128 * t + 128]
            total[:, 0 : 2 * SROWS] += lax.dot_general(
                jnp.concatenate(left, 1),
                jnp.concatenate(right, 1),
                (((1,), (1,)), ((), ())),
                preferred_element_type=f32,
            )
            for c in range(2):
                nh[HIDDEN * c : HIDDEN * c + HIDDEN, :] += partial[c]
        return carry

    lax.fori_loop(0, SIDE // 8, strip, 0)
    turned = total[...].T
    turned = turned + pltpu.roll(turned, HIDDEN, 1)
    pulled = turned[0:SROWS] + turned[SROWS : 2 * SROWS]
    first = wout_ref[0:1, :] * pulled[0:10] + wout_ref[1:2, :] * pulled[10:20]
    second = jnp.sum(nh[...].T, axis=0, keepdims=True)
    sums_ref[...] = jnp.zeros_like(sums_ref)
    sums_ref[0:10, :] = first
    sums_ref[10:11, :] = second

    lane = lax.broadcasted_iota(jnp.int32, (8, width), 1)

    def combine(i, carry):
        parts = []
        deep = [near_rows(c, i * 8, 24) for c in range(2)]
        for b in range(3):
            acc = None
            for a in range(3):
                x0 = i * 8 + 9 - a
                for c in range(2):
                    term = deep[c][9 - a : 17 - a] * take(
                        ps, x0 * SROWS + 9 * c + 3 * a + b, SROWS
                    )
                    acc = term if acc is None else acc + term
            parts.append(acc)
        low = jnp.where(lane == width - 1, 0.0, pltpu.roll(parts[0], width - 1, 1))
        high = jnp.where(lane == 0, 0.0, pltpu.roll(parts[2], 1, 1))
        at = pl.ds(pl.multiple_of(i * 8, 8), 8)
        grad_ref[at, :] = parts[1] + low + high
        west_ref[at, :] = parts[0][:, 0:128]
        east_ref[at, :] = parts[2][:, width - 128 : width]
        return carry

    lax.fori_loop(0, SIDE // 8 + 2, combine, 0)


def cell_model(p3, near, first, back, out_weights):
    rows = SIDE + 16
    return pl.pallas_call(
        cell_kernel,
        out_shape=[
            jax.ShapeDtypeStruct((rows, SIDE), f32),
            jax.ShapeDtypeStruct((rows, 128), f32),
            jax.ShapeDtypeStruct((rows, 128), f32),
            jax.ShapeDtypeStruct((16, 128), f32),
        ],
        in_specs=[pl.BlockSpec(memory_space=pltpu.VMEM)] * 5,
        out_specs=[pl.BlockSpec(memory_space=pltpu.VMEM)] * 4,
        scratch_shapes=[
            pltpu.VMEM((4, 128, 128), f32),
            pltpu.VMEM((SIDE + 16, 16, SIDE), bf16),
            pltpu.VMEM((4, 8 * SROWS, 128), f32),
            pltpu.VMEM((4, (SIDE + 2 * PADROWS) * SROWS, 128), f32),
            pltpu.VMEM((128, 128), f32),
            pltpu.VMEM((128, 128), f32),
        ],
        compiler_params=pltpu.CompilerParams(vmem_limit_bytes=VMEM_BYTES),
        name="cell_model",
    )(p3, near, first, back, out_weights)


AROUND = [(dx, dy) for dx in (-1, 0, 1) for dy in (-1, 0, 1) if (dx, dy) != (0, 0)]


def front_kernel(
    shape, far_ref, pillar_ref, ext_ref, p3_ref, field, flat, edge_in, turned, side, sends, recvs
):
    nx, ny = shape
    tx = lax.axis_index("tx")
    ty = lax.axis_index("ty")
    barrier = pltpu.get_barrier_semaphore()
    for dx, dy in AROUND:
        pl.semaphore_signal(
            barrier,
            inc=1,
            device_id=(lax.rem(tx + dx + nx, nx), lax.rem(ty + dy + ny, ny)),
            device_id_type=MESH,
        )

    for q in range(4):
        tile = slice(128 * q, 128 * q + 128)
        turned[0, :, tile] = pillar_ref[tile, 0:128].T[0:8]
        turned[1, :, tile] = pillar_ref[tile, SIDE - 128 : SIDE].T[120:128]
    pl.semaphore_wait(barrier, len(AROUND))

    def there(dx, dy):
        fits = None
        for delta, index, count in ((dx, tx, nx), (dy, ty, ny)):
            if delta:
                one = index > 0 if delta < 0 else index < count - 1
                fits = one if fits is None else jnp.logical_and(fits, one)
        return fits

    def rim(delta, length, reach):
        if delta < 0:
            return (0, reach), (length, reach)
        if delta > 0:
            return (length - reach, reach), (-reach, reach)
        return (0, length), (0, length)

    def far_copy(n):
        dx, dy = AROUND[n]
        (x, wx), (ox, _) = rim(dx, NB, CONE)
        (y, wy), (oy, _) = rim(dy, NB // 4, CONE // 4)
        return pltpu.make_async_remote_copy(
            src_ref=ext_ref.at[pl.ds(CONE + x, wx), pl.ds(CONE // 4 + y, wy)],
            dst_ref=ext_ref.at[pl.ds(CONE + ox, wx), pl.ds(CONE // 4 + oy, wy)],
            send_sem=sends.at[n],
            recv_sem=recvs.at[n],
            device_id=(tx + dx, ty + dy),
            device_id_type=MESH,
        )

    def edge_copy(n):
        dx, dy = AROUND[n]
        if dy == 0:
            source = pillar_ref.at[pl.ds(0 if dx < 0 else SIDE - 8, 8), :]
        elif dx == 0:
            source = turned.at[0 if dy < 0 else 1]
        else:
            source = pillar_ref.at[
                pl.ds(0 if dx < 0 else SIDE - 8, 8), pl.ds(0 if dy < 0 else SIDE - 128, 128)
            ]
        wide = SIDE if dx == 0 or dy == 0 else 128
        return pltpu.make_async_remote_copy(
            src_ref=source,
            dst_ref=edge_in.at[n, :, pl.ds(0, wide)],
            send_sem=sends.at[8 + n],
            recv_sem=recvs.at[8 + n],
            device_id=(tx + dx, ty + dy),
            device_id_type=MESH,
        )

    for n, (dx, dy) in enumerate(AROUND):
        pl.when(there(dx, dy))(lambda n=n: edge_copy(n).start())

    def spread(i, carry):
        at = pl.ds(pl.multiple_of(i * BLK, BLK), BLK)
        for c in range(2):
            strip = far_ref[c, at, :].astype(f32)
            for t in range(4):
                field[c, t, at, :] = strip[:, 128 * t : 128 * t + 128]
        return carry

    lax.fori_loop(0, SIDE // BLK, spread, 0)

    def turn(i, carry):
        for j in range(4):
            for t in range(4):
                first = i * 128 + 8 * (j % 2)
                vectors = [
                    field[j // 2, t, pl.ds(first + x, 8, stride=BLK), :] for x in range(8)
                ]
                for b, v in enumerate(swap_pieces(vectors)):
                    flat[pl.ds(i * 1024 + (8 * t + b) * 4 + j, 8, stride=128), :] = v
        return carry

    lax.fori_loop(0, NB // 8, turn, 0)

    def pack(r, carry):
        value = flat[pl.ds(pl.multiple_of(r * 128, 128), 128), :].astype(bf16)
        ext_ref[CONE + r, CONE // 4 : CONE // 4 + NB // 4] = value.reshape(NB // 4, 16, 128)
        return carry

    lax.fori_loop(0, NB, pack, 0)
    for n, (dx, dy) in enumerate(AROUND):
        pl.when(there(dx, dy))(lambda n=n: far_copy(n).start())

    for n, (dx, dy) in enumerate(AROUND):

        @pl.when(jnp.logical_not(there(dx, dy)))
        def _(n=n, dx=dx, dy=dy):
            edge_in[7 - n] = jnp.zeros((8, SIDE), f32)
            x = {-1: 0, 0: CONE, 1: CONE + NB}[dx]
            y = {-1: 0, 0: CONE // 4, 1: (CONE + NB) // 4}[dy]
            wy = CONE // 4 if dy else NB // 4

            def clear(i, carry):
                ext_ref[x + i, y : y + wy] = jnp.zeros((wy, 16, 128), bf16)
                return carry

            lax.fori_loop(0, CONE if dx else NB, clear, 0)

    for n, (dx, dy) in enumerate(AROUND):
        pl.when(there(dx, dy))(lambda n=n: edge_copy(7 - n).wait_recv())
    at_of = {place: n for n, place in enumerate(AROUND)}

    def got(dx, dy):
        return edge_in.at[7 - at_of[(dx, dy)]]

    for s, dy in ((0, -1), (1, 1)):
        lane = 127 if s == 0 else 0
        side[s, 0:8, :] = jnp.broadcast_to(got(-1, dy)[:, lane : lane + 1], (8, 128))
        side[s, SIDE + 8 : SIDE + 16, :] = jnp.broadcast_to(
            got(1, dy)[:, lane : lane + 1], (8, 128)
        )
        row = 7 if s == 0 else 0
        for q in range(4):
            tile = slice(128 * q, 128 * q + 128)
            side[s, 8 + 128 * q : 136 + 128 * q, :] = jnp.broadcast_to(
                got(0, dy)[row : row + 1, tile], (128, 128)
            ).T

    lanes = lax.broadcasted_iota(jnp.int32, (8, SIDE), 1)

    def shifted(at, value):
        p3_ref[1, at, :] = value
        west = jnp.concatenate([side[0, at, :]] * 4, 1)
        east = jnp.concatenate([side[1, at, :]] * 4, 1)
        p3_ref[0, at, :] = jnp.where(lanes == 0, west, pltpu.roll(value, 1, 1))
        p3_ref[2, at, :] = jnp.where(lanes == SIDE - 1, east, pltpu.roll(value, SIDE - 1, 1))

    def interior(i, carry):
        r0 = pl.multiple_of(i * 8, 8)
        shifted(pl.ds(r0 + 8, 8), pillar_ref[pl.ds(r0, 8), :])
        return carry

    lax.fori_loop(0, SIDE // 8, interior, 0)
    shifted(pl.ds(0, 8), got(-1, 0)[...])
    shifted(pl.ds(SIDE + 8, 8), got(1, 0)[...])

    for n, (dx, dy) in enumerate(AROUND):
        pl.when(there(dx, dy))(lambda n=n: far_copy(7 - n).wait_recv())
    for n, (dx, dy) in enumerate(AROUND):

        @pl.when(there(dx, dy))
        def _(n=n):
            far_copy(n).wait_send()
            edge_copy(n).wait_send()


def front(far, pillar):
    nx, ny = lax.axis_size("tx"), lax.axis_size("ty")
    return pl.pallas_call(
        functools.partial(front_kernel, (nx, ny)),
        out_shape=[
            jax.ShapeDtypeStruct((EXT, EXT // 4, 16, 128), bf16),
            jax.ShapeDtypeStruct((3, SIDE + 16, SIDE), f32),
        ],
        in_specs=[pl.BlockSpec(memory_space=pltpu.VMEM)] * 2,
        out_specs=[pl.BlockSpec(memory_space=pltpu.VMEM)] * 2,
        scratch_shapes=[
            pltpu.VMEM((2, 4, SIDE, 128), f32),
            pltpu.VMEM((NB * NB * 4, 128), f32),
            pltpu.VMEM((8, 8, SIDE), f32),
            pltpu.VMEM((2, 8, SIDE), f32),
            pltpu.VMEM((2, SIDE + 16, 128), f32),
            pltpu.SemaphoreType.DMA((16,)),
            pltpu.SemaphoreType.DMA((16,)),
        ],
        compiler_params=pltpu.CompilerParams(
            vmem_limit_bytes=VMEM_BYTES, collective_id=1, has_side_effects=True
        ),
        name="front",
    )(far, pillar)


def rounded(value):
    return lax.reduce_precision(value, 8, 7)


def first_weights(w_in, b_in):
    w = w_in.reshape(HIDDEN, 3, 3)
    w1 = rounded(w)
    w2 = rounded(w - w1)
    b1 = rounded(b_in)
    b2 = rounded(b_in - b1)
    b3 = b_in - b1 - b2
    cells = jnp.stack([w1, w2, w1, w2, w1], 3).reshape(HIDDEN, 3, 15)
    bias = jnp.stack([b1, b2, b3], 1)[:, :, None]
    one = jnp.concatenate([cells, bias], 2).reshape(HIDDEN, 48)
    return jnp.concatenate(
        [jnp.pad(one, ((0, 0), (16 * r, 48 - 16 * r))) for r in range(4)], 0
    ).astype(bf16)


def back_weights(w_in, w_out):
    v = (w_in.T[None] * w_out[:, None, :]).reshape(18, HIDDEN)
    v1 = rounded(v)
    v2 = v - v1
    wide = jnp.concatenate(
        [
            jnp.pad(jnp.concatenate([v1, v1], 1), ((0, 6), (0, 0))),
            jnp.pad(v2, ((0, 6), (0, HIDDEN))),
        ],
        0,
    )
    upper = jnp.pad(wide, ((0, 0), (0, 2 * HIDDEN)))
    lower = jnp.pad(wide, ((0, 0), (2 * HIDDEN, 0)))
    return jnp.concatenate([upper, lower], 0).astype(bf16)


def local(far_adjoint, pillar, green_blocks, pair_src, pair_dst, group_end, w_in, b_in, w_out):
    ext, p3 = front(far_adjoint, pillar)
    near = sparse_near(
        pair_dst.reshape(-1),
        group_end.reshape(-1),
        pair_src.reshape(-1),
        ext.reshape(EXT * EXT * 4, 128),
        green_blocks,
    )
    grad, west, east, sums = cell_model(
        p3,
        near,
        first_weights(w_in, b_in),
        back_weights(w_in, w_out),
        jnp.pad(w_out, ((0, 6), (0, HIDDEN))),
    )
    grad, sums = finish(grad, west, east, sums)
    return (
        grad,
        sums[0:9, 0:HIDDEN].T,
        sums[9, 0:HIDDEN],
        sums[10].reshape(2, HIDDEN),
    )


def finish_kernel(
    shape,
    grad_ref,
    west_ref,
    east_ref,
    msg_ref,
    out_ref,
    sums_ref,
    row_out,
    row_in,
    col_out,
    col_in,
    cols,
    buf_a,
    buf_b,
    row_send,
    row_recv,
    col_send,
    col_recv,
    send_a,
    recv_a,
    send_b,
    recv_b,
):
    nx, ny = shape
    tx = lax.axis_index("tx")
    ty = lax.axis_index("ty")

    barrier = pltpu.get_barrier_semaphore()
    for d in range(1, nx):
        pl.semaphore_signal(
            barrier, inc=1, device_id=(lax.rem(tx + d, nx), ty), device_id_type=MESH
        )
    for d in range(1, ny):
        pl.semaphore_signal(
            barrier, inc=1, device_id=(tx, lax.rem(ty + d, ny)), device_id_type=MESH
        )
    if nx + ny > 2:
        pl.semaphore_wait(barrier, nx + ny - 2)

    def line(side, which):
        out, into, send, recv, axis = which
        at = (tx, ty)[axis] + 2 * side - 1
        device = (at, ty) if axis == 0 else (tx, at)
        return pltpu.make_async_remote_copy(
            src_ref=out.at[side],
            dst_ref=into.at[side],
            send_sem=send.at[side],
            recv_sem=recv.at[side],
            device_id=device,
            device_id_type=MESH,
        )

    rows = (row_out, row_in, row_send, row_recv, 0)
    columns = (col_out, col_in, col_send, col_recv, 1)

    def has(side, index, count):
        return index > 0 if side == 0 else index < count - 1

    row_out[0, :, 0:128] = west_ref[0:8, :]
    row_out[0, :, 128 : 128 + SIDE] = grad_ref[0:8, :]
    row_out[0, :, 128 + SIDE : 256 + SIDE] = east_ref[0:8, :]
    row_out[1, :, 0:128] = west_ref[SIDE + 8 : SIDE + 16, :]
    row_out[1, :, 128 : 128 + SIDE] = grad_ref[SIDE + 8 : SIDE + 16, :]
    row_out[1, :, 128 + SIDE : 256 + SIDE] = east_ref[SIDE + 8 : SIDE + 16, :]
    for side in range(2):
        pl.when(has(side, tx, nx))(lambda side=side: line(side, rows).start())

    def sums_copy(d, buf, send, recv, index, count, axis):
        other = lax.rem(index + d, count)
        return pltpu.make_async_remote_copy(
            src_ref=buf.at[index],
            dst_ref=buf.at[index],
            send_sem=send.at[d],
            recv_sem=recv.at[index],
            device_id=(other, ty) if axis == 0 else (tx, other),
            device_id_type=MESH,
        )

    def sums_wait(d, buf, send, recv, index, count, axis):
        sender = lax.rem(index + d, count)
        pltpu.make_async_remote_copy(
            src_ref=buf.at[sender],
            dst_ref=buf.at[sender],
            send_sem=send.at[d],
            recv_sem=recv.at[sender],
            device_id=(sender, ty) if axis == 0 else (tx, sender),
            device_id_type=MESH,
        ).wait_recv()

    along_x = (buf_a, send_a, recv_a, tx, nx, 0)
    along_y = (buf_b, send_b, recv_b, ty, ny, 1)
    buf_a[tx] = msg_ref[...]
    for d in range(1, nx):
        sums_copy(d, *along_x).start()

    def copy(i, carry):
        at = pl.multiple_of(i * 8, 8)
        out_ref[pl.ds(at, 8), :] = grad_ref[pl.ds(at + 8, 8), :]
        cols[0, pl.ds(at, 8), :] = west_ref[pl.ds(at + 8, 8), :]
        cols[1, pl.ds(at, 8), :] = east_ref[pl.ds(at + 8, 8), :]
        return carry

    lax.fori_loop(0, SIDE // 8, copy, 0)
    for side, row, first in ((0, 7, SIDE - 8), (1, 0, 0)):

        @pl.when(has(1 - side, tx, nx))
        def _(side=side, row=row, first=first):
            line(side, rows).wait_recv()
            got = row_in[side]
            got = jnp.where(
                lax.broadcasted_iota(jnp.int32, got.shape, 0) == row, got, 0.0
            )
            out_ref[first : first + 8, :] += got[:, 128 : 128 + SIDE]
            cols[0, first : first + 8, :] += got[:, 0:128]
            cols[1, first : first + 8, :] += got[:, 128 + SIDE : 256 + SIDE]

    for q in range(4):
        tile = slice(128 * q, 128 * q + 128)
        col_out[0, :, tile] = cols[0, tile, :].T[0:8]
        col_out[1, :, tile] = cols[1, tile, :].T[120:128]
    for side in range(2):
        pl.when(has(side, ty, ny))(lambda side=side: line(side, columns).start())

    for d in range(1, nx):
        sums_wait(d, *along_x)
    value = buf_a[0]
    for d in range(1, nx):
        value = value + buf_a[d]
    buf_b[ty] = value
    for d in range(1, ny):
        sums_copy(d, *along_y).start()

    lane = lax.broadcasted_iota(jnp.int32, (128, 128), 1)
    for side, row, first, spot in ((0, 0, SIDE - 128, 127), (1, 7, 0, 0)):

        @pl.when(has(1 - side, ty, ny))
        def _(side=side, row=row, first=first, spot=spot):
            line(side, columns).wait_recv()
            for q in range(4):
                tile = slice(128 * q, 128 * q + 128)
                got = jnp.broadcast_to(col_in[side, row : row + 1, tile], (128, 128)).T
                out_ref[tile, first : first + 128] += jnp.where(lane == spot, got, 0.0)

    for d in range(1, ny):
        sums_wait(d, *along_y)
    value = buf_b[0]
    for d in range(1, ny):
        value = value + buf_b[d]
    sums_ref[...] = value * (float(SIDE * SIDE * nx * ny) ** (-0.5))
    for side in range(2):
        pl.when(has(side, tx, nx))(lambda side=side: line(side, rows).wait_send())
        pl.when(has(side, ty, ny))(lambda side=side: line(side, columns).wait_send())
    for d in range(1, nx):
        sums_copy(d, *along_x).wait_send()
    for d in range(1, ny):
        sums_copy(d, *along_y).wait_send()


def finish(grad, west, east, sums):
    nx, ny = lax.axis_size("tx"), lax.axis_size("ty")
    dma = pltpu.SemaphoreType.DMA
    return pl.pallas_call(
        functools.partial(finish_kernel, (nx, ny)),
        out_shape=[
            jax.ShapeDtypeStruct((SIDE, SIDE), f32),
            jax.ShapeDtypeStruct((16, 128), f32),
        ],
        in_specs=[pl.BlockSpec(memory_space=pltpu.VMEM)] * 4,
        out_specs=[pl.BlockSpec(memory_space=pltpu.VMEM)] * 2,
        scratch_shapes=[
            pltpu.VMEM((2, 8, SIDE + 256), f32),
            pltpu.VMEM((2, 8, SIDE + 256), f32),
            pltpu.VMEM((2, 8, SIDE), f32),
            pltpu.VMEM((2, 8, SIDE), f32),
            pltpu.VMEM((2, SIDE, 128), f32),
            pltpu.VMEM((nx, 16, 128), f32),
            pltpu.VMEM((ny, 16, 128), f32),
            dma((2,)),
            dma((2,)),
            dma((2,)),
            dma((2,)),
            dma((nx,)),
            dma((nx,)),
            dma((ny,)),
            dma((ny,)),
        ],
        compiler_params=pltpu.CompilerParams(
            vmem_limit_bytes=VMEM_BYTES, collective_id=0, has_side_effects=True
        ),
        name="finish",
    )(grad, west, east, sums)


def solution(mesh):
    return jax.shard_map(
        local,
        mesh=mesh,
        in_specs=(
            P(None, "tx", "ty"),
            P("tx", "ty"),
            P(),
            P("tx", "ty", None),
            P("tx", "ty", None),
            P("tx", "ty", None),
            P(),
            P(),
            P(),
        ),
        out_specs=(P("tx", "ty"), P(), P(), P()),
        check_vma=False,
    )
```

```python
import functools

import jax
import jax.numpy as jnp
from jax import lax
from jax.experimental import pallas as pl
from jax.experimental.pallas import tpu as pltpu
from jax.sharding import PartitionSpec as P

BLK = 16
CONE = 12
SIDE = 512
NB = SIDE // BLK
EXT = NB + 2 * CONE
GROUPS = 8
CHUNK = 512
PARTS = 1
HIDDEN = 64
PADROWS = 16
SROWS = 24
VMEM_BYTES = 60 * 1024 * 1024

f32 = jnp.float32
bf16 = jnp.bfloat16
MESH = pl.DeviceIdType.MESH


def swap_pieces(vectors):
    lane = lax.broadcasted_iota(jnp.int32, (8, 128), 1) // 16
    for d in (1, 2, 4):
        mixed = []
        for x in range(8):
            if x & d:
                moved = pltpu.roll(vectors[x ^ d], 128 - 16 * d, 1)
                mixed.append(jnp.where((lane & d) == 0, moved, vectors[x]))
            else:
                moved = pltpu.roll(vectors[x ^ d], 16 * d, 1)
                mixed.append(jnp.where((lane & d) == 0, vectors[x], moved))
        vectors = mixed
    return vectors


def sparse_kernel(
    dst_ref, ends_ref, src_ref, ext_ref, green_ref, near_ref, table, rows, rows16, stack, seg, acc
):
    chunks = dst_ref.shape[0] // CHUNK

    def widen(i, carry):
        at = pl.ds(pl.multiple_of(i * 128, 128), 128)
        table[at, :] = ext_ref[at, :].astype(f32)
        return carry

    lax.fori_loop(0, EXT * EXT * 4 // 128, widen, 0)
    acc[...] = jnp.zeros_like(acc)

    def gather(base, first, count):
        for q in range(first, first + count):
            d = dst_ref[base + q] * 4
            rows[4 * q : 4 * q + 4, :] = table[pl.ds(pl.multiple_of(d, 4), 4), :]

    def narrow():
        for j in range(4):
            rows16[:, 128 * j : 128 * j + 128] = rows[
                pl.ds(j, CHUNK, stride=4), :
            ].astype(bf16)

    gather(0, 0, CHUNK)
    narrow()

    def group(k, carry):
        start = jnp.where(k == 0, 0, ends_ref[jnp.maximum(k - 1, 0)])
        stop = ends_ref[k]
        seg[...] = jnp.zeros_like(seg)

        def chunk(c, inner):
            ahead = jnp.minimum(c + 1, chunks - 1) * CHUNK
            slot = c * CHUNK + lax.broadcasted_iota(jnp.int32, (1, CHUNK), 1)
            live = (slot >= start) & (slot < stop)
            source = jnp.where(live, src_ref[c], -1)
            for m in range(PARTS):
                size = NB * NB // PARTS
                ids = lax.broadcasted_iota(jnp.int32, (size, CHUNK), 0) + size * m
                hot = jnp.where(ids == source, 1.0, 0.0).astype(bf16)
                gather(ahead, CHUNK // PARTS * m, CHUNK // PARTS)
                seg[size * m : size * m + size, :] += jnp.dot(
                    hot, rows16[...], preferred_element_type=f32
                )
            pl.when((c + 1) * CHUNK <= stop)(narrow)
            return inner

        lax.fori_loop(start // CHUNK, (stop + CHUNK - 1) // CHUNK, chunk, 0)

        half = BLK * BLK
        real = green_ref[k, 0]
        imag = green_ref[k, 1]
        stack[0:half, 0:half] = real
        stack[0:half, half : 2 * half] = -imag
        stack[half : 2 * half, 0:half] = imag
        stack[half : 2 * half, half : 2 * half] = real

        def apply(m, inner):
            at = pl.ds(pl.multiple_of(m * 512, 512), 512)
            value = seg[at, :]
            high = value.astype(bf16)
            low = (value - high.astype(f32)).astype(bf16)
            near = jnp.dot(high, stack[...], preferred_element_type=f32) + jnp.dot(
                low, stack[...], preferred_element_type=f32
            )
            for j in range(4):
                acc[j, at, :] += near[:, 128 * j : 128 * j + 128]
            return inner

        lax.fori_loop(0, 2, apply, 0)
        return carry

    lax.fori_loop(0, GROUPS, group, 0)

    def lay(i, carry):
        for j in range(4):
            for t in range(SIDE // 128):
                vectors = [
                    acc[j, pl.ds(i * 256 + 8 * t + b, 8, stride=NB), :] for b in range(8)
                ]
                for x, v in enumerate(swap_pieces(vectors)):
                    at = pl.ds(PADROWS + i * 128 + 8 * (j % 2) + x, 8, stride=BLK)
                    near_ref[j // 2, t, at, :] = v
        return carry

    lax.fori_loop(0, NB // 8, lay, 0)
    for c in range(2):
        for t in range(4):
            near_ref[c, t, 0:PADROWS, :] = jnp.zeros((PADROWS, 128), f32)
            near_ref[c, t, PADROWS + SIDE : 2 * PADROWS + SIDE, :] = jnp.zeros(
                (PADROWS, 128), f32
            )


def sparse_near(targets, ends, sources, ext, green):
    slots = targets.shape[0]
    return pl.pallas_call(
        sparse_kernel,
        out_shape=jax.ShapeDtypeStruct((2, 4, SIDE + 2 * PADROWS, 128), f32),
        in_specs=[
            pl.BlockSpec(memory_space=pltpu.SMEM),
            pl.BlockSpec(memory_space=pltpu.SMEM),
            pl.BlockSpec(memory_space=pltpu.VMEM),
            pl.BlockSpec(memory_space=pltpu.VMEM),
            pl.BlockSpec(memory_space=pltpu.VMEM),
        ],
        out_specs=pl.BlockSpec(memory_space=pltpu.VMEM),
        scratch_shapes=[
            pltpu.VMEM((EXT * EXT * 4, 128), f32),
            pltpu.VMEM((CHUNK * 4, 128), f32),
            pltpu.VMEM((CHUNK, 512), bf16),
            pltpu.VMEM((512, 512), bf16),
            pltpu.VMEM((NB * NB, 512), f32),
            pltpu.VMEM((4, NB * NB, 128), f32),
        ],
        compiler_params=pltpu.CompilerParams(vmem_limit_bytes=VMEM_BYTES),
        name="sparse_near",
    )(
        targets,
        ends,
        sources.reshape(slots // CHUNK, 1, CHUNK),
        ext,
        green,
    )


def split2(value):
    high = value.astype(bf16).astype(f32)
    return high, value - high


def put(ref, start, stride, value):
    for t in range(SIDE // 128):
        ref[t, pl.ds(start, 8, stride=stride), :] = value[:, 128 * t : 128 * t + 128]


def take(ref, start, stride):
    tiles = [ref[t, pl.ds(start, 8, stride=stride), :] for t in range(SIDE // 128)]
    return jnp.concatenate(tiles, 1)


def cell_kernel(
    p3_ref,
    near_ref,
    w1_ref,
    v_ref,
    wout_ref,
    grad_ref,
    west_ref,
    east_ref,
    sums_ref,
    q32,
    qs,
    gs,
    ps,
    total,
    nh,
    first_buf,
    second_buf,
):
    width = SIDE

    def near_rows(c, first, count):
        at = pl.ds(pl.multiple_of(first, 8), count)
        return jnp.concatenate([near_ref[c, t, at, :] for t in range(4)], 1)

    def build(i, carry):
        r0 = pl.multiple_of(i * 8, 8)
        for b in range(3):
            x = p3_ref[b, pl.ds(r0, 8), :]
            x1, rest = split2(x)
            x2, x3 = split2(rest)
            for n, piece in enumerate((x1, x1, x2, x2, x3)):
                put(q32, b * 5 + n, 16, piece)
        put(q32, 15, 16, jnp.ones((8, width), f32))
        for t in range(4):
            qs[pl.ds(r0, 8), :, 128 * t : 128 * t + 128] = (
                q32[t].astype(bf16).reshape(8, 16, 128)
            )
        return carry

    lax.fori_loop(0, 3, build, 0)
    total[...] = jnp.zeros_like(total)
    nh[...] = jnp.zeros_like(nh)
    gs[...] = jnp.zeros_like(gs)
    zero_rows = jnp.zeros((PADROWS * SROWS, 128), f32)
    for t in range(4):
        ps[t, 0 : PADROWS * SROWS, :] = zero_rows
        ps[t, (PADROWS + SIDE) * SROWS : (2 * PADROWS + SIDE) * SROWS, :] = zero_rows

    lane = lax.broadcasted_iota(jnp.int32, (8, width), 1)

    def combine(i, carry):
        parts = []
        deep = [near_rows(c, i * 8, 24) for c in range(2)]
        for b in range(3):
            acc = None
            for a in range(3):
                x0 = i * 8 + 9 - a
                for c in range(2):
                    term = deep[c][9 - a : 17 - a] * take(
                        ps, x0 * SROWS + 9 * c + 3 * a + b, SROWS
                    )
                    acc = term if acc is None else acc + term
            parts.append(acc)
        low = jnp.where(lane == width - 1, 0.0, pltpu.roll(parts[0], width - 1, 1))
        high = jnp.where(lane == 0, 0.0, pltpu.roll(parts[2], 1, 1))
        at = pl.ds(pl.multiple_of(i * 8, 8), 8)
        grad_ref[at, :] = parts[1] + low + high
        west_ref[at, :] = parts[0][:, 0:128]
        east_ref[at, :] = parts[2][:, width - 128 : width]
        return carry

    def strip(i, carry):
        r0 = pl.multiple_of(i * 8, 8)
        n = [near_rows(c, r0 + PADROWS, 8) for c in range(2)]
        deep = [p3_ref[b, pl.ds(r0, 24), :] for b in range(3)]
        for a in range(3):
            for b in range(3):
                feat = deep[b][7 + a : 15 + a]
                for c in range(2):
                    put(gs, 10 * c + 3 * a + b, SROWS, n[c] * feat)
        for c in range(2):
            put(gs, 10 * c + 9, SROWS, n[c])

        def make_next():
            build(jnp.minimum(i + 3, SIDE // 8 + 1), 0)

        def finish_last():
            combine(jnp.maximum(i - 1, 0), 0)

        after = [near_rows(c, r0 + PADROWS + 8, 8)[0:4] for c in range(2)]
        step(r0, 0, r0 + 4, [n[c][4:8] for c in range(2)], first_buf, second_buf, make_next)
        step(r0, 4, r0 + 8, after, second_buf, first_buf, finish_last)
        return carry

    def hidden(x0):
        feats = qs[pl.ds(x0 + 7, 6)].reshape(96, width)
        return jnp.dot(w1_ref[...], feats, preferred_element_type=f32)

    def activate(z, r, n, into, partial):
        hr = jnp.tanh(z[HIDDEN * r : HIDDEN * r + HIDDEN])
        u = 1.0 - hr * hr
        u1 = u.astype(bf16)
        into[2 * HIDDEN * r : 2 * HIDDEN * r + HIDDEN, :] = u1
        into[2 * HIDDEN * r + HIDDEN : 2 * HIDDEN * r + 2 * HIDDEN, :] = (
            u - u1.astype(f32)
        ).astype(bf16)
        for c in range(2):
            for t in range(4):
                tile = slice(128 * t, 128 * t + 128)
                term = n[c][r : r + 1, tile] * hr[:, tile]
                partial[c] = term if partial[c] is None else partial[c] + term

    def back(r0, j, pair, held):
        slope = jnp.dot(
            v_ref[...],
            held[4 * HIDDEN * pair : 4 * HIDDEN * pair + 4 * HIDDEN, :],
            preferred_element_type=f32,
        )
        for r in range(2):
            one = (
                slope[2 * SROWS * r : 2 * SROWS * r + SROWS]
                + slope[2 * SROWS * r + SROWS : 2 * SROWS * r + 2 * SROWS]
            )
            at = pl.ds(pl.multiple_of((r0 + PADROWS + j + 2 * pair + r) * SROWS, 8), SROWS)
            for t in range(4):
                ps[t, at, :] = one[:, 128 * t : 128 * t + 128]

    def sums(j, pair, held):
        left, right = [], []
        for r in range(2 * pair, 2 * pair + 2):
            first = SROWS * (j + r)
            g = jnp.concatenate([gs[t, first : first + SROWS, :] for t in range(4)], 1)
            left.append(held[2 * HIDDEN * r : 2 * HIDDEN * r + 2 * HIDDEN, :])
            right.append(jnp.concatenate(split2(g), 0).astype(bf16))
        return lax.dot_general(
            jnp.concatenate(left, 1),
            jnp.concatenate(right, 1),
            (((1,), (1,)), ((), ())),
            preferred_element_type=f32,
        )

    def step(r0, j, x0, n, held, into, extra):
        partial = [None, None]
        z = hidden(x0)
        activate(z, 0, n, into, partial)
        back(r0, j, 0, held)
        activate(z, 1, n, into, partial)
        one = sums(j, 0, held)
        activate(z, 2, n, into, partial)
        back(r0, j, 1, held)
        activate(z, 3, n, into, partial)
        extra()
        two = sums(j, 1, held)
        total[:, 0 : 2 * SROWS] += one + two
        for c in range(2):
            nh[HIDDEN * c : HIDDEN * c + HIDDEN, :] += partial[c]

    partial = [None, None]
    z = hidden(0)
    for r in range(4):
        activate(z, r, [near_rows(c, PADROWS, 8) for c in range(2)], first_buf, partial)
    for c in range(2):
        nh[HIDDEN * c : HIDDEN * c + HIDDEN, :] += partial[c]
    lax.fori_loop(0, SIDE // 8, strip, 0)
    turned = total[...].T
    turned = turned + pltpu.roll(turned, HIDDEN, 1)
    pulled = turned[0:SROWS] + turned[SROWS : 2 * SROWS]
    first = wout_ref[0:1, :] * pulled[0:10] + wout_ref[1:2, :] * pulled[10:20]
    second = jnp.sum(nh[...].T, axis=0, keepdims=True)
    sums_ref[...] = jnp.zeros_like(sums_ref)
    sums_ref[0:10, :] = first
    sums_ref[10:11, :] = second

    lax.fori_loop(SIDE // 8 - 1, SIDE // 8 + 2, combine, 0)


def cell_model(p3, near, first, back, out_weights):
    rows = SIDE + 16
    return pl.pallas_call(
        cell_kernel,
        out_shape=[
            jax.ShapeDtypeStruct((rows, SIDE), f32),
            jax.ShapeDtypeStruct((rows, 128), f32),
            jax.ShapeDtypeStruct((rows, 128), f32),
            jax.ShapeDtypeStruct((16, 128), f32),
        ],
        in_specs=[pl.BlockSpec(memory_space=pltpu.VMEM)] * 5,
        out_specs=[pl.BlockSpec(memory_space=pltpu.VMEM)] * 4,
        scratch_shapes=[
            pltpu.VMEM((4, 128, 128), f32),
            pltpu.VMEM((SIDE + 16, 16, SIDE), bf16),
            pltpu.VMEM((4, 8 * SROWS, 128), f32),
            pltpu.VMEM((4, (SIDE + 2 * PADROWS) * SROWS, 128), f32),
            pltpu.VMEM((128, 128), f32),
            pltpu.VMEM((128, 128), f32),
            pltpu.VMEM((8 * HIDDEN, SIDE), bf16),
            pltpu.VMEM((8 * HIDDEN, SIDE), bf16),
        ],
        compiler_params=pltpu.CompilerParams(vmem_limit_bytes=VMEM_BYTES),
        name="cell_model",
    )(p3, near, first, back, out_weights)


AROUND = [(dx, dy) for dx in (-1, 0, 1) for dy in (-1, 0, 1) if (dx, dy) != (0, 0)]


def front_kernel(
    shape, far_ref, pillar_ref, ext_ref, p3_ref, field, flat, edge_in, turned, side, sends, recvs
):
    nx, ny = shape
    tx = lax.axis_index("tx")
    ty = lax.axis_index("ty")
    barrier = pltpu.get_barrier_semaphore()
    for dx, dy in AROUND:
        pl.semaphore_signal(
            barrier,
            inc=1,
            device_id=(lax.rem(tx + dx + nx, nx), lax.rem(ty + dy + ny, ny)),
            device_id_type=MESH,
        )

    for q in range(4):
        tile = slice(128 * q, 128 * q + 128)
        turned[0, :, tile] = pillar_ref[tile, 0:128].T[0:8]
        turned[1, :, tile] = pillar_ref[tile, SIDE - 128 : SIDE].T[120:128]
    pl.semaphore_wait(barrier, len(AROUND))

    def there(dx, dy):
        fits = None
        for delta, index, count in ((dx, tx, nx), (dy, ty, ny)):
            if delta:
                one = index > 0 if delta < 0 else index < count - 1
                fits = one if fits is None else jnp.logical_and(fits, one)
        return fits

    def rim(delta, length, reach):
        if delta < 0:
            return (0, reach), (length, reach)
        if delta > 0:
            return (length - reach, reach), (-reach, reach)
        return (0, length), (0, length)

    def far_copy(n):
        dx, dy = AROUND[n]
        (x, wx), (ox, _) = rim(dx, NB, CONE)
        (y, wy), (oy, _) = rim(dy, NB // 4, CONE // 4)
        return pltpu.make_async_remote_copy(
            src_ref=ext_ref.at[pl.ds(CONE + x, wx), pl.ds(CONE // 4 + y, wy)],
            dst_ref=ext_ref.at[pl.ds(CONE + ox, wx), pl.ds(CONE // 4 + oy, wy)],
            send_sem=sends.at[n],
            recv_sem=recvs.at[n],
            device_id=(tx + dx, ty + dy),
            device_id_type=MESH,
        )

    def edge_copy(n):
        dx, dy = AROUND[n]
        if dy == 0:
            source = pillar_ref.at[pl.ds(0 if dx < 0 else SIDE - 8, 8), :]
        elif dx == 0:
            source = turned.at[0 if dy < 0 else 1]
        else:
            source = pillar_ref.at[
                pl.ds(0 if dx < 0 else SIDE - 8, 8), pl.ds(0 if dy < 0 else SIDE - 128, 128)
            ]
        wide = SIDE if dx == 0 or dy == 0 else 128
        return pltpu.make_async_remote_copy(
            src_ref=source,
            dst_ref=edge_in.at[n, :, pl.ds(0, wide)],
            send_sem=sends.at[8 + n],
            recv_sem=recvs.at[8 + n],
            device_id=(tx + dx, ty + dy),
            device_id_type=MESH,
        )

    for n, (dx, dy) in enumerate(AROUND):
        pl.when(there(dx, dy))(lambda n=n: edge_copy(n).start())

    def spread(i, carry):
        at = pl.ds(pl.multiple_of(i * BLK, BLK), BLK)
        for c in range(2):
            strip = far_ref[c, at, :].astype(f32)
            for t in range(4):
                field[c, t, at, :] = strip[:, 128 * t : 128 * t + 128]
        return carry

    lax.fori_loop(0, SIDE // BLK, spread, 0)

    def turn(i, carry):
        for j in range(4):
            for t in range(4):
                first = i * 128 + 8 * (j % 2)
                vectors = [
                    field[j // 2, t, pl.ds(first + x, 8, stride=BLK), :] for x in range(8)
                ]
                for b, v in enumerate(swap_pieces(vectors)):
                    flat[pl.ds(i * 1024 + (8 * t + b) * 4 + j, 8, stride=128), :] = v
        return carry

    lax.fori_loop(0, NB // 8, turn, 0)

    def pack(r, carry):
        value = flat[pl.ds(pl.multiple_of(r * 128, 128), 128), :].astype(bf16)
        ext_ref[CONE + r, CONE // 4 : CONE // 4 + NB // 4] = value.reshape(NB // 4, 16, 128)
        return carry

    lax.fori_loop(0, NB, pack, 0)
    for n, (dx, dy) in enumerate(AROUND):
        pl.when(there(dx, dy))(lambda n=n: far_copy(n).start())

    for n, (dx, dy) in enumerate(AROUND):

        @pl.when(jnp.logical_not(there(dx, dy)))
        def _(n=n, dx=dx, dy=dy):
            edge_in[7 - n] = jnp.zeros((8, SIDE), f32)
            x = {-1: 0, 0: CONE, 1: CONE + NB}[dx]
            y = {-1: 0, 0: CONE // 4, 1: (CONE + NB) // 4}[dy]
            wy = CONE // 4 if dy else NB // 4

            def clear(i, carry):
                ext_ref[x + i, y : y + wy] = jnp.zeros((wy, 16, 128), bf16)
                return carry

            lax.fori_loop(0, CONE if dx else NB, clear, 0)

    for n, (dx, dy) in enumerate(AROUND):
        pl.when(there(dx, dy))(lambda n=n: edge_copy(7 - n).wait_recv())
    at_of = {place: n for n, place in enumerate(AROUND)}

    def got(dx, dy):
        return edge_in.at[7 - at_of[(dx, dy)]]

    for s, dy in ((0, -1), (1, 1)):
        lane = 127 if s == 0 else 0
        side[s, 0:8, :] = jnp.broadcast_to(got(-1, dy)[:, lane : lane + 1], (8, 128))
        side[s, SIDE + 8 : SIDE + 16, :] = jnp.broadcast_to(
            got(1, dy)[:, lane : lane + 1], (8, 128)
        )
        row = 7 if s == 0 else 0
        for q in range(4):
            tile = slice(128 * q, 128 * q + 128)
            side[s, 8 + 128 * q : 136 + 128 * q, :] = jnp.broadcast_to(
                got(0, dy)[row : row + 1, tile], (128, 128)
            ).T

    lanes = lax.broadcasted_iota(jnp.int32, (8, SIDE), 1)

    def shifted(at, value):
        p3_ref[1, at, :] = value
        west = jnp.concatenate([side[0, at, :]] * 4, 1)
        east = jnp.concatenate([side[1, at, :]] * 4, 1)
        p3_ref[0, at, :] = jnp.where(lanes == 0, west, pltpu.roll(value, 1, 1))
        p3_ref[2, at, :] = jnp.where(lanes == SIDE - 1, east, pltpu.roll(value, SIDE - 1, 1))

    def interior(i, carry):
        r0 = pl.multiple_of(i * 8, 8)
        shifted(pl.ds(r0 + 8, 8), pillar_ref[pl.ds(r0, 8), :])
        return carry

    lax.fori_loop(0, SIDE // 8, interior, 0)
    shifted(pl.ds(0, 8), got(-1, 0)[...])
    shifted(pl.ds(SIDE + 8, 8), got(1, 0)[...])

    for n, (dx, dy) in enumerate(AROUND):
        pl.when(there(dx, dy))(lambda n=n: far_copy(7 - n).wait_recv())
    for n, (dx, dy) in enumerate(AROUND):

        @pl.when(there(dx, dy))
        def _(n=n):
            far_copy(n).wait_send()
            edge_copy(n).wait_send()


def front(far, pillar):
    nx, ny = lax.axis_size("tx"), lax.axis_size("ty")
    return pl.pallas_call(
        functools.partial(front_kernel, (nx, ny)),
        out_shape=[
            jax.ShapeDtypeStruct((EXT, EXT // 4, 16, 128), bf16),
            jax.ShapeDtypeStruct((3, SIDE + 16, SIDE), f32),
        ],
        in_specs=[pl.BlockSpec(memory_space=pltpu.VMEM)] * 2,
        out_specs=[pl.BlockSpec(memory_space=pltpu.VMEM)] * 2,
        scratch_shapes=[
            pltpu.VMEM((2, 4, SIDE, 128), f32),
            pltpu.VMEM((NB * NB * 4, 128), f32),
            pltpu.VMEM((8, 8, SIDE), f32),
            pltpu.VMEM((2, 8, SIDE), f32),
            pltpu.VMEM((2, SIDE + 16, 128), f32),
            pltpu.SemaphoreType.DMA((16,)),
            pltpu.SemaphoreType.DMA((16,)),
        ],
        compiler_params=pltpu.CompilerParams(
            vmem_limit_bytes=VMEM_BYTES, collective_id=1, has_side_effects=True
        ),
        name="front",
    )(far, pillar)


def rounded(value):
    return lax.reduce_precision(value, 8, 7)


def first_weights(w_in, b_in):
    w = w_in.reshape(HIDDEN, 3, 3)
    w1 = rounded(w)
    w2 = rounded(w - w1)
    b1 = rounded(b_in)
    b2 = rounded(b_in - b1)
    b3 = b_in - b1 - b2
    cells = jnp.stack([w1, w2, w1, w2, w1], 3).reshape(HIDDEN, 3, 15)
    bias = jnp.stack([b1, b2, b3], 1)[:, :, None]
    one = jnp.concatenate([cells, bias], 2).reshape(HIDDEN, 48)
    return jnp.concatenate(
        [jnp.pad(one, ((0, 0), (16 * r, 48 - 16 * r))) for r in range(4)], 0
    ).astype(bf16)


def back_weights(w_in, w_out):
    v = (w_in.T[None] * w_out[:, None, :]).reshape(18, HIDDEN)
    v1 = rounded(v)
    v2 = v - v1
    wide = jnp.concatenate(
        [
            jnp.pad(jnp.concatenate([v1, v1], 1), ((0, 6), (0, 0))),
            jnp.pad(v2, ((0, 6), (0, HIDDEN))),
        ],
        0,
    )
    upper = jnp.pad(wide, ((0, 0), (0, 2 * HIDDEN)))
    lower = jnp.pad(wide, ((0, 0), (2 * HIDDEN, 0)))
    return jnp.concatenate([upper, lower], 0).astype(bf16)


def local(far_adjoint, pillar, green_blocks, pair_src, pair_dst, group_end, w_in, b_in, w_out):
    ext, p3 = front(far_adjoint, pillar)
    near = sparse_near(
        pair_dst.reshape(-1),
        group_end.reshape(-1),
        pair_src.reshape(-1),
        ext.reshape(EXT * EXT * 4, 128),
        green_blocks,
    )
    grad, west, east, sums = cell_model(
        p3,
        near,
        first_weights(w_in, b_in),
        back_weights(w_in, w_out),
        jnp.pad(w_out, ((0, 6), (0, HIDDEN))),
    )
    grad, sums = finish(grad, west, east, sums)
    return (
        grad,
        sums[0:9, 0:HIDDEN].T,
        sums[9, 0:HIDDEN],
        sums[10].reshape(2, HIDDEN),
    )


def finish_kernel(
    shape,
    grad_ref,
    west_ref,
    east_ref,
    msg_ref,
    out_ref,
    sums_ref,
    row_out,
    row_in,
    col_out,
    col_in,
    cols,
    buf_a,
    buf_b,
    row_send,
    row_recv,
    col_send,
    col_recv,
    send_a,
    recv_a,
    send_b,
    recv_b,
):
    nx, ny = shape
    tx = lax.axis_index("tx")
    ty = lax.axis_index("ty")

    barrier = pltpu.get_barrier_semaphore()
    for d in range(1, nx):
        pl.semaphore_signal(
            barrier, inc=1, device_id=(lax.rem(tx + d, nx), ty), device_id_type=MESH
        )
    for d in range(1, ny):
        pl.semaphore_signal(
            barrier, inc=1, device_id=(tx, lax.rem(ty + d, ny)), device_id_type=MESH
        )
    if nx + ny > 2:
        pl.semaphore_wait(barrier, nx + ny - 2)

    def line(side, which):
        out, into, send, recv, axis = which
        at = (tx, ty)[axis] + 2 * side - 1
        device = (at, ty) if axis == 0 else (tx, at)
        return pltpu.make_async_remote_copy(
            src_ref=out.at[side],
            dst_ref=into.at[side],
            send_sem=send.at[side],
            recv_sem=recv.at[side],
            device_id=device,
            device_id_type=MESH,
        )

    rows = (row_out, row_in, row_send, row_recv, 0)
    columns = (col_out, col_in, col_send, col_recv, 1)

    def has(side, index, count):
        return index > 0 if side == 0 else index < count - 1

    row_out[0, :, 0:128] = west_ref[0:8, :]
    row_out[0, :, 128 : 128 + SIDE] = grad_ref[0:8, :]
    row_out[0, :, 128 + SIDE : 256 + SIDE] = east_ref[0:8, :]
    row_out[1, :, 0:128] = west_ref[SIDE + 8 : SIDE + 16, :]
    row_out[1, :, 128 : 128 + SIDE] = grad_ref[SIDE + 8 : SIDE + 16, :]
    row_out[1, :, 128 + SIDE : 256 + SIDE] = east_ref[SIDE + 8 : SIDE + 16, :]
    for side in range(2):
        pl.when(has(side, tx, nx))(lambda side=side: line(side, rows).start())

    def sums_copy(d, buf, send, recv, index, count, axis):
        other = lax.rem(index + d, count)
        return pltpu.make_async_remote_copy(
            src_ref=buf.at[index],
            dst_ref=buf.at[index],
            send_sem=send.at[d],
            recv_sem=recv.at[index],
            device_id=(other, ty) if axis == 0 else (tx, other),
            device_id_type=MESH,
        )

    def sums_wait(d, buf, send, recv, index, count, axis):
        sender = lax.rem(index + d, count)
        pltpu.make_async_remote_copy(
            src_ref=buf.at[sender],
            dst_ref=buf.at[sender],
            send_sem=send.at[d],
            recv_sem=recv.at[sender],
            device_id=(sender, ty) if axis == 0 else (tx, sender),
            device_id_type=MESH,
        ).wait_recv()

    along_x = (buf_a, send_a, recv_a, tx, nx, 0)
    along_y = (buf_b, send_b, recv_b, ty, ny, 1)
    buf_a[tx] = msg_ref[...]
    for d in range(1, nx):
        sums_copy(d, *along_x).start()

    def copy(i, carry):
        at = pl.multiple_of(i * 8, 8)
        out_ref[pl.ds(at, 8), :] = grad_ref[pl.ds(at + 8, 8), :]
        cols[0, pl.ds(at, 8), :] = west_ref[pl.ds(at + 8, 8), :]
        cols[1, pl.ds(at, 8), :] = east_ref[pl.ds(at + 8, 8), :]
        return carry

    lax.fori_loop(0, SIDE // 8, copy, 0)
    for side, row, first in ((0, 7, SIDE - 8), (1, 0, 0)):

        @pl.when(has(1 - side, tx, nx))
        def _(side=side, row=row, first=first):
            line(side, rows).wait_recv()
            got = row_in[side]
            got = jnp.where(
                lax.broadcasted_iota(jnp.int32, got.shape, 0) == row, got, 0.0
            )
            out_ref[first : first + 8, :] += got[:, 128 : 128 + SIDE]
            cols[0, first : first + 8, :] += got[:, 0:128]
            cols[1, first : first + 8, :] += got[:, 128 + SIDE : 256 + SIDE]

    for q in range(4):
        tile = slice(128 * q, 128 * q + 128)
        col_out[0, :, tile] = cols[0, tile, :].T[0:8]
        col_out[1, :, tile] = cols[1, tile, :].T[120:128]
    for side in range(2):
        pl.when(has(side, ty, ny))(lambda side=side: line(side, columns).start())

    for d in range(1, nx):
        sums_wait(d, *along_x)
    value = buf_a[0]
    for d in range(1, nx):
        value = value + buf_a[d]
    buf_b[ty] = value
    for d in range(1, ny):
        sums_copy(d, *along_y).start()

    lane = lax.broadcasted_iota(jnp.int32, (128, 128), 1)
    for side, row, first, spot in ((0, 0, SIDE - 128, 127), (1, 7, 0, 0)):

        @pl.when(has(1 - side, ty, ny))
        def _(side=side, row=row, first=first, spot=spot):
            line(side, columns).wait_recv()
            for q in range(4):
                tile = slice(128 * q, 128 * q + 128)
                got = jnp.broadcast_to(col_in[side, row : row + 1, tile], (128, 128)).T
                out_ref[tile, first : first + 128] += jnp.where(lane == spot, got, 0.0)

    for d in range(1, ny):
        sums_wait(d, *along_y)
    value = buf_b[0]
    for d in range(1, ny):
        value = value + buf_b[d]
    sums_ref[...] = value * (float(SIDE * SIDE * nx * ny) ** (-0.5))
    for side in range(2):
        pl.when(has(side, tx, nx))(lambda side=side: line(side, rows).wait_send())
        pl.when(has(side, ty, ny))(lambda side=side: line(side, columns).wait_send())
    for d in range(1, nx):
        sums_copy(d, *along_x).wait_send()
    for d in range(1, ny):
        sums_copy(d, *along_y).wait_send()


def finish(grad, west, east, sums):
    nx, ny = lax.axis_size("tx"), lax.axis_size("ty")
    dma = pltpu.SemaphoreType.DMA
    return pl.pallas_call(
        functools.partial(finish_kernel, (nx, ny)),
        out_shape=[
            jax.ShapeDtypeStruct((SIDE, SIDE), f32),
            jax.ShapeDtypeStruct((16, 128), f32),
        ],
        in_specs=[pl.BlockSpec(memory_space=pltpu.VMEM)] * 4,
        out_specs=[pl.BlockSpec(memory_space=pltpu.VMEM)] * 2,
        scratch_shapes=[
            pltpu.VMEM((2, 8, SIDE + 256), f32),
            pltpu.VMEM((2, 8, SIDE + 256), f32),
            pltpu.VMEM((2, 8, SIDE), f32),
            pltpu.VMEM((2, 8, SIDE), f32),
            pltpu.VMEM((2, SIDE, 128), f32),
            pltpu.VMEM((nx, 16, 128), f32),
            pltpu.VMEM((ny, 16, 128), f32),
            dma((2,)),
            dma((2,)),
            dma((2,)),
            dma((2,)),
            dma((nx,)),
            dma((nx,)),
            dma((ny,)),
            dma((ny,)),
        ],
        compiler_params=pltpu.CompilerParams(
            vmem_limit_bytes=VMEM_BYTES, collective_id=0, has_side_effects=True
        ),
        name="finish",
    )(grad, west, east, sums)


def solution(mesh):
    return jax.shard_map(
        local,
        mesh=mesh,
        in_specs=(
            P(None, "tx", "ty"),
            P("tx", "ty"),
            P(),
            P("tx", "ty", None),
            P("tx", "ty", None),
            P("tx", "ty", None),
            P(),
            P(),
            P(),
        ),
        out_specs=(P("tx", "ty"), P(), P(), P()),
        check_vma=False,
    )
```

```python
import functools

import jax
import jax.numpy as jnp
from jax import lax
from jax.experimental import pallas as pl
from jax.experimental.pallas import tpu as pltpu
from jax.sharding import PartitionSpec as P

BLK = 16
CONE = 12
SIDE = 512
NB = SIDE // BLK
EXT = NB + 2 * CONE
GROUPS = 8
CHUNK = 512
PARTS = 1
HIDDEN = 64
PADROWS = 16
SROWS = 24
VMEM_BYTES = 60 * 1024 * 1024

f32 = jnp.float32
bf16 = jnp.bfloat16
MESH = pl.DeviceIdType.MESH


def swap_pieces(vectors):
    lane = lax.broadcasted_iota(jnp.int32, (8, 128), 1) // 16
    for d in (1, 2, 4):
        mixed = []
        for x in range(8):
            if x & d:
                moved = pltpu.roll(vectors[x ^ d], 128 - 16 * d, 1)
                mixed.append(jnp.where((lane & d) == 0, moved, vectors[x]))
            else:
                moved = pltpu.roll(vectors[x ^ d], 16 * d, 1)
                mixed.append(jnp.where((lane & d) == 0, vectors[x], moved))
        vectors = mixed
    return vectors


def sparse_kernel(
    dst_ref, ends_ref, src_ref, ext_ref, green_ref, near_ref, table, rows, rows16, stack, seg, acc
):
    chunks = dst_ref.shape[0] // CHUNK

    def widen(i, carry):
        at = pl.ds(pl.multiple_of(i * 128, 128), 128)
        table[at, :] = ext_ref[at, :].astype(f32)
        return carry

    lax.fori_loop(0, EXT * EXT * 4 // 128, widen, 0)
    acc[...] = jnp.zeros_like(acc)

    def gather(base, first, count):
        for q in range(first, first + count):
            d = dst_ref[base + q] * 4
            rows[4 * q : 4 * q + 4, :] = table[pl.ds(pl.multiple_of(d, 4), 4), :]

    def narrow():
        for j in range(4):
            rows16[:, 128 * j : 128 * j + 128] = rows[
                pl.ds(j, CHUNK, stride=4), :
            ].astype(bf16)

    gather(0, 0, CHUNK)
    narrow()

    def group(k, carry):
        start = jnp.where(k == 0, 0, ends_ref[jnp.maximum(k - 1, 0)])
        stop = ends_ref[k]
        seg[...] = jnp.zeros_like(seg)

        def chunk(c, inner):
            ahead = jnp.minimum(c + 1, chunks - 1) * CHUNK
            slot = c * CHUNK + lax.broadcasted_iota(jnp.int32, (1, CHUNK), 1)
            live = (slot >= start) & (slot < stop)
            source = jnp.where(live, src_ref[c], -1)
            for m in range(PARTS):
                size = NB * NB // PARTS
                ids = lax.broadcasted_iota(jnp.int32, (size, CHUNK), 0) + size * m
                hot = jnp.where(ids == source, 1.0, 0.0).astype(bf16)
                gather(ahead, CHUNK // PARTS * m, CHUNK // PARTS)
                seg[size * m : size * m + size, :] += jnp.dot(
                    hot, rows16[...], preferred_element_type=f32
                )
            pl.when((c + 1) * CHUNK <= stop)(narrow)
            return inner

        lax.fori_loop(start // CHUNK, (stop + CHUNK - 1) // CHUNK, chunk, 0)

        half = BLK * BLK
        real = green_ref[k, 0]
        imag = green_ref[k, 1]
        stack[0:half, 0:half] = real
        stack[0:half, half : 2 * half] = -imag
        stack[half : 2 * half, 0:half] = imag
        stack[half : 2 * half, half : 2 * half] = real

        def apply(m, inner):
            at = pl.ds(pl.multiple_of(m * 512, 512), 512)
            value = seg[at, :]
            high = value.astype(bf16)
            low = (value - high.astype(f32)).astype(bf16)
            near = jnp.dot(high, stack[...], preferred_element_type=f32) + jnp.dot(
                low, stack[...], preferred_element_type=f32
            )
            for j in range(4):
                acc[j, at, :] += near[:, 128 * j : 128 * j + 128]
            return inner

        lax.fori_loop(0, 2, apply, 0)
        return carry

    lax.fori_loop(0, GROUPS, group, 0)

    def lay(i, carry):
        for j in range(4):
            for t in range(SIDE // 128):
                vectors = [
                    acc[j, pl.ds(i * 256 + 8 * t + b, 8, stride=NB), :] for b in range(8)
                ]
                for x, v in enumerate(swap_pieces(vectors)):
                    at = pl.ds(PADROWS + i * 128 + 8 * (j % 2) + x, 8, stride=BLK)
                    near_ref[j // 2, t, at, :] = v
        return carry

    lax.fori_loop(0, NB // 8, lay, 0)
    for c in range(2):
        for t in range(4):
            near_ref[c, t, 0:PADROWS, :] = jnp.zeros((PADROWS, 128), f32)
            near_ref[c, t, PADROWS + SIDE : 2 * PADROWS + SIDE, :] = jnp.zeros(
                (PADROWS, 128), f32
            )


def sparse_near(targets, ends, sources, ext, green):
    slots = targets.shape[0]
    return pl.pallas_call(
        sparse_kernel,
        out_shape=jax.ShapeDtypeStruct((2, 4, SIDE + 2 * PADROWS, 128), f32),
        in_specs=[
            pl.BlockSpec(memory_space=pltpu.SMEM),
            pl.BlockSpec(memory_space=pltpu.SMEM),
            pl.BlockSpec(memory_space=pltpu.VMEM),
            pl.BlockSpec(memory_space=pltpu.VMEM),
            pl.BlockSpec(memory_space=pltpu.VMEM),
        ],
        out_specs=pl.BlockSpec(memory_space=pltpu.VMEM),
        scratch_shapes=[
            pltpu.VMEM((EXT * EXT * 4, 128), f32),
            pltpu.VMEM((CHUNK * 4, 128), f32),
            pltpu.VMEM((CHUNK, 512), bf16),
            pltpu.VMEM((512, 512), bf16),
            pltpu.VMEM((NB * NB, 512), f32),
            pltpu.VMEM((4, NB * NB, 128), f32),
        ],
        compiler_params=pltpu.CompilerParams(vmem_limit_bytes=VMEM_BYTES),
        name="sparse_near",
    )(
        targets,
        ends,
        sources.reshape(slots // CHUNK, 1, CHUNK),
        ext,
        green,
    )


def split2(value):
    high = value.astype(bf16).astype(f32)
    return high, value - high


def put(ref, start, stride, value):
    for t in range(SIDE // 128):
        ref[t, pl.ds(start, 8, stride=stride), :] = value[:, 128 * t : 128 * t + 128]


def take(ref, start, stride):
    tiles = [ref[t, pl.ds(start, 8, stride=stride), :] for t in range(SIDE // 128)]
    return jnp.concatenate(tiles, 1)


def greet(nx, ny, tx, ty):
    barrier = pltpu.get_barrier_semaphore()
    for d in range(1, nx):
        pl.semaphore_signal(
            barrier, inc=1, device_id=(lax.rem(tx + d, nx), ty), device_id_type=MESH
        )
    for d in range(1, ny):
        pl.semaphore_signal(
            barrier, inc=1, device_id=(tx, lax.rem(ty + d, ny)), device_id_type=MESH
        )


def finish(
    shape,
    grad_ref,
    west_ref,
    east_ref,
    message,
    out_ref,
    first_ref,
    bias_ref,
    second_ref,
    row_out,
    row_in,
    col_out,
    col_in,
    cols,
    buf_a,
    buf_b,
    row_send,
    row_recv,
    col_send,
    col_recv,
    send_a,
    recv_a,
    send_b,
    recv_b,
):
    nx, ny = shape
    tx = lax.axis_index("tx")
    ty = lax.axis_index("ty")

    pl.semaphore_wait(pltpu.get_barrier_semaphore(), nx + ny - 2)

    def line(side, which):
        out, into, send, recv, axis = which
        at = (tx, ty)[axis] + 2 * side - 1
        device = (at, ty) if axis == 0 else (tx, at)
        return pltpu.make_async_remote_copy(
            src_ref=out.at[side],
            dst_ref=into.at[side],
            send_sem=send.at[side],
            recv_sem=recv.at[side],
            device_id=device,
            device_id_type=MESH,
        )

    rows = (row_out, row_in, row_send, row_recv, 0)
    columns = (col_out, col_in, col_send, col_recv, 1)

    def has(side, index, count):
        return index > 0 if side == 0 else index < count - 1

    def sums_copy(d, buf, send, recv, index, count, axis):
        other = lax.rem(index + d, count)
        return pltpu.make_async_remote_copy(
            src_ref=buf.at[index],
            dst_ref=buf.at[index],
            send_sem=send.at[d],
            recv_sem=recv.at[index],
            device_id=(other, ty) if axis == 0 else (tx, other),
            device_id_type=MESH,
        )

    def sums_wait(d, buf, send, recv, index, count, axis):
        sender = lax.rem(index + d, count)
        pltpu.make_async_remote_copy(
            src_ref=buf.at[sender],
            dst_ref=buf.at[sender],
            send_sem=send.at[d],
            recv_sem=recv.at[sender],
            device_id=(sender, ty) if axis == 0 else (tx, sender),
            device_id_type=MESH,
        ).wait_recv()

    along_x = (buf_a, send_a, recv_a, tx, nx, 0)
    along_y = (buf_b, send_b, recv_b, ty, ny, 1)
    buf_a[tx] = message
    for d in range(1, nx):
        sums_copy(d, *along_x).start()

    row_out[0, :, 0:128] = west_ref[0:8, :]
    row_out[0, :, 128 : 128 + SIDE] = grad_ref[0:8, :]
    row_out[0, :, 128 + SIDE : 256 + SIDE] = east_ref[0:8, :]
    row_out[1, :, 0:128] = west_ref[SIDE + 8 : SIDE + 16, :]
    row_out[1, :, 128 : 128 + SIDE] = grad_ref[SIDE + 8 : SIDE + 16, :]
    row_out[1, :, 128 + SIDE : 256 + SIDE] = east_ref[SIDE + 8 : SIDE + 16, :]
    for side in range(2):
        pl.when(has(side, tx, nx))(lambda side=side: line(side, rows).start())

    def copy(i, carry):
        at = pl.multiple_of(i * 8, 8)
        out_ref[pl.ds(at, 8), :] = grad_ref[pl.ds(at + 8, 8), :]
        cols[0, pl.ds(at, 8), :] = west_ref[pl.ds(at + 8, 8), :]
        cols[1, pl.ds(at, 8), :] = east_ref[pl.ds(at + 8, 8), :]
        return carry

    lax.fori_loop(0, SIDE // 8, copy, 0)
    for d in range(1, nx):
        sums_wait(d, *along_x)
    value = buf_a[0]
    for d in range(1, nx):
        value = value + buf_a[d]
    buf_b[ty] = value
    for d in range(1, ny):
        sums_copy(d, *along_y).start()

    for side, row, first in ((0, 7, SIDE - 8), (1, 0, 0)):

        @pl.when(has(1 - side, tx, nx))
        def _(side=side, row=row, first=first):
            line(side, rows).wait_recv()
            got = row_in[side]
            got = jnp.where(
                lax.broadcasted_iota(jnp.int32, got.shape, 0) == row, got, 0.0
            )
            out_ref[first : first + 8, :] += got[:, 128 : 128 + SIDE]
            cols[0, first : first + 8, :] += got[:, 0:128]
            cols[1, first : first + 8, :] += got[:, 128 + SIDE : 256 + SIDE]

    for q in range(4):
        tile = slice(128 * q, 128 * q + 128)
        col_out[0, :, tile] = cols[0, tile, :].T[0:8]
        col_out[1, :, tile] = cols[1, tile, :].T[120:128]
    for side in range(2):
        pl.when(has(side, ty, ny))(lambda side=side: line(side, columns).start())

    lane = lax.broadcasted_iota(jnp.int32, (128, 128), 1)
    for side, row, first, spot in ((0, 0, SIDE - 128, 127), (1, 7, 0, 0)):

        @pl.when(has(1 - side, ty, ny))
        def _(side=side, row=row, first=first, spot=spot):
            line(side, columns).wait_recv()
            for q in range(4):
                tile = slice(128 * q, 128 * q + 128)
                got = jnp.broadcast_to(col_in[side, row : row + 1, tile], (128, 128)).T
                out_ref[tile, first : first + 128] += jnp.where(lane == spot, got, 0.0)

    for d in range(1, ny):
        sums_wait(d, *along_y)
    value = buf_b[0]
    for d in range(1, ny):
        value = value + buf_b[d]
    value = value * (float(SIDE * SIDE * nx * ny) ** (-0.5))
    first_ref[...] = value.T[0:HIDDEN, 0:9]
    bias_ref[...] = value[9:10, 0:HIDDEN]
    second_ref[0:1, :] = value[10:11, 0:HIDDEN]
    second_ref[1:2, :] = pltpu.roll(value, HIDDEN, 1)[10:11, 0:HIDDEN]
    for side in range(2):
        pl.when(has(side, tx, nx))(lambda side=side: line(side, rows).wait_send())
        pl.when(has(side, ty, ny))(lambda side=side: line(side, columns).wait_send())
    for d in range(1, nx):
        sums_copy(d, *along_x).wait_send()
    for d in range(1, ny):
        sums_copy(d, *along_y).wait_send()


def cell_kernel(
    shape,
    p3_ref,
    near_ref,
    w1_ref,
    v_ref,
    wout_ref,
    out_ref,
    first_ref,
    bias_ref,
    second_ref,
    grad_ref,
    west_ref,
    east_ref,
    q32,
    qs,
    gs,
    ps,
    total,
    nh,
    first_buf,
    second_buf,
    *exchange,
):
    width = SIDE
    nx, ny = shape
    greet(nx, ny, lax.axis_index("tx"), lax.axis_index("ty"))

    def near_rows(c, first, count):
        at = pl.ds(pl.multiple_of(first, 8), count)
        return jnp.concatenate([near_ref[c, t, at, :] for t in range(4)], 1)

    def build(i, carry):
        r0 = pl.multiple_of(i * 8, 8)
        for b in range(3):
            x = p3_ref[b, pl.ds(r0, 8), :]
            x1, rest = split2(x)
            x2, x3 = split2(rest)
            for n, piece in enumerate((x1, x1, x2, x2, x3)):
                put(q32, b * 5 + n, 16, piece)
        put(q32, 15, 16, jnp.ones((8, width), f32))
        for t in range(4):
            qs[pl.ds(r0, 8), :, 128 * t : 128 * t + 128] = (
                q32[t].astype(bf16).reshape(8, 16, 128)
            )
        return carry

    lax.fori_loop(0, 3, build, 0)
    total[...] = jnp.zeros_like(total)
    nh[...] = jnp.zeros_like(nh)
    gs[...] = jnp.zeros_like(gs)
    zero_rows = jnp.zeros((PADROWS * SROWS, 128), f32)
    for t in range(4):
        ps[t, 0 : PADROWS * SROWS, :] = zero_rows
        ps[t, (PADROWS + SIDE) * SROWS : (2 * PADROWS + SIDE) * SROWS, :] = zero_rows

    lane = lax.broadcasted_iota(jnp.int32, (8, width), 1)

    def combine(i, carry):
        parts = []
        deep = [near_rows(c, i * 8, 24) for c in range(2)]
        for b in range(3):
            acc = None
            for a in range(3):
                x0 = i * 8 + 9 - a
                for c in range(2):
                    term = deep[c][9 - a : 17 - a] * take(
                        ps, x0 * SROWS + 9 * c + 3 * a + b, SROWS
                    )
                    acc = term if acc is None else acc + term
            parts.append(acc)
        low = jnp.where(lane == width - 1, 0.0, pltpu.roll(parts[0], width - 1, 1))
        high = jnp.where(lane == 0, 0.0, pltpu.roll(parts[2], 1, 1))
        at = pl.ds(pl.multiple_of(i * 8, 8), 8)
        grad_ref[at, :] = parts[1] + low + high
        west_ref[at, :] = parts[0][:, 0:128]
        east_ref[at, :] = parts[2][:, width - 128 : width]
        return carry

    def strip(i, carry):
        r0 = pl.multiple_of(i * 8, 8)
        n = [near_rows(c, r0 + PADROWS, 8) for c in range(2)]
        deep = [p3_ref[b, pl.ds(r0, 24), :] for b in range(3)]
        for a in range(3):
            for b in range(3):
                feat = deep[b][7 + a : 15 + a]
                for c in range(2):
                    put(gs, 10 * c + 3 * a + b, SROWS, n[c] * feat)
        for c in range(2):
            put(gs, 10 * c + 9, SROWS, n[c])

        def make_next():
            build(jnp.minimum(i + 3, SIDE // 8 + 1), 0)

        def finish_last():
            combine(jnp.maximum(i - 1, 0), 0)

        after = [near_rows(c, r0 + PADROWS + 8, 8)[0:4] for c in range(2)]
        step(r0, 0, r0 + 4, [n[c][4:8] for c in range(2)], first_buf, second_buf, make_next)
        step(r0, 4, r0 + 8, after, second_buf, first_buf, finish_last)
        return carry

    def hidden(x0):
        feats = qs[pl.ds(x0 + 7, 6)].reshape(96, width)
        return jnp.dot(w1_ref[...], feats, preferred_element_type=f32)

    def activate(z, r, n, into, partial):
        hr = jnp.tanh(z[HIDDEN * r : HIDDEN * r + HIDDEN])
        u = 1.0 - hr * hr
        u1 = u.astype(bf16)
        into[2 * HIDDEN * r : 2 * HIDDEN * r + HIDDEN, :] = u1
        into[2 * HIDDEN * r + HIDDEN : 2 * HIDDEN * r + 2 * HIDDEN, :] = (
            u - u1.astype(f32)
        ).astype(bf16)
        for c in range(2):
            for t in range(4):
                tile = slice(128 * t, 128 * t + 128)
                term = n[c][r : r + 1, tile] * hr[:, tile]
                partial[c] = term if partial[c] is None else partial[c] + term

    def back(r0, j, pair, held):
        slope = jnp.dot(
            v_ref[...],
            held[4 * HIDDEN * pair : 4 * HIDDEN * pair + 4 * HIDDEN, :],
            preferred_element_type=f32,
        )
        for r in range(2):
            one = (
                slope[2 * SROWS * r : 2 * SROWS * r + SROWS]
                + slope[2 * SROWS * r + SROWS : 2 * SROWS * r + 2 * SROWS]
            )
            at = pl.ds(pl.multiple_of((r0 + PADROWS + j + 2 * pair + r) * SROWS, 8), SROWS)
            for t in range(4):
                ps[t, at, :] = one[:, 128 * t : 128 * t + 128]

    def sums(j, pair, held):
        left, right = [], []
        for r in range(2 * pair, 2 * pair + 2):
            first = SROWS * (j + r)
            g = jnp.concatenate([gs[t, first : first + SROWS, :] for t in range(4)], 1)
            left.append(held[2 * HIDDEN * r : 2 * HIDDEN * r + 2 * HIDDEN, :])
            right.append(jnp.concatenate(split2(g), 0).astype(bf16))
        return lax.dot_general(
            jnp.concatenate(left, 1),
            jnp.concatenate(right, 1),
            (((1,), (1,)), ((), ())),
            preferred_element_type=f32,
        )

    def step(r0, j, x0, n, held, into, extra):
        partial = [None, None]
        z = hidden(x0)
        activate(z, 0, n, into, partial)
        back(r0, j, 0, held)
        activate(z, 1, n, into, partial)
        one = sums(j, 0, held)
        activate(z, 2, n, into, partial)
        back(r0, j, 1, held)
        activate(z, 3, n, into, partial)
        extra()
        two = sums(j, 1, held)
        total[:, 0 : 2 * SROWS] += one + two
        for c in range(2):
            nh[HIDDEN * c : HIDDEN * c + HIDDEN, :] += partial[c]

    partial = [None, None]
    z = hidden(0)
    for r in range(4):
        activate(z, r, [near_rows(c, PADROWS, 8) for c in range(2)], first_buf, partial)
    for c in range(2):
        nh[HIDDEN * c : HIDDEN * c + HIDDEN, :] += partial[c]
    lax.fori_loop(0, SIDE // 8, strip, 0)
    lax.fori_loop(SIDE // 8 - 1, SIDE // 8 + 2, combine, 0)
    turned = total[...].T
    turned = turned + pltpu.roll(turned, HIDDEN, 1)
    pulled = turned[0:SROWS] + turned[SROWS : 2 * SROWS]
    first = wout_ref[0:1, :] * pulled[0:10] + wout_ref[1:2, :] * pulled[10:20]
    second = jnp.sum(nh[...].T, axis=0, keepdims=True)
    message = jnp.concatenate([first, second, jnp.zeros((5, 128), f32)], 0)
    finish(
        shape,
        grad_ref,
        west_ref,
        east_ref,
        message,
        out_ref,
        first_ref,
        bias_ref,
        second_ref,
        *exchange,
    )


def cell_model(p3, near, first, back, out_weights):
    nx, ny = lax.axis_size("tx"), lax.axis_size("ty")
    dma = pltpu.SemaphoreType.DMA
    rows = SIDE + 16
    return pl.pallas_call(
        functools.partial(cell_kernel, (nx, ny)),
        out_shape=[
            jax.ShapeDtypeStruct((SIDE, SIDE), f32),
            jax.ShapeDtypeStruct((HIDDEN, 9), f32),
            jax.ShapeDtypeStruct((1, HIDDEN), f32),
            jax.ShapeDtypeStruct((2, HIDDEN), f32),
        ],
        in_specs=[pl.BlockSpec(memory_space=pltpu.VMEM)] * 5,
        out_specs=[pl.BlockSpec(memory_space=pltpu.VMEM)] * 4,
        scratch_shapes=[
            pltpu.VMEM((rows, SIDE), f32),
            pltpu.VMEM((rows, 128), f32),
            pltpu.VMEM((rows, 128), f32),
            pltpu.VMEM((4, 128, 128), f32),
            pltpu.VMEM((rows, 16, SIDE), bf16),
            pltpu.VMEM((4, 8 * SROWS, 128), f32),
            pltpu.VMEM((4, (SIDE + 2 * PADROWS) * SROWS, 128), f32),
            pltpu.VMEM((128, 128), f32),
            pltpu.VMEM((128, 128), f32),
            pltpu.VMEM((8 * HIDDEN, SIDE), bf16),
            pltpu.VMEM((8 * HIDDEN, SIDE), bf16),
            pltpu.VMEM((2, 8, SIDE + 256), f32),
            pltpu.VMEM((2, 8, SIDE + 256), f32),
            pltpu.VMEM((2, 8, SIDE), f32),
            pltpu.VMEM((2, 8, SIDE), f32),
            pltpu.VMEM((2, SIDE, 128), f32),
            pltpu.VMEM((nx, 16, 128), f32),
            pltpu.VMEM((ny, 16, 128), f32),
            dma((2,)),
            dma((2,)),
            dma((2,)),
            dma((2,)),
            dma((nx,)),
            dma((nx,)),
            dma((ny,)),
            dma((ny,)),
        ],
        compiler_params=pltpu.CompilerParams(
            vmem_limit_bytes=VMEM_BYTES, collective_id=0, has_side_effects=True
        ),
        name="cell_model",
    )(p3, near, first, back, out_weights)


AROUND = [(dx, dy) for dx in (-1, 0, 1) for dy in (-1, 0, 1) if (dx, dy) != (0, 0)]


def front_kernel(
    shape, far_ref, pillar_ref, ext_ref, p3_ref, field, flat, edge_in, turned, side, sends, recvs
):
    nx, ny = shape
    tx = lax.axis_index("tx")
    ty = lax.axis_index("ty")
    barrier = pltpu.get_barrier_semaphore()
    for dx, dy in AROUND:
        pl.semaphore_signal(
            barrier,
            inc=1,
            device_id=(lax.rem(tx + dx + nx, nx), lax.rem(ty + dy + ny, ny)),
            device_id_type=MESH,
        )

    for q in range(4):
        tile = slice(128 * q, 128 * q + 128)
        turned[0, :, tile] = pillar_ref[tile, 0:128].T[0:8]
        turned[1, :, tile] = pillar_ref[tile, SIDE - 128 : SIDE].T[120:128]
    pl.semaphore_wait(barrier, len(AROUND))

    def there(dx, dy):
        fits = None
        for delta, index, count in ((dx, tx, nx), (dy, ty, ny)):
            if delta:
                one = index > 0 if delta < 0 else index < count - 1
                fits = one if fits is None else jnp.logical_and(fits, one)
        return fits

    def rim(delta, length, reach):
        if delta < 0:
            return (0, reach), (length, reach)
        if delta > 0:
            return (length - reach, reach), (-reach, reach)
        return (0, length), (0, length)

    def far_copy(n):
        dx, dy = AROUND[n]
        (x, wx), (ox, _) = rim(dx, NB, CONE)
        (y, wy), (oy, _) = rim(dy, NB // 4, CONE // 4)
        return pltpu.make_async_remote_copy(
            src_ref=ext_ref.at[pl.ds(CONE + x, wx), pl.ds(CONE // 4 + y, wy)],
            dst_ref=ext_ref.at[pl.ds(CONE + ox, wx), pl.ds(CONE // 4 + oy, wy)],
            send_sem=sends.at[n],
            recv_sem=recvs.at[n],
            device_id=(tx + dx, ty + dy),
            device_id_type=MESH,
        )

    def edge_copy(n):
        dx, dy = AROUND[n]
        if dy == 0:
            source = pillar_ref.at[pl.ds(0 if dx < 0 else SIDE - 8, 8), :]
        elif dx == 0:
            source = turned.at[0 if dy < 0 else 1]
        else:
            source = pillar_ref.at[
                pl.ds(0 if dx < 0 else SIDE - 8, 8), pl.ds(0 if dy < 0 else SIDE - 128, 128)
            ]
        wide = SIDE if dx == 0 or dy == 0 else 128
        return pltpu.make_async_remote_copy(
            src_ref=source,
            dst_ref=edge_in.at[n, :, pl.ds(0, wide)],
            send_sem=sends.at[8 + n],
            recv_sem=recvs.at[8 + n],
            device_id=(tx + dx, ty + dy),
            device_id_type=MESH,
        )

    for n, (dx, dy) in enumerate(AROUND):
        pl.when(there(dx, dy))(lambda n=n: edge_copy(n).start())

    def spread(i, carry):
        at = pl.ds(pl.multiple_of(i * BLK, BLK), BLK)
        for c in range(2):
            strip = far_ref[c, at, :].astype(f32)
            for t in range(4):
                field[c, t, at, :] = strip[:, 128 * t : 128 * t + 128]
        return carry

    lax.fori_loop(0, SIDE // BLK, spread, 0)

    def turn(i, carry):
        for j in range(4):
            for t in range(4):
                first = i * 128 + 8 * (j % 2)
                vectors = [
                    field[j // 2, t, pl.ds(first + x, 8, stride=BLK), :] for x in range(8)
                ]
                for b, v in enumerate(swap_pieces(vectors)):
                    flat[pl.ds(i * 1024 + (8 * t + b) * 4 + j, 8, stride=128), :] = v
        return carry

    lax.fori_loop(0, NB // 8, turn, 0)

    def pack(r, carry):
        value = flat[pl.ds(pl.multiple_of(r * 128, 128), 128), :].astype(bf16)
        ext_ref[CONE + r, CONE // 4 : CONE // 4 + NB // 4] = value.reshape(NB // 4, 16, 128)
        return carry

    lax.fori_loop(0, NB, pack, 0)
    for n, (dx, dy) in enumerate(AROUND):
        pl.when(there(dx, dy))(lambda n=n: far_copy(n).start())

    for n, (dx, dy) in enumerate(AROUND):

        @pl.when(jnp.logical_not(there(dx, dy)))
        def _(n=n, dx=dx, dy=dy):
            edge_in[7 - n] = jnp.zeros((8, SIDE), f32)
            x = {-1: 0, 0: CONE, 1: CONE + NB}[dx]
            y = {-1: 0, 0: CONE // 4, 1: (CONE + NB) // 4}[dy]
            wy = CONE // 4 if dy else NB // 4

            def clear(i, carry):
                ext_ref[x + i, y : y + wy] = jnp.zeros((wy, 16, 128), bf16)
                return carry

            lax.fori_loop(0, CONE if dx else NB, clear, 0)

    for n, (dx, dy) in enumerate(AROUND):
        pl.when(there(dx, dy))(lambda n=n: edge_copy(7 - n).wait_recv())
    at_of = {place: n for n, place in enumerate(AROUND)}

    def got(dx, dy):
        return edge_in.at[7 - at_of[(dx, dy)]]

    for s, dy in ((0, -1), (1, 1)):
        lane = 127 if s == 0 else 0
        side[s, 0:8, :] = jnp.broadcast_to(got(-1, dy)[:, lane : lane + 1], (8, 128))
        side[s, SIDE + 8 : SIDE + 16, :] = jnp.broadcast_to(
            got(1, dy)[:, lane : lane + 1], (8, 128)
        )
        row = 7 if s == 0 else 0
        for q in range(4):
            tile = slice(128 * q, 128 * q + 128)
            side[s, 8 + 128 * q : 136 + 128 * q, :] = jnp.broadcast_to(
                got(0, dy)[row : row + 1, tile], (128, 128)
            ).T

    lanes = lax.broadcasted_iota(jnp.int32, (8, SIDE), 1)

    def shifted(at, value):
        p3_ref[1, at, :] = value
        west = jnp.concatenate([side[0, at, :]] * 4, 1)
        east = jnp.concatenate([side[1, at, :]] * 4, 1)
        p3_ref[0, at, :] = jnp.where(lanes == 0, west, pltpu.roll(value, 1, 1))
        p3_ref[2, at, :] = jnp.where(lanes == SIDE - 1, east, pltpu.roll(value, SIDE - 1, 1))

    def interior(i, carry):
        r0 = pl.multiple_of(i * 8, 8)
        shifted(pl.ds(r0 + 8, 8), pillar_ref[pl.ds(r0, 8), :])
        return carry

    lax.fori_loop(0, SIDE // 8, interior, 0)
    shifted(pl.ds(0, 8), got(-1, 0)[...])
    shifted(pl.ds(SIDE + 8, 8), got(1, 0)[...])

    for n, (dx, dy) in enumerate(AROUND):
        pl.when(there(dx, dy))(lambda n=n: far_copy(7 - n).wait_recv())
    for n, (dx, dy) in enumerate(AROUND):

        @pl.when(there(dx, dy))
        def _(n=n):
            far_copy(n).wait_send()
            edge_copy(n).wait_send()


def front(far, pillar):
    nx, ny = lax.axis_size("tx"), lax.axis_size("ty")
    return pl.pallas_call(
        functools.partial(front_kernel, (nx, ny)),
        out_shape=[
            jax.ShapeDtypeStruct((EXT, EXT // 4, 16, 128), bf16),
            jax.ShapeDtypeStruct((3, SIDE + 16, SIDE), f32),
        ],
        in_specs=[pl.BlockSpec(memory_space=pltpu.VMEM)] * 2,
        out_specs=[pl.BlockSpec(memory_space=pltpu.VMEM)] * 2,
        scratch_shapes=[
            pltpu.VMEM((2, 4, SIDE, 128), f32),
            pltpu.VMEM((NB * NB * 4, 128), f32),
            pltpu.VMEM((8, 8, SIDE), f32),
            pltpu.VMEM((2, 8, SIDE), f32),
            pltpu.VMEM((2, SIDE + 16, 128), f32),
            pltpu.SemaphoreType.DMA((16,)),
            pltpu.SemaphoreType.DMA((16,)),
        ],
        compiler_params=pltpu.CompilerParams(
            vmem_limit_bytes=VMEM_BYTES, collective_id=1, has_side_effects=True
        ),
        name="front",
    )(far, pillar)


def rounded(value):
    return lax.reduce_precision(value, 8, 7)


def first_weights(w_in, b_in):
    w = w_in.reshape(HIDDEN, 3, 3)
    w1 = rounded(w)
    w2 = rounded(w - w1)
    b1 = rounded(b_in)
    b2 = rounded(b_in - b1)
    b3 = b_in - b1 - b2
    cells = jnp.stack([w1, w2, w1, w2, w1], 3).reshape(HIDDEN, 3, 15)
    bias = jnp.stack([b1, b2, b3], 1)[:, :, None]
    one = jnp.concatenate([cells, bias], 2).reshape(HIDDEN, 48)
    return jnp.concatenate(
        [jnp.pad(one, ((0, 0), (16 * r, 48 - 16 * r))) for r in range(4)], 0
    ).astype(bf16)


def back_weights(w_in, w_out):
    v = (w_in.T[None] * w_out[:, None, :]).reshape(18, HIDDEN)
    v1 = rounded(v)
    v2 = v - v1
    wide = jnp.concatenate(
        [
            jnp.pad(jnp.concatenate([v1, v1], 1), ((0, 6), (0, 0))),
            jnp.pad(v2, ((0, 6), (0, HIDDEN))),
        ],
        0,
    )
    upper = jnp.pad(wide, ((0, 0), (0, 2 * HIDDEN)))
    lower = jnp.pad(wide, ((0, 0), (2 * HIDDEN, 0)))
    return jnp.concatenate([upper, lower], 0).astype(bf16)


def local(far_adjoint, pillar, green_blocks, pair_src, pair_dst, group_end, w_in, b_in, w_out):
    ext, p3 = front(far_adjoint, pillar)
    near = sparse_near(
        pair_dst.reshape(-1),
        group_end.reshape(-1),
        pair_src.reshape(-1),
        ext.reshape(EXT * EXT * 4, 128),
        green_blocks,
    )
    grad, grad_in, grad_bias, grad_out = cell_model(
        p3,
        near,
        first_weights(w_in, b_in),
        back_weights(w_in, w_out),
        jnp.pad(w_out, ((0, 6), (0, HIDDEN))),
    )
    return grad, grad_in, grad_bias.reshape(HIDDEN), grad_out


def solution(mesh):
    return jax.shard_map(
        local,
        mesh=mesh,
        in_specs=(
            P(None, "tx", "ty"),
            P("tx", "ty"),
            P(),
            P("tx", "ty", None),
            P("tx", "ty", None),
            P("tx", "ty", None),
            P(),
            P(),
            P(),
        ),
        out_specs=(P("tx", "ty"), P(), P(), P()),
        check_vma=False,
    )
```

```python
import functools

import jax
import jax.numpy as jnp
from jax import lax
from jax.experimental import pallas as pl
from jax.experimental.pallas import tpu as pltpu
from jax.sharding import PartitionSpec as P

BLK = 16
CONE = 12
SIDE = 512
NB = SIDE // BLK
EXT = NB + 2 * CONE
GROUPS = 8
CHUNK = 512
PARTS = 1
HIDDEN = 64
PADROWS = 16
SROWS = 24
VMEM_BYTES = 60 * 1024 * 1024

f32 = jnp.float32
bf16 = jnp.bfloat16
MESH = pl.DeviceIdType.MESH


def swap_pieces(vectors):
    lane = lax.broadcasted_iota(jnp.int32, (8, 128), 1) // 16
    for d in (1, 2, 4):
        mixed = []
        for x in range(8):
            if x & d:
                moved = pltpu.roll(vectors[x ^ d], 128 - 16 * d, 1)
                mixed.append(jnp.where((lane & d) == 0, moved, vectors[x]))
            else:
                moved = pltpu.roll(vectors[x ^ d], 16 * d, 1)
                mixed.append(jnp.where((lane & d) == 0, vectors[x], moved))
        vectors = mixed
    return vectors


def sparse_kernel(
    dst_ref, ends_ref, src_ref, ext_ref, green_ref, near_ref, table, rows, rows16, stack, seg, acc
):
    chunks = dst_ref.shape[0] // CHUNK

    def widen(i, carry):
        at = pl.ds(pl.multiple_of(i * 128, 128), 128)
        table[at, :] = ext_ref[at, :].astype(f32)
        return carry

    lax.fori_loop(0, EXT * EXT * 4 // 128, widen, 0)
    acc[...] = jnp.zeros_like(acc)

    def gather(base, first, count):
        for q in range(first, first + count):
            d = dst_ref[base + q] * 4
            rows[4 * q : 4 * q + 4, :] = table[pl.ds(pl.multiple_of(d, 4), 4), :]

    def narrow():
        for j in range(4):
            rows16[:, 128 * j : 128 * j + 128] = rows[
                pl.ds(j, CHUNK, stride=4), :
            ].astype(bf16)

    gather(0, 0, CHUNK)
    narrow()

    def group(k, carry):
        start = jnp.where(k == 0, 0, ends_ref[jnp.maximum(k - 1, 0)])
        stop = ends_ref[k]
        seg[...] = jnp.zeros_like(seg)

        def chunk(c, inner):
            ahead = jnp.minimum(c + 1, chunks - 1) * CHUNK
            slot = c * CHUNK + lax.broadcasted_iota(jnp.int32, (1, CHUNK), 1)
            live = (slot >= start) & (slot < stop)
            source = jnp.where(live, src_ref[c], -1)
            for m in range(PARTS):
                size = NB * NB // PARTS
                ids = lax.broadcasted_iota(jnp.int32, (size, CHUNK), 0) + size * m
                hot = jnp.where(ids == source, 1.0, 0.0).astype(bf16)
                gather(ahead, CHUNK // PARTS * m, CHUNK // PARTS)
                seg[size * m : size * m + size, :] += jnp.dot(
                    hot, rows16[...], preferred_element_type=f32
                )
            pl.when((c + 1) * CHUNK <= stop)(narrow)
            return inner

        lax.fori_loop(start // CHUNK, (stop + CHUNK - 1) // CHUNK, chunk, 0)

        half = BLK * BLK
        real = green_ref[k, 0]
        imag = green_ref[k, 1]
        stack[0:half, 0:half] = real
        stack[0:half, half : 2 * half] = -imag
        stack[half : 2 * half, 0:half] = imag
        stack[half : 2 * half, half : 2 * half] = real

        def apply(m, inner):
            at = pl.ds(pl.multiple_of(m * 512, 512), 512)
            value = seg[at, :]
            high = value.astype(bf16)
            low = (value - high.astype(f32)).astype(bf16)
            near = jnp.dot(high, stack[...], preferred_element_type=f32) + jnp.dot(
                low, stack[...], preferred_element_type=f32
            )
            for j in range(4):
                acc[j, at, :] += near[:, 128 * j : 128 * j + 128]
            return inner

        lax.fori_loop(0, 2, apply, 0)
        return carry

    lax.fori_loop(0, GROUPS, group, 0)

    def lay(i, carry):
        for j in range(4):
            for t in range(SIDE // 128):
                vectors = [
                    acc[j, pl.ds(i * 256 + 8 * t + b, 8, stride=NB), :] for b in range(8)
                ]
                for x, v in enumerate(swap_pieces(vectors)):
                    at = pl.ds(PADROWS + i * 128 + 8 * (j % 2) + x, 8, stride=BLK)
                    near_ref[j // 2, t, at, :] = v
        return carry

    lax.fori_loop(0, NB // 8, lay, 0)
    for c in range(2):
        for t in range(4):
            near_ref[c, t, 0:PADROWS, :] = jnp.zeros((PADROWS, 128), f32)
            near_ref[c, t, PADROWS + SIDE : 2 * PADROWS + SIDE, :] = jnp.zeros(
                (PADROWS, 128), f32
            )


def sparse_near(targets, ends, sources, ext, green):
    slots = targets.shape[0]
    return pl.pallas_call(
        sparse_kernel,
        out_shape=jax.ShapeDtypeStruct((2, 4, SIDE + 2 * PADROWS, 128), f32),
        in_specs=[
            pl.BlockSpec(memory_space=pltpu.SMEM),
            pl.BlockSpec(memory_space=pltpu.SMEM),
            pl.BlockSpec(memory_space=pltpu.VMEM),
            pl.BlockSpec(memory_space=pltpu.VMEM),
            pl.BlockSpec(memory_space=pltpu.VMEM),
        ],
        out_specs=pl.BlockSpec(memory_space=pltpu.VMEM),
        scratch_shapes=[
            pltpu.VMEM((EXT * EXT * 4, 128), f32),
            pltpu.VMEM((CHUNK * 4, 128), f32),
            pltpu.VMEM((CHUNK, 512), bf16),
            pltpu.VMEM((512, 512), bf16),
            pltpu.VMEM((NB * NB, 512), f32),
            pltpu.VMEM((4, NB * NB, 128), f32),
        ],
        compiler_params=pltpu.CompilerParams(vmem_limit_bytes=VMEM_BYTES),
        name="sparse_near",
    )(
        targets,
        ends,
        sources.reshape(slots // CHUNK, 1, CHUNK),
        ext,
        green,
    )


def split2(value):
    high = value.astype(bf16).astype(f32)
    return high, value - high


def put(ref, start, stride, value):
    for t in range(SIDE // 128):
        ref[t, pl.ds(start, 8, stride=stride), :] = value[:, 128 * t : 128 * t + 128]


def take(ref, start, stride):
    tiles = [ref[t, pl.ds(start, 8, stride=stride), :] for t in range(SIDE // 128)]
    return jnp.concatenate(tiles, 1)


def greet(nx, ny, tx, ty):
    barrier = pltpu.get_barrier_semaphore()
    for d in range(1, nx):
        pl.semaphore_signal(
            barrier, inc=1, device_id=(lax.rem(tx + d, nx), ty), device_id_type=MESH
        )
    for d in range(1, ny):
        pl.semaphore_signal(
            barrier, inc=1, device_id=(tx, lax.rem(ty + d, ny)), device_id_type=MESH
        )


def finish(
    shape,
    grad_ref,
    west_ref,
    east_ref,
    message,
    out_ref,
    sums_ref,
    row_out,
    row_in,
    col_out,
    col_in,
    cols,
    buf_a,
    buf_b,
    row_send,
    row_recv,
    col_send,
    col_recv,
    send_a,
    recv_a,
    send_b,
    recv_b,
):
    nx, ny = shape
    tx = lax.axis_index("tx")
    ty = lax.axis_index("ty")

    pl.semaphore_wait(pltpu.get_barrier_semaphore(), nx + ny - 2)

    def line(side, which):
        out, into, send, recv, axis = which
        at = (tx, ty)[axis] + 2 * side - 1
        device = (at, ty) if axis == 0 else (tx, at)
        return pltpu.make_async_remote_copy(
            src_ref=out.at[side],
            dst_ref=into.at[side],
            send_sem=send.at[side],
            recv_sem=recv.at[side],
            device_id=device,
            device_id_type=MESH,
        )

    rows = (row_out, row_in, row_send, row_recv, 0)
    columns = (col_out, col_in, col_send, col_recv, 1)

    def has(side, index, count):
        return index > 0 if side == 0 else index < count - 1

    def sums_copy(d, buf, send, recv, index, count, axis):
        other = lax.rem(index + d, count)
        return pltpu.make_async_remote_copy(
            src_ref=buf.at[index],
            dst_ref=buf.at[index],
            send_sem=send.at[d],
            recv_sem=recv.at[index],
            device_id=(other, ty) if axis == 0 else (tx, other),
            device_id_type=MESH,
        )

    def sums_wait(d, buf, send, recv, index, count, axis):
        sender = lax.rem(index + d, count)
        pltpu.make_async_remote_copy(
            src_ref=buf.at[sender],
            dst_ref=buf.at[sender],
            send_sem=send.at[d],
            recv_sem=recv.at[sender],
            device_id=(sender, ty) if axis == 0 else (tx, sender),
            device_id_type=MESH,
        ).wait_recv()

    along_x = (buf_a, send_a, recv_a, tx, nx, 0)
    along_y = (buf_b, send_b, recv_b, ty, ny, 1)
    buf_a[tx] = message
    for d in range(1, nx):
        sums_copy(d, *along_x).start()

    row_out[0, :, 0:128] = west_ref[0:8, :]
    row_out[0, :, 128 : 128 + SIDE] = grad_ref[0:8, :]
    row_out[0, :, 128 + SIDE : 256 + SIDE] = east_ref[0:8, :]
    row_out[1, :, 0:128] = west_ref[SIDE + 8 : SIDE + 16, :]
    row_out[1, :, 128 : 128 + SIDE] = grad_ref[SIDE + 8 : SIDE + 16, :]
    row_out[1, :, 128 + SIDE : 256 + SIDE] = east_ref[SIDE + 8 : SIDE + 16, :]
    for side in range(2):
        pl.when(has(side, tx, nx))(lambda side=side: line(side, rows).start())

    def copy(i, carry):
        at = pl.multiple_of(i * 8, 8)
        out_ref[pl.ds(at, 8), :] = grad_ref[pl.ds(at + 8, 8), :]
        cols[0, pl.ds(at, 8), :] = west_ref[pl.ds(at + 8, 8), :]
        cols[1, pl.ds(at, 8), :] = east_ref[pl.ds(at + 8, 8), :]
        return carry

    lax.fori_loop(0, SIDE // 8, copy, 0)
    for d in range(1, nx):
        sums_wait(d, *along_x)
    value = buf_a[0]
    for d in range(1, nx):
        value = value + buf_a[d]
    buf_b[ty] = value
    for d in range(1, ny):
        sums_copy(d, *along_y).start()

    for side, row, first in ((0, 7, SIDE - 8), (1, 0, 0)):

        @pl.when(has(1 - side, tx, nx))
        def _(side=side, row=row, first=first):
            line(side, rows).wait_recv()
            got = row_in[side]
            got = jnp.where(
                lax.broadcasted_iota(jnp.int32, got.shape, 0) == row, got, 0.0
            )
            out_ref[first : first + 8, :] += got[:, 128 : 128 + SIDE]
            cols[0, first : first + 8, :] += got[:, 0:128]
            cols[1, first : first + 8, :] += got[:, 128 + SIDE : 256 + SIDE]

    for q in range(4):
        tile = slice(128 * q, 128 * q + 128)
        col_out[0, :, tile] = cols[0, tile, :].T[0:8]
        col_out[1, :, tile] = cols[1, tile, :].T[120:128]
    for side in range(2):
        pl.when(has(side, ty, ny))(lambda side=side: line(side, columns).start())

    lane = lax.broadcasted_iota(jnp.int32, (128, 128), 1)
    for side, row, first, spot in ((0, 0, SIDE - 128, 127), (1, 7, 0, 0)):

        @pl.when(has(1 - side, ty, ny))
        def _(side=side, row=row, first=first, spot=spot):
            line(side, columns).wait_recv()
            for q in range(4):
                tile = slice(128 * q, 128 * q + 128)
                got = jnp.broadcast_to(col_in[side, row : row + 1, tile], (128, 128)).T
                out_ref[tile, first : first + 128] += jnp.where(lane == spot, got, 0.0)

    for d in range(1, ny):
        sums_wait(d, *along_y)
    value = buf_b[0]
    for d in range(1, ny):
        value = value + buf_b[d]
    value = value * (float(SIDE * SIDE * nx * ny) ** (-0.5))
    sums_ref[...] = value
    for side in range(2):
        pl.when(has(side, tx, nx))(lambda side=side: line(side, rows).wait_send())
        pl.when(has(side, ty, ny))(lambda side=side: line(side, columns).wait_send())
    for d in range(1, nx):
        sums_copy(d, *along_x).wait_send()
    for d in range(1, ny):
        sums_copy(d, *along_y).wait_send()


def cell_kernel(
    shape,
    p3_ref,
    near_ref,
    w1_ref,
    v_ref,
    wout_ref,
    out_ref,
    sums_ref,
    grad_ref,
    west_ref,
    east_ref,
    q32,
    qs,
    gs,
    ps,
    total,
    nh,
    first_buf,
    second_buf,
    *exchange,
):
    width = SIDE
    nx, ny = shape
    greet(nx, ny, lax.axis_index("tx"), lax.axis_index("ty"))

    def near_rows(c, first, count):
        at = pl.ds(pl.multiple_of(first, 8), count)
        return jnp.concatenate([near_ref[c, t, at, :] for t in range(4)], 1)

    def build(i, carry):
        r0 = pl.multiple_of(i * 8, 8)
        for b in range(3):
            x = p3_ref[b, pl.ds(r0, 8), :]
            x1, rest = split2(x)
            x2, x3 = split2(rest)
            for n, piece in enumerate((x1, x1, x2, x2, x3)):
                put(q32, b * 5 + n, 16, piece)
        put(q32, 15, 16, jnp.ones((8, width), f32))
        for t in range(4):
            qs[pl.ds(r0, 8), :, 128 * t : 128 * t + 128] = (
                q32[t].astype(bf16).reshape(8, 16, 128)
            )
        return carry

    lax.fori_loop(0, 3, build, 0)
    total[...] = jnp.zeros_like(total)
    nh[...] = jnp.zeros_like(nh)
    gs[...] = jnp.zeros_like(gs)
    zero_rows = jnp.zeros((PADROWS * SROWS, 128), f32)
    for t in range(4):
        ps[t, 0 : PADROWS * SROWS, :] = zero_rows
        ps[t, (PADROWS + SIDE) * SROWS : (2 * PADROWS + SIDE) * SROWS, :] = zero_rows

    lane = lax.broadcasted_iota(jnp.int32, (8, width), 1)

    def combine(i, carry):
        parts = []
        deep = [near_rows(c, i * 8, 24) for c in range(2)]
        for b in range(3):
            acc = None
            for a in range(3):
                x0 = i * 8 + 9 - a
                for c in range(2):
                    term = deep[c][9 - a : 17 - a] * take(
                        ps, x0 * SROWS + 9 * c + 3 * a + b, SROWS
                    )
                    acc = term if acc is None else acc + term
            parts.append(acc)
        low = jnp.where(lane == width - 1, 0.0, pltpu.roll(parts[0], width - 1, 1))
        high = jnp.where(lane == 0, 0.0, pltpu.roll(parts[2], 1, 1))
        at = pl.ds(pl.multiple_of(i * 8, 8), 8)
        grad_ref[at, :] = parts[1] + low + high
        west_ref[at, :] = parts[0][:, 0:128]
        east_ref[at, :] = parts[2][:, width - 128 : width]
        return carry

    def strip(i, carry):
        r0 = pl.multiple_of(i * 8, 8)
        n = [near_rows(c, r0 + PADROWS, 8) for c in range(2)]
        deep = [p3_ref[b, pl.ds(r0, 24), :] for b in range(3)]
        for a in range(3):
            for b in range(3):
                feat = deep[b][7 + a : 15 + a]
                for c in range(2):
                    put(gs, 10 * c + 3 * a + b, SROWS, n[c] * feat)
        for c in range(2):
            put(gs, 10 * c + 9, SROWS, n[c])

        def make_next():
            build(jnp.minimum(i + 3, SIDE // 8 + 1), 0)

        def finish_last():
            combine(jnp.maximum(i - 1, 0), 0)

        after = [near_rows(c, r0 + PADROWS + 8, 8)[0:4] for c in range(2)]
        step(r0, 0, r0 + 4, [n[c][4:8] for c in range(2)], first_buf, second_buf, make_next)
        step(r0, 4, r0 + 8, after, second_buf, first_buf, finish_last)
        return carry

    def hidden(x0):
        feats = qs[pl.ds(x0 + 7, 6)].reshape(96, width)
        return jnp.dot(w1_ref[...], feats, preferred_element_type=f32)

    def activate(z, r, n, into, partial):
        hr = jnp.tanh(z[HIDDEN * r : HIDDEN * r + HIDDEN])
        u = 1.0 - hr * hr
        u1 = u.astype(bf16)
        into[2 * HIDDEN * r : 2 * HIDDEN * r + HIDDEN, :] = u1
        into[2 * HIDDEN * r + HIDDEN : 2 * HIDDEN * r + 2 * HIDDEN, :] = (
            u - u1.astype(f32)
        ).astype(bf16)
        for c in range(2):
            for t in range(4):
                tile = slice(128 * t, 128 * t + 128)
                term = n[c][r : r + 1, tile] * hr[:, tile]
                partial[c] = term if partial[c] is None else partial[c] + term

    def back(r0, j, pair, held):
        slope = jnp.dot(
            v_ref[...],
            held[4 * HIDDEN * pair : 4 * HIDDEN * pair + 4 * HIDDEN, :],
            preferred_element_type=f32,
        )
        for r in range(2):
            one = (
                slope[2 * SROWS * r : 2 * SROWS * r + SROWS]
                + slope[2 * SROWS * r + SROWS : 2 * SROWS * r + 2 * SROWS]
            )
            at = pl.ds(pl.multiple_of((r0 + PADROWS + j + 2 * pair + r) * SROWS, 8), SROWS)
            for t in range(4):
                ps[t, at, :] = one[:, 128 * t : 128 * t + 128]

    def sums(j, pair, held):
        left, right = [], []
        for r in range(2 * pair, 2 * pair + 2):
            first = SROWS * (j + r)
            g = jnp.concatenate([gs[t, first : first + SROWS, :] for t in range(4)], 1)
            left.append(held[2 * HIDDEN * r : 2 * HIDDEN * r + 2 * HIDDEN, :])
            right.append(jnp.concatenate(split2(g), 0).astype(bf16))
        return lax.dot_general(
            jnp.concatenate(left, 1),
            jnp.concatenate(right, 1),
            (((1,), (1,)), ((), ())),
            preferred_element_type=f32,
        )

    def step(r0, j, x0, n, held, into, extra):
        partial = [None, None]
        z = hidden(x0)
        activate(z, 0, n, into, partial)
        back(r0, j, 0, held)
        activate(z, 1, n, into, partial)
        one = sums(j, 0, held)
        activate(z, 2, n, into, partial)
        back(r0, j, 1, held)
        activate(z, 3, n, into, partial)
        extra()
        two = sums(j, 1, held)
        total[:, 0 : 2 * SROWS] += one + two
        for c in range(2):
            nh[HIDDEN * c : HIDDEN * c + HIDDEN, :] += partial[c]

    partial = [None, None]
    z = hidden(0)
    for r in range(4):
        activate(z, r, [near_rows(c, PADROWS, 8) for c in range(2)], first_buf, partial)
    for c in range(2):
        nh[HIDDEN * c : HIDDEN * c + HIDDEN, :] += partial[c]
    lax.fori_loop(0, SIDE // 8, strip, 0)
    lax.fori_loop(SIDE // 8 - 1, SIDE // 8 + 2, combine, 0)
    turned = total[...].T
    turned = turned + pltpu.roll(turned, HIDDEN, 1)
    pulled = turned[0:SROWS] + turned[SROWS : 2 * SROWS]
    first = wout_ref[0:1, :] * pulled[0:10] + wout_ref[1:2, :] * pulled[10:20]
    second = jnp.sum(nh[...].T, axis=0, keepdims=True)
    message = jnp.concatenate([first, second, jnp.zeros((5, 128), f32)], 0)
    finish(
        shape,
        grad_ref,
        west_ref,
        east_ref,
        message,
        out_ref,
        sums_ref,
        *exchange,
    )


def cell_model(p3, near, first, back, out_weights):
    nx, ny = lax.axis_size("tx"), lax.axis_size("ty")
    dma = pltpu.SemaphoreType.DMA
    rows = SIDE + 16
    return pl.pallas_call(
        functools.partial(cell_kernel, (nx, ny)),
        out_shape=[
            jax.ShapeDtypeStruct((SIDE, SIDE), f32),
            jax.ShapeDtypeStruct((16, 128), f32),
        ],
        in_specs=[pl.BlockSpec(memory_space=pltpu.VMEM)] * 5,
        out_specs=[pl.BlockSpec(memory_space=pltpu.VMEM)] * 2,
        scratch_shapes=[
            pltpu.VMEM((rows, SIDE), f32),
            pltpu.VMEM((rows, 128), f32),
            pltpu.VMEM((rows, 128), f32),
            pltpu.VMEM((4, 128, 128), f32),
            pltpu.VMEM((rows, 16, SIDE), bf16),
            pltpu.VMEM((4, 8 * SROWS, 128), f32),
            pltpu.VMEM((4, (SIDE + 2 * PADROWS) * SROWS, 128), f32),
            pltpu.VMEM((128, 128), f32),
            pltpu.VMEM((128, 128), f32),
            pltpu.VMEM((8 * HIDDEN, SIDE), bf16),
            pltpu.VMEM((8 * HIDDEN, SIDE), bf16),
            pltpu.VMEM((2, 8, SIDE + 256), f32),
            pltpu.VMEM((2, 8, SIDE + 256), f32),
            pltpu.VMEM((2, 8, SIDE), f32),
            pltpu.VMEM((2, 8, SIDE), f32),
            pltpu.VMEM((2, SIDE, 128), f32),
            pltpu.VMEM((nx, 16, 128), f32),
            pltpu.VMEM((ny, 16, 128), f32),
            dma((2,)),
            dma((2,)),
            dma((2,)),
            dma((2,)),
            dma((nx,)),
            dma((nx,)),
            dma((ny,)),
            dma((ny,)),
        ],
        compiler_params=pltpu.CompilerParams(
            vmem_limit_bytes=VMEM_BYTES, collective_id=0, has_side_effects=True
        ),
        name="cell_model",
    )(p3, near, first, back, out_weights)


AROUND = [(dx, dy) for dx in (-1, 0, 1) for dy in (-1, 0, 1) if (dx, dy) != (0, 0)]


def front_kernel(
    shape,
    far_ref,
    pillar_ref,
    ext_ref,
    p3_ref,
    field,
    flat,
    order,
    pieces,
    placed,
    edge_in,
    turned,
    side,
    sends,
    recvs,
):
    nx, ny = shape
    tx = lax.axis_index("tx")
    ty = lax.axis_index("ty")
    barrier = pltpu.get_barrier_semaphore()
    for dx, dy in AROUND:
        pl.semaphore_signal(
            barrier,
            inc=1,
            device_id=(lax.rem(tx + dx + nx, nx), lax.rem(ty + dy + ny, ny)),
            device_id_type=MESH,
        )

    for q in range(4):
        tile = slice(128 * q, 128 * q + 128)
        turned[0, :, tile] = pillar_ref[tile, 0:128].T[0:8]
        turned[1, :, tile] = pillar_ref[tile, SIDE - 128 : SIDE].T[120:128]

    def mark(x, carry):
        r = lax.broadcasted_iota(jnp.int32, (128, 128), 0)
        spot = (r // 16) * 128 + x * 16 + r % 16
        lane = lax.broadcasted_iota(jnp.int32, (128, 128), 1)
        at = pl.ds(pl.multiple_of(x * 128, 128), 128)
        for b in range(8):
            order[at, 128 * b : 128 * b + 128] = jnp.where(
                spot == lane + 128 * b, 1.0, 0.0
            ).astype(bf16)
        return carry

    lax.fori_loop(0, 8, mark, 0)

    def there(dx, dy):
        fits = None
        for delta, index, count in ((dx, tx, nx), (dy, ty, ny)):
            if delta:
                one = index > 0 if delta < 0 else index < count - 1
                fits = one if fits is None else jnp.logical_and(fits, one)
        return fits

    def rim(delta, length, reach):
        if delta < 0:
            return (0, reach), (length, reach)
        if delta > 0:
            return (length - reach, reach), (-reach, reach)
        return (0, length), (0, length)

    def far_copy(n):
        dx, dy = AROUND[n]
        (x, wx), (ox, _) = rim(dx, NB, CONE)
        (y, wy), (oy, _) = rim(dy, NB // 4, CONE // 4)
        return pltpu.make_async_remote_copy(
            src_ref=ext_ref.at[pl.ds(CONE + x, wx), pl.ds(CONE // 4 + y, wy)],
            dst_ref=ext_ref.at[pl.ds(CONE + ox, wx), pl.ds(CONE // 4 + oy, wy)],
            send_sem=sends.at[n],
            recv_sem=recvs.at[n],
            device_id=(tx + dx, ty + dy),
            device_id_type=MESH,
        )

    def edge_copy(n):
        dx, dy = AROUND[n]
        if dy == 0:
            source = pillar_ref.at[pl.ds(0 if dx < 0 else SIDE - 8, 8), :]
        elif dx == 0:
            source = turned.at[0 if dy < 0 else 1]
        else:
            source = pillar_ref.at[
                pl.ds(0 if dx < 0 else SIDE - 8, 8), pl.ds(0 if dy < 0 else SIDE - 128, 128)
            ]
        wide = SIDE if dx == 0 or dy == 0 else 128
        return pltpu.make_async_remote_copy(
            src_ref=source,
            dst_ref=edge_in.at[n, :, pl.ds(0, wide)],
            send_sem=sends.at[8 + n],
            recv_sem=recvs.at[8 + n],
            device_id=(tx + dx, ty + dy),
            device_id_type=MESH,
        )

    pl.semaphore_wait(barrier, len(AROUND))
    for n, (dx, dy) in enumerate(AROUND):
        pl.when(there(dx, dy))(lambda n=n: edge_copy(n).start())

    def spread(i, carry):
        at = pl.ds(pl.multiple_of(i * BLK, BLK), BLK)
        for c in range(2):
            strip = far_ref[c, at, :].astype(f32)
            for t in range(4):
                field[c, t, at, :] = strip[:, 128 * t : 128 * t + 128]
        return carry

    lax.fori_loop(0, SIDE // BLK, spread, 0)

    def collect(i, carry):
        for j in range(4):
            for t in range(0, 4, 2):
                at = pl.ds(pl.multiple_of(i * 128 + 32 * j + 8 * t, 16), 16)
                for x in range(8):
                    first = i * 128 + 8 * (j % 2) + x
                    two = [field[j // 2, t + s, pl.ds(first, 8, stride=BLK), :] for s in (0, 1)]
                    pieces[at, 128 * x : 128 * x + 128] = jnp.concatenate(two, 0).astype(bf16)
        return carry

    lax.fori_loop(0, NB // 8, collect, 0)
    placed[...] = jnp.dot(pieces[...], order[...], preferred_element_type=f32)

    def turn(i, carry):
        for j in range(4):
            for t in range(4):
                at = pl.ds(pl.multiple_of(i * 128 + 32 * j + 8 * t, 8), 8)
                for b in range(8):
                    flat[pl.ds(i * 1024 + (8 * t + b) * 4 + j, 8, stride=128), :] = placed[
                        at, 128 * b : 128 * b + 128
                    ]
        return carry

    lax.fori_loop(0, NB // 8, turn, 0)

    def pack(r, carry):
        value = flat[pl.ds(pl.multiple_of(r * 128, 128), 128), :].astype(bf16)
        ext_ref[CONE + r, CONE // 4 : CONE // 4 + NB // 4] = value.reshape(NB // 4, 16, 128)
        return carry

    lax.fori_loop(0, NB, pack, 0)
    for n, (dx, dy) in enumerate(AROUND):
        pl.when(there(dx, dy))(lambda n=n: far_copy(n).start())

    for n, (dx, dy) in enumerate(AROUND):

        @pl.when(jnp.logical_not(there(dx, dy)))
        def _(n=n, dx=dx, dy=dy):
            edge_in[7 - n] = jnp.zeros((8, SIDE), f32)
            x = {-1: 0, 0: CONE, 1: CONE + NB}[dx]
            y = {-1: 0, 0: CONE // 4, 1: (CONE + NB) // 4}[dy]
            wy = CONE // 4 if dy else NB // 4

            def clear(i, carry):
                ext_ref[x + i, y : y + wy] = jnp.zeros((wy, 16, 128), bf16)
                return carry

            lax.fori_loop(0, CONE if dx else NB, clear, 0)

    for n, (dx, dy) in enumerate(AROUND):
        pl.when(there(dx, dy))(lambda n=n: edge_copy(7 - n).wait_recv())
    at_of = {place: n for n, place in enumerate(AROUND)}

    def got(dx, dy):
        return edge_in.at[7 - at_of[(dx, dy)]]

    for s, dy in ((0, -1), (1, 1)):
        lane = 127 if s == 0 else 0
        side[s, 0:8, :] = jnp.broadcast_to(got(-1, dy)[:, lane : lane + 1], (8, 128))
        side[s, SIDE + 8 : SIDE + 16, :] = jnp.broadcast_to(
            got(1, dy)[:, lane : lane + 1], (8, 128)
        )
        row = 7 if s == 0 else 0
        for q in range(4):
            tile = slice(128 * q, 128 * q + 128)
            side[s, 8 + 128 * q : 136 + 128 * q, :] = jnp.broadcast_to(
                got(0, dy)[row : row + 1, tile], (128, 128)
            ).T

    lanes = lax.broadcasted_iota(jnp.int32, (8, SIDE), 1)

    def shifted(at, value):
        p3_ref[1, at, :] = value
        west = jnp.concatenate([side[0, at, :]] * 4, 1)
        east = jnp.concatenate([side[1, at, :]] * 4, 1)
        p3_ref[0, at, :] = jnp.where(lanes == 0, west, pltpu.roll(value, 1, 1))
        p3_ref[2, at, :] = jnp.where(lanes == SIDE - 1, east, pltpu.roll(value, SIDE - 1, 1))

    def interior(i, carry):
        r0 = pl.multiple_of(i * 8, 8)
        shifted(pl.ds(r0 + 8, 8), pillar_ref[pl.ds(r0, 8), :])
        return carry

    lax.fori_loop(0, SIDE // 8, interior, 0)
    shifted(pl.ds(0, 8), got(-1, 0)[...])
    shifted(pl.ds(SIDE + 8, 8), got(1, 0)[...])

    for n, (dx, dy) in enumerate(AROUND):
        pl.when(there(dx, dy))(lambda n=n: far_copy(7 - n).wait_recv())
    for n, (dx, dy) in enumerate(AROUND):

        @pl.when(there(dx, dy))
        def _(n=n):
            far_copy(n).wait_send()
            edge_copy(n).wait_send()


def front(far, pillar):
    nx, ny = lax.axis_size("tx"), lax.axis_size("ty")
    return pl.pallas_call(
        functools.partial(front_kernel, (nx, ny)),
        out_shape=[
            jax.ShapeDtypeStruct((EXT, EXT // 4, 16, 128), bf16),
            jax.ShapeDtypeStruct((3, SIDE + 16, SIDE), f32),
        ],
        in_specs=[pl.BlockSpec(memory_space=pltpu.VMEM)] * 2,
        out_specs=[pl.BlockSpec(memory_space=pltpu.VMEM)] * 2,
        scratch_shapes=[
            pltpu.VMEM((2, 4, SIDE, 128), f32),
            pltpu.VMEM((NB * NB * 4, 128), f32),
            pltpu.VMEM((1024, 1024), bf16),
            pltpu.VMEM((512, 1024), bf16),
            pltpu.VMEM((512, 1024), f32),
            pltpu.VMEM((8, 8, SIDE), f32),
            pltpu.VMEM((2, 8, SIDE), f32),
            pltpu.VMEM((2, SIDE + 16, 128), f32),
            pltpu.SemaphoreType.DMA((16,)),
            pltpu.SemaphoreType.DMA((16,)),
        ],
        compiler_params=pltpu.CompilerParams(
            vmem_limit_bytes=VMEM_BYTES, collective_id=1, has_side_effects=True
        ),
        name="front",
    )(far, pillar)


def rounded(value):
    return lax.reduce_precision(value, 8, 7)


def first_weights(w_in, b_in):
    w = w_in.reshape(HIDDEN, 3, 3)
    w1 = rounded(w)
    w2 = rounded(w - w1)
    b1 = rounded(b_in)
    b2 = rounded(b_in - b1)
    b3 = b_in - b1 - b2
    cells = jnp.stack([w1, w2, w1, w2, w1], 3).reshape(HIDDEN, 3, 15)
    bias = jnp.stack([b1, b2, b3], 1)[:, :, None]
    one = jnp.concatenate([cells, bias], 2).reshape(HIDDEN, 48)
    return jnp.concatenate(
        [jnp.pad(one, ((0, 0), (16 * r, 48 - 16 * r))) for r in range(4)], 0
    ).astype(bf16)


def back_weights(w_in, w_out):
    v = (w_in.T[None] * w_out[:, None, :]).reshape(18, HIDDEN)
    v1 = rounded(v)
    v2 = v - v1
    wide = jnp.concatenate(
        [
            jnp.pad(jnp.concatenate([v1, v1], 1), ((0, 6), (0, 0))),
            jnp.pad(v2, ((0, 6), (0, HIDDEN))),
        ],
        0,
    )
    upper = jnp.pad(wide, ((0, 0), (0, 2 * HIDDEN)))
    lower = jnp.pad(wide, ((0, 0), (2 * HIDDEN, 0)))
    return jnp.concatenate([upper, lower], 0).astype(bf16)


def local(far_adjoint, pillar, green_blocks, pair_src, pair_dst, group_end, w_in, b_in, w_out):
    ext, p3 = front(far_adjoint, pillar)
    near = sparse_near(
        pair_dst.reshape(-1),
        group_end.reshape(-1),
        pair_src.reshape(-1),
        ext.reshape(EXT * EXT * 4, 128),
        green_blocks,
    )
    grad, sums = cell_model(
        p3,
        near,
        first_weights(w_in, b_in),
        back_weights(w_in, w_out),
        jnp.pad(w_out, ((0, 6), (0, HIDDEN))),
    )
    grad, grad_in, grad_bias, grad_out = hand_out(grad, sums)
    return grad, grad_in.T, grad_bias.reshape(HIDDEN), grad_out


def hand_out_kernel(grad_ref, sums_ref, out_ref, first_ref, bias_ref, second_ref):
    out_ref[...] = grad_ref[...]
    value = sums_ref[...]
    first_ref[...] = value[0:9, 0:HIDDEN]
    bias_ref[...] = value[9:10, 0:HIDDEN]
    second_ref[0:1, :] = value[10:11, 0:HIDDEN]
    second_ref[1:2, :] = pltpu.roll(value, HIDDEN, 1)[10:11, 0:HIDDEN]


def hand_out(grad, sums):
    return pl.pallas_call(
        hand_out_kernel,
        out_shape=[
            jax.ShapeDtypeStruct((SIDE, SIDE), f32),
            jax.ShapeDtypeStruct((9, HIDDEN), f32),
            jax.ShapeDtypeStruct((1, HIDDEN), f32),
            jax.ShapeDtypeStruct((2, HIDDEN), f32),
        ],
        in_specs=[pl.BlockSpec(memory_space=pltpu.VMEM)] * 2,
        out_specs=[pl.BlockSpec(memory_space=pltpu.VMEM)] * 4,
        compiler_params=pltpu.CompilerParams(vmem_limit_bytes=VMEM_BYTES),
        name="hand_out",
    )(grad, sums)


def solution(mesh):
    return jax.shard_map(
        local,
        mesh=mesh,
        in_specs=(
            P(None, "tx", "ty"),
            P("tx", "ty"),
            P(),
            P("tx", "ty", None),
            P("tx", "ty", None),
            P("tx", "ty", None),
            P(),
            P(),
            P(),
        ),
        out_specs=(P("tx", "ty"), P(), P(), P()),
        check_vma=False,
    )
```

```python
import functools

import jax
import jax.numpy as jnp
from jax import lax
from jax.experimental import pallas as pl
from jax.experimental.pallas import tpu as pltpu
from jax.sharding import PartitionSpec as P

BLK = 16
CONE = 12
SIDE = 512
NB = SIDE // BLK
EXT = NB + 2 * CONE
GROUPS = 8
CHUNK = 512
HIDDEN = 64
PADROWS = 16
SROWS = 24
VMEM_BYTES = 60 * 1024 * 1024

f32 = jnp.float32
bf16 = jnp.bfloat16
MESH = pl.DeviceIdType.MESH


def swap_pieces(vectors):
    lane = lax.broadcasted_iota(jnp.int32, (8, 128), 1) // 16
    for d in (1, 2, 4):
        mixed = []
        for x in range(8):
            if x & d:
                moved = pltpu.roll(vectors[x ^ d], 128 - 16 * d, 1)
                mixed.append(jnp.where((lane & d) == 0, moved, vectors[x]))
            else:
                moved = pltpu.roll(vectors[x ^ d], 16 * d, 1)
                mixed.append(jnp.where((lane & d) == 0, vectors[x], moved))
        vectors = mixed
    return vectors


def sparse_kernel(
    dst_ref, ends_ref, src_ref, ext_ref, green_ref, near_ref, table, rows, even, odd, stack, seg, acc
):
    chunks = dst_ref.shape[0] // CHUNK

    def widen(i, carry):
        at = pl.ds(pl.multiple_of(i * 128, 128), 128)
        table[at, :] = ext_ref[at, :].astype(f32)
        return carry

    lax.fori_loop(0, EXT * EXT * 4 // 128, widen, 0)
    acc[...] = jnp.zeros_like(acc)
    seg[...] = jnp.zeros_like(seg)

    def gather(base, first, count):
        for q in range(first, first + count):
            d = dst_ref[base + q] * 4
            rows[4 * q : 4 * q + 4, :] = table[pl.ds(pl.multiple_of(d, 4), 4), :]

    def narrow(into):
        for j in range(4):
            into[:, 128 * j : 128 * j + 128] = rows[
                pl.ds(j, CHUNK, stride=4), :
            ].astype(bf16)

    gather(0, 0, CHUNK)
    narrow(even)

    def group(k, parity):
        start = jnp.where(k == 0, 0, ends_ref[jnp.maximum(k - 1, 0)])
        stop = ends_ref[k]

        def visit(c, held, into):
            slot = c * CHUNK + lax.broadcasted_iota(jnp.int32, (1, CHUNK), 1)
            live = (slot >= start) & (slot < stop)
            source = jnp.where(live, src_ref[c], -1)
            ids = lax.broadcasted_iota(jnp.int32, (NB * NB, CHUNK), 0)
            hot = jnp.where(ids == source, 1.0, 0.0).astype(bf16)
            gather(jnp.minimum(c + 1, chunks - 1) * CHUNK, 0, CHUNK)
            seg[...] += jnp.dot(hot, held[...], preferred_element_type=f32)
            narrow(into)

        def chunk(c, parity):
            pl.when(parity == 0)(lambda: visit(c, even, odd))
            pl.when(parity == 1)(lambda: visit(c, odd, even))
            return jnp.where((c + 1) * CHUNK <= stop, 1 - parity, parity)

        parity = lax.fori_loop(start // CHUNK, (stop + CHUNK - 1) // CHUNK, chunk, parity)

        half = BLK * BLK
        real = green_ref[k, 0]
        imag = green_ref[k, 1]
        stack[0:half, 0:half] = real
        stack[0:half, half : 2 * half] = -imag
        stack[half : 2 * half, 0:half] = imag
        stack[half : 2 * half, half : 2 * half] = real

        def apply(m, inner):
            at = pl.ds(pl.multiple_of(m * 512, 512), 512)
            value = seg[at, :]
            seg[at, :] = jnp.zeros((512, 512), f32)
            high = value.astype(bf16)
            low = (value - high.astype(f32)).astype(bf16)
            near = jnp.dot(high, stack[...], preferred_element_type=f32) + jnp.dot(
                low, stack[...], preferred_element_type=f32
            )
            for j in range(4):
                acc[j, at, :] += near[:, 128 * j : 128 * j + 128]
            return inner

        lax.fori_loop(0, 2, apply, 0)
        return parity

    lax.fori_loop(0, GROUPS, group, 0)

    def lay(i, carry):
        for j in range(4):
            for t in range(SIDE // 128):
                vectors = [
                    acc[j, pl.ds(i * 256 + 8 * t + b, 8, stride=NB), :] for b in range(8)
                ]
                for x, v in enumerate(swap_pieces(vectors)):
                    at = pl.ds(PADROWS + i * 128 + 8 * (j % 2) + x, 8, stride=BLK)
                    near_ref[j // 2, t, at, :] = v
        return carry

    lax.fori_loop(0, NB // 8, lay, 0)
    for c in range(2):
        for t in range(4):
            near_ref[c, t, 0:PADROWS, :] = jnp.zeros((PADROWS, 128), f32)
            near_ref[c, t, PADROWS + SIDE : 2 * PADROWS + SIDE, :] = jnp.zeros(
                (PADROWS, 128), f32
            )


def sparse_near(targets, ends, sources, ext, green):
    slots = targets.shape[0]
    return pl.pallas_call(
        sparse_kernel,
        out_shape=jax.ShapeDtypeStruct((2, 4, SIDE + 2 * PADROWS, 128), f32),
        in_specs=[
            pl.BlockSpec(memory_space=pltpu.SMEM),
            pl.BlockSpec(memory_space=pltpu.SMEM),
            pl.BlockSpec(memory_space=pltpu.VMEM),
            pl.BlockSpec(memory_space=pltpu.VMEM),
            pl.BlockSpec(memory_space=pltpu.VMEM),
        ],
        out_specs=pl.BlockSpec(memory_space=pltpu.VMEM),
        scratch_shapes=[
            pltpu.VMEM((EXT * EXT * 4, 128), f32),
            pltpu.VMEM((CHUNK * 4, 128), f32),
            pltpu.VMEM((CHUNK, 512), bf16),
            pltpu.VMEM((CHUNK, 512), bf16),
            pltpu.VMEM((512, 512), bf16),
            pltpu.VMEM((NB * NB, 512), f32),
            pltpu.VMEM((4, NB * NB, 128), f32),
        ],
        compiler_params=pltpu.CompilerParams(vmem_limit_bytes=VMEM_BYTES),
        name="sparse_near",
    )(
        targets,
        ends,
        sources.reshape(slots // CHUNK, 1, CHUNK),
        ext,
        green,
    )


def split2(value):
    high = value.astype(bf16).astype(f32)
    return high, value - high


def put(ref, start, stride, value):
    for t in range(SIDE // 128):
        ref[t, pl.ds(start, 8, stride=stride), :] = value[:, 128 * t : 128 * t + 128]


def take(ref, start, stride):
    tiles = [ref[t, pl.ds(start, 8, stride=stride), :] for t in range(SIDE // 128)]
    return jnp.concatenate(tiles, 1)


def greet(nx, ny, tx, ty):
    barrier = pltpu.get_barrier_semaphore()
    for d in range(1, nx):
        pl.semaphore_signal(
            barrier, inc=1, device_id=(lax.rem(tx + d, nx), ty), device_id_type=MESH
        )
    for d in range(1, ny):
        pl.semaphore_signal(
            barrier, inc=1, device_id=(tx, lax.rem(ty + d, ny)), device_id_type=MESH
        )


def finish(
    shape,
    grad_ref,
    west_ref,
    east_ref,
    message,
    out_ref,
    sums_ref,
    row_out,
    row_in,
    col_out,
    col_in,
    cols,
    buf_a,
    buf_b,
    row_send,
    row_recv,
    col_send,
    col_recv,
    send_a,
    recv_a,
    send_b,
    recv_b,
):
    nx, ny = shape
    tx = lax.axis_index("tx")
    ty = lax.axis_index("ty")

    pl.semaphore_wait(pltpu.get_barrier_semaphore(), nx + ny - 2)

    def line(side, which):
        out, into, send, recv, axis = which
        at = (tx, ty)[axis] + 2 * side - 1
        device = (at, ty) if axis == 0 else (tx, at)
        return pltpu.make_async_remote_copy(
            src_ref=out.at[side],
            dst_ref=into.at[side],
            send_sem=send.at[side],
            recv_sem=recv.at[side],
            device_id=device,
            device_id_type=MESH,
        )

    rows = (row_out, row_in, row_send, row_recv, 0)
    columns = (col_out, col_in, col_send, col_recv, 1)

    def has(side, index, count):
        return index > 0 if side == 0 else index < count - 1

    def sums_copy(d, buf, send, recv, index, count, axis):
        other = lax.rem(index + d, count)
        return pltpu.make_async_remote_copy(
            src_ref=buf.at[index],
            dst_ref=buf.at[index],
            send_sem=send.at[d],
            recv_sem=recv.at[index],
            device_id=(other, ty) if axis == 0 else (tx, other),
            device_id_type=MESH,
        )

    def sums_wait(d, buf, send, recv, index, count, axis):
        sender = lax.rem(index + d, count)
        pltpu.make_async_remote_copy(
            src_ref=buf.at[sender],
            dst_ref=buf.at[sender],
            send_sem=send.at[d],
            recv_sem=recv.at[sender],
            device_id=(sender, ty) if axis == 0 else (tx, sender),
            device_id_type=MESH,
        ).wait_recv()

    along_x = (buf_a, send_a, recv_a, tx, nx, 0)
    along_y = (buf_b, send_b, recv_b, ty, ny, 1)
    buf_a[tx] = message
    for d in range(1, nx):
        sums_copy(d, *along_x).start()

    row_out[0, :, 0:128] = west_ref[0:8, :]
    row_out[0, :, 128 : 128 + SIDE] = grad_ref[0:8, :]
    row_out[0, :, 128 + SIDE : 256 + SIDE] = east_ref[0:8, :]
    row_out[1, :, 0:128] = west_ref[SIDE + 8 : SIDE + 16, :]
    row_out[1, :, 128 : 128 + SIDE] = grad_ref[SIDE + 8 : SIDE + 16, :]
    row_out[1, :, 128 + SIDE : 256 + SIDE] = east_ref[SIDE + 8 : SIDE + 16, :]
    for side in range(2):
        pl.when(has(side, tx, nx))(lambda side=side: line(side, rows).start())

    def copy(i, carry):
        at = pl.multiple_of(i * 8, 8)
        out_ref[pl.ds(at, 8), :] = grad_ref[pl.ds(at + 8, 8), :]
        cols[0, pl.ds(at, 8), :] = west_ref[pl.ds(at + 8, 8), :]
        cols[1, pl.ds(at, 8), :] = east_ref[pl.ds(at + 8, 8), :]
        return carry

    lax.fori_loop(0, SIDE // 8, copy, 0)
    for d in range(1, nx):
        sums_wait(d, *along_x)
    value = buf_a[0]
    for d in range(1, nx):
        value = value + buf_a[d]
    buf_b[ty] = value
    for d in range(1, ny):
        sums_copy(d, *along_y).start()

    for side, row, first in ((0, 7, SIDE - 8), (1, 0, 0)):

        @pl.when(has(1 - side, tx, nx))
        def _(side=side, row=row, first=first):
            line(side, rows).wait_recv()
            got = row_in[side]
            got = jnp.where(
                lax.broadcasted_iota(jnp.int32, got.shape, 0) == row, got, 0.0
            )
            out_ref[first : first + 8, :] += got[:, 128 : 128 + SIDE]
            cols[0, first : first + 8, :] += got[:, 0:128]
            cols[1, first : first + 8, :] += got[:, 128 + SIDE : 256 + SIDE]

    for q in range(4):
        tile = slice(128 * q, 128 * q + 128)
        col_out[0, :, tile] = cols[0, tile, :].T[0:8]
        col_out[1, :, tile] = cols[1, tile, :].T[120:128]
    for side in range(2):
        pl.when(has(side, ty, ny))(lambda side=side: line(side, columns).start())

    lane = lax.broadcasted_iota(jnp.int32, (128, 128), 1)
    for side, row, first, spot in ((0, 0, SIDE - 128, 127), (1, 7, 0, 0)):

        @pl.when(has(1 - side, ty, ny))
        def _(side=side, row=row, first=first, spot=spot):
            line(side, columns).wait_recv()
            for q in range(4):
                tile = slice(128 * q, 128 * q + 128)
                got = jnp.broadcast_to(col_in[side, row : row + 1, tile], (128, 128)).T
                out_ref[tile, first : first + 128] += jnp.where(lane == spot, got, 0.0)

    for d in range(1, ny):
        sums_wait(d, *along_y)
    value = buf_b[0]
    for d in range(1, ny):
        value = value + buf_b[d]
    value = value * (float(SIDE * SIDE * nx * ny) ** (-0.5))
    sums_ref[...] = value
    for side in range(2):
        pl.when(has(side, tx, nx))(lambda side=side: line(side, rows).wait_send())
        pl.when(has(side, ty, ny))(lambda side=side: line(side, columns).wait_send())
    for d in range(1, nx):
        sums_copy(d, *along_x).wait_send()
    for d in range(1, ny):
        sums_copy(d, *along_y).wait_send()


def cell_kernel(
    shape,
    p3_ref,
    near_ref,
    w1_ref,
    v_ref,
    wout_ref,
    out_ref,
    sums_ref,
    grad_ref,
    west_ref,
    east_ref,
    q32,
    qs,
    gs,
    ps,
    total,
    nh,
    first_buf,
    second_buf,
    *exchange,
):
    width = SIDE
    nx, ny = shape
    greet(nx, ny, lax.axis_index("tx"), lax.axis_index("ty"))

    def near_rows(c, first, count):
        at = pl.ds(pl.multiple_of(first, 8), count)
        return jnp.concatenate([near_ref[c, t, at, :] for t in range(4)], 1)

    def build(i, carry):
        r0 = pl.multiple_of(i * 8, 8)
        for b in range(3):
            x = p3_ref[b, pl.ds(r0, 8), :]
            x1, rest = split2(x)
            x2, x3 = split2(rest)
            for n, piece in enumerate((x1, x1, x2, x2, x3)):
                put(q32, b * 5 + n, 16, piece)
        put(q32, 15, 16, jnp.ones((8, width), f32))
        for t in range(4):
            qs[pl.ds(r0, 8), :, 128 * t : 128 * t + 128] = (
                q32[t].astype(bf16).reshape(8, 16, 128)
            )
        return carry

    lax.fori_loop(0, 3, build, 0)
    total[...] = jnp.zeros_like(total)
    nh[...] = jnp.zeros_like(nh)
    gs[...] = jnp.zeros_like(gs)
    zero_rows = jnp.zeros((PADROWS * SROWS, 128), f32)
    for t in range(4):
        ps[t, 0 : PADROWS * SROWS, :] = zero_rows
        ps[t, (PADROWS + SIDE) * SROWS : (2 * PADROWS + SIDE) * SROWS, :] = zero_rows

    lane = lax.broadcasted_iota(jnp.int32, (8, width), 1)

    def combine(i, carry):
        parts = []
        deep = [near_rows(c, i * 8, 24) for c in range(2)]
        for b in range(3):
            acc = None
            for a in range(3):
                x0 = i * 8 + 9 - a
                for c in range(2):
                    term = deep[c][9 - a : 17 - a] * take(
                        ps, x0 * SROWS + 9 * c + 3 * a + b, SROWS
                    )
                    acc = term if acc is None else acc + term
            parts.append(acc)
        low = jnp.where(lane == width - 1, 0.0, pltpu.roll(parts[0], width - 1, 1))
        high = jnp.where(lane == 0, 0.0, pltpu.roll(parts[2], 1, 1))
        at = pl.ds(pl.multiple_of(i * 8, 8), 8)
        grad_ref[at, :] = parts[1] + low + high
        west_ref[at, :] = parts[0][:, 0:128]
        east_ref[at, :] = parts[2][:, width - 128 : width]
        return carry

    def strip(i, carry):
        r0 = pl.multiple_of(i * 8, 8)
        n = [near_rows(c, r0 + PADROWS, 8) for c in range(2)]
        deep = [p3_ref[b, pl.ds(r0, 24), :] for b in range(3)]
        for a in range(3):
            for b in range(3):
                feat = deep[b][7 + a : 15 + a]
                for c in range(2):
                    put(gs, 10 * c + 3 * a + b, SROWS, n[c] * feat)
        for c in range(2):
            put(gs, 10 * c + 9, SROWS, n[c])

        def make_next():
            build(jnp.minimum(i + 3, SIDE // 8 + 1), 0)

        def finish_last():
            combine(jnp.maximum(i - 1, 0), 0)

        after = [near_rows(c, r0 + PADROWS + 8, 8)[0:4] for c in range(2)]
        step(r0, 0, r0 + 4, [n[c][4:8] for c in range(2)], first_buf, second_buf, make_next)
        step(r0, 4, r0 + 8, after, second_buf, first_buf, finish_last)
        return carry

    def hidden(x0):
        feats = qs[pl.ds(x0 + 7, 6)].reshape(96, width)
        return jnp.dot(w1_ref[...], feats, preferred_element_type=f32)

    def activate(z, r, n, into, partial):
        hr = jnp.tanh(z[HIDDEN * r : HIDDEN * r + HIDDEN])
        u = 1.0 - hr * hr
        u1 = u.astype(bf16)
        into[2 * HIDDEN * r : 2 * HIDDEN * r + HIDDEN, :] = u1
        into[2 * HIDDEN * r + HIDDEN : 2 * HIDDEN * r + 2 * HIDDEN, :] = (
            u - u1.astype(f32)
        ).astype(bf16)
        for c in range(2):
            for t in range(4):
                tile = slice(128 * t, 128 * t + 128)
                term = n[c][r : r + 1, tile] * hr[:, tile]
                partial[c] = term if partial[c] is None else partial[c] + term

    def back(r0, j, pair, held):
        slope = jnp.dot(
            v_ref[...],
            held[4 * HIDDEN * pair : 4 * HIDDEN * pair + 4 * HIDDEN, :],
            preferred_element_type=f32,
        )
        for r in range(2):
            one = (
                slope[2 * SROWS * r : 2 * SROWS * r + SROWS]
                + slope[2 * SROWS * r + SROWS : 2 * SROWS * r + 2 * SROWS]
            )
            at = pl.ds(pl.multiple_of((r0 + PADROWS + j + 2 * pair + r) * SROWS, 8), SROWS)
            for t in range(4):
                ps[t, at, :] = one[:, 128 * t : 128 * t + 128]

    def sums(j, pair, held):
        left, right = [], []
        for r in range(2 * pair, 2 * pair + 2):
            first = SROWS * (j + r)
            g = jnp.concatenate([gs[t, first : first + SROWS, :] for t in range(4)], 1)
            left.append(held[2 * HIDDEN * r : 2 * HIDDEN * r + 2 * HIDDEN, :])
            right.append(jnp.concatenate(split2(g), 0).astype(bf16))
        return lax.dot_general(
            jnp.concatenate(left, 1),
            jnp.concatenate(right, 1),
            (((1,), (1,)), ((), ())),
            preferred_element_type=f32,
        )

    def step(r0, j, x0, n, held, into, extra):
        partial = [None, None]
        z = hidden(x0)
        activate(z, 0, n, into, partial)
        back(r0, j, 0, held)
        activate(z, 1, n, into, partial)
        one = sums(j, 0, held)
        activate(z, 2, n, into, partial)
        back(r0, j, 1, held)
        activate(z, 3, n, into, partial)
        extra()
        two = sums(j, 1, held)
        total[:, 0 : 2 * SROWS] += one + two
        for c in range(2):
            nh[HIDDEN * c : HIDDEN * c + HIDDEN, :] += partial[c]

    partial = [None, None]
    z = hidden(0)
    for r in range(4):
        activate(z, r, [near_rows(c, PADROWS, 8) for c in range(2)], first_buf, partial)
    for c in range(2):
        nh[HIDDEN * c : HIDDEN * c + HIDDEN, :] += partial[c]
    lax.fori_loop(0, SIDE // 8, strip, 0)
    lax.fori_loop(SIDE // 8 - 1, SIDE // 8 + 2, combine, 0)
    turned = total[...].T
    turned = turned + pltpu.roll(turned, HIDDEN, 1)
    pulled = turned[0:SROWS] + turned[SROWS : 2 * SROWS]
    first = (
        wout_ref[0:1, :] * pulled[0:10, 0:HIDDEN] + wout_ref[1:2, :] * pulled[10:20, 0:HIDDEN]
    )
    first = jnp.concatenate([first, jnp.zeros((10, 128 - HIDDEN), f32)], 1)
    second = jnp.sum(nh[...].T, axis=0, keepdims=True)
    message = jnp.concatenate([first, second, jnp.zeros((5, 128), f32)], 0)
    finish(
        shape,
        grad_ref,
        west_ref,
        east_ref,
        message,
        out_ref,
        sums_ref,
        *exchange,
    )


def cell_model(p3, near, first, back, out_weights):
    nx, ny = lax.axis_size("tx"), lax.axis_size("ty")
    dma = pltpu.SemaphoreType.DMA
    rows = SIDE + 16
    return pl.pallas_call(
        functools.partial(cell_kernel, (nx, ny)),
        out_shape=[
            jax.ShapeDtypeStruct((SIDE, SIDE), f32),
            jax.ShapeDtypeStruct((16, 128), f32),
        ],
        in_specs=[pl.BlockSpec(memory_space=pltpu.VMEM)] * 5,
        out_specs=[pl.BlockSpec(memory_space=pltpu.VMEM)] * 2,
        scratch_shapes=[
            pltpu.VMEM((rows, SIDE), f32),
            pltpu.VMEM((rows, 128), f32),
            pltpu.VMEM((rows, 128), f32),
            pltpu.VMEM((4, 128, 128), f32),
            pltpu.VMEM((rows, 16, SIDE), bf16),
            pltpu.VMEM((4, 8 * SROWS, 128), f32),
            pltpu.VMEM((4, (SIDE + 2 * PADROWS) * SROWS, 128), f32),
            pltpu.VMEM((128, 128), f32),
            pltpu.VMEM((128, 128), f32),
            pltpu.VMEM((8 * HIDDEN, SIDE), bf16),
            pltpu.VMEM((8 * HIDDEN, SIDE), bf16),
            pltpu.VMEM((2, 8, SIDE + 256), f32),
            pltpu.VMEM((2, 8, SIDE + 256), f32),
            pltpu.VMEM((2, 8, SIDE), f32),
            pltpu.VMEM((2, 8, SIDE), f32),
            pltpu.VMEM((2, SIDE, 128), f32),
            pltpu.VMEM((nx, 16, 128), f32),
            pltpu.VMEM((ny, 16, 128), f32),
            dma((2,)),
            dma((2,)),
            dma((2,)),
            dma((2,)),
            dma((nx,)),
            dma((nx,)),
            dma((ny,)),
            dma((ny,)),
        ],
        compiler_params=pltpu.CompilerParams(
            vmem_limit_bytes=VMEM_BYTES, collective_id=0, has_side_effects=True
        ),
        name="cell_model",
    )(p3, near, first, back, out_weights)


AROUND = [(dx, dy) for dx in (-1, 0, 1) for dy in (-1, 0, 1) if (dx, dy) != (0, 0)]


def front_kernel(
    shape,
    far_ref,
    pillar_ref,
    ext_ref,
    p3_ref,
    field,
    flat,
    order,
    pieces,
    placed,
    edge_in,
    turned,
    side,
    sends,
    recvs,
):
    nx, ny = shape
    tx = lax.axis_index("tx")
    ty = lax.axis_index("ty")
    barrier = pltpu.get_barrier_semaphore()
    for dx, dy in AROUND:
        pl.semaphore_signal(
            barrier,
            inc=1,
            device_id=(lax.rem(tx + dx + nx, nx), lax.rem(ty + dy + ny, ny)),
            device_id_type=MESH,
        )

    for q in range(4):
        tile = slice(128 * q, 128 * q + 128)
        turned[0, :, tile] = pillar_ref[tile, 0:128].T[0:8]
        turned[1, :, tile] = pillar_ref[tile, SIDE - 128 : SIDE].T[120:128]

    def mark(x, carry):
        r = lax.broadcasted_iota(jnp.int32, (128, 128), 0)
        spot = (r // 16) * 128 + x * 16 + r % 16
        lane = lax.broadcasted_iota(jnp.int32, (128, 128), 1)
        at = pl.ds(pl.multiple_of(x * 128, 128), 128)
        for b in range(8):
            order[at, 128 * b : 128 * b + 128] = jnp.where(
                spot == lane + 128 * b, 1.0, 0.0
            ).astype(bf16)
        return carry

    lax.fori_loop(0, 8, mark, 0)

    def there(dx, dy):
        fits = None
        for delta, index, count in ((dx, tx, nx), (dy, ty, ny)):
            if delta:
                one = index > 0 if delta < 0 else index < count - 1
                fits = one if fits is None else jnp.logical_and(fits, one)
        return fits

    def rim(delta, length, reach):
        if delta < 0:
            return (0, reach), (length, reach)
        if delta > 0:
            return (length - reach, reach), (-reach, reach)
        return (0, length), (0, length)

    def far_copy(n):
        dx, dy = AROUND[n]
        (x, wx), (ox, _) = rim(dx, NB, CONE)
        (y, wy), (oy, _) = rim(dy, NB // 4, CONE // 4)
        return pltpu.make_async_remote_copy(
            src_ref=ext_ref.at[pl.ds(CONE + x, wx), pl.ds(CONE // 4 + y, wy)],
            dst_ref=ext_ref.at[pl.ds(CONE + ox, wx), pl.ds(CONE // 4 + oy, wy)],
            send_sem=sends.at[n],
            recv_sem=recvs.at[n],
            device_id=(tx + dx, ty + dy),
            device_id_type=MESH,
        )

    def edge_copy(n):
        dx, dy = AROUND[n]
        if dy == 0:
            source = pillar_ref.at[pl.ds(0 if dx < 0 else SIDE - 8, 8), :]
        elif dx == 0:
            source = turned.at[0 if dy < 0 else 1]
        else:
            source = pillar_ref.at[
                pl.ds(0 if dx < 0 else SIDE - 8, 8), pl.ds(0 if dy < 0 else SIDE - 128, 128)
            ]
        wide = SIDE if dx == 0 or dy == 0 else 128
        return pltpu.make_async_remote_copy(
            src_ref=source,
            dst_ref=edge_in.at[n, :, pl.ds(0, wide)],
            send_sem=sends.at[8 + n],
            recv_sem=recvs.at[8 + n],
            device_id=(tx + dx, ty + dy),
            device_id_type=MESH,
        )


    def spread(i, carry):
        at = pl.ds(pl.multiple_of(i * BLK, BLK), BLK)
        for c in range(2):
            strip = far_ref[c, at, :].astype(f32)
            for t in range(4):
                field[c, t, at, :] = strip[:, 128 * t : 128 * t + 128]
        return carry

    lax.fori_loop(0, SIDE // BLK, spread, 0)

    def collect(i, carry):
        for j in range(4):
            for t in range(0, 4, 2):
                at = pl.ds(pl.multiple_of(i * 128 + 32 * j + 8 * t, 16), 16)
                for x in range(8):
                    first = i * 128 + 8 * (j % 2) + x
                    two = [field[j // 2, t + s, pl.ds(first, 8, stride=BLK), :] for s in (0, 1)]
                    pieces[at, 128 * x : 128 * x + 128] = jnp.concatenate(two, 0).astype(bf16)
        return carry

    lax.fori_loop(0, NB // 8, collect, 0)
    placed[...] = jnp.dot(pieces[...], order[...], preferred_element_type=f32)

    def turn(i, carry):
        for j in range(4):
            for t in range(4):
                at = pl.ds(pl.multiple_of(i * 128 + 32 * j + 8 * t, 8), 8)
                for b in range(8):
                    flat[pl.ds(i * 1024 + (8 * t + b) * 4 + j, 8, stride=128), :] = placed[
                        at, 128 * b : 128 * b + 128
                    ]
        return carry

    lax.fori_loop(0, NB // 8, turn, 0)

    def pack(r, carry):
        value = flat[pl.ds(pl.multiple_of(r * 128, 128), 128), :].astype(bf16)
        ext_ref[CONE + r, CONE // 4 : CONE // 4 + NB // 4] = value.reshape(NB // 4, 16, 128)
        return carry

    lax.fori_loop(0, NB, pack, 0)
    pl.semaphore_wait(barrier, len(AROUND))
    for n, (dx, dy) in enumerate(AROUND):
        pl.when(there(dx, dy))(lambda n=n: edge_copy(n).start())
    for n, (dx, dy) in enumerate(AROUND):
        pl.when(there(dx, dy))(lambda n=n: far_copy(n).start())

    for n, (dx, dy) in enumerate(AROUND):

        @pl.when(jnp.logical_not(there(dx, dy)))
        def _(n=n, dx=dx, dy=dy):
            edge_in[7 - n] = jnp.zeros((8, SIDE), f32)
            x = {-1: 0, 0: CONE, 1: CONE + NB}[dx]
            y = {-1: 0, 0: CONE // 4, 1: (CONE + NB) // 4}[dy]
            wy = CONE // 4 if dy else NB // 4

            def clear(i, carry):
                ext_ref[x + i, y : y + wy] = jnp.zeros((wy, 16, 128), bf16)
                return carry

            lax.fori_loop(0, CONE if dx else NB, clear, 0)

    for n, (dx, dy) in enumerate(AROUND):
        pl.when(there(dx, dy))(lambda n=n: edge_copy(7 - n).wait_recv())
    at_of = {place: n for n, place in enumerate(AROUND)}

    def got(dx, dy):
        return edge_in.at[7 - at_of[(dx, dy)]]

    for s, dy in ((0, -1), (1, 1)):
        lane = 127 if s == 0 else 0
        side[s, 0:8, :] = jnp.broadcast_to(got(-1, dy)[:, lane : lane + 1], (8, 128))
        side[s, SIDE + 8 : SIDE + 16, :] = jnp.broadcast_to(
            got(1, dy)[:, lane : lane + 1], (8, 128)
        )
        row = 7 if s == 0 else 0
        for q in range(4):
            tile = slice(128 * q, 128 * q + 128)
            side[s, 8 + 128 * q : 136 + 128 * q, :] = jnp.broadcast_to(
                got(0, dy)[row : row + 1, tile], (128, 128)
            ).T

    lanes = lax.broadcasted_iota(jnp.int32, (8, SIDE), 1)

    def shifted(at, value):
        p3_ref[1, at, :] = value
        west = jnp.concatenate([side[0, at, :]] * 4, 1)
        east = jnp.concatenate([side[1, at, :]] * 4, 1)
        p3_ref[0, at, :] = jnp.where(lanes == 0, west, pltpu.roll(value, 1, 1))
        p3_ref[2, at, :] = jnp.where(lanes == SIDE - 1, east, pltpu.roll(value, SIDE - 1, 1))

    def interior(i, carry):
        r0 = pl.multiple_of(i * 8, 8)
        shifted(pl.ds(r0 + 8, 8), pillar_ref[pl.ds(r0, 8), :])
        return carry

    lax.fori_loop(0, SIDE // 8, interior, 0)
    shifted(pl.ds(0, 8), got(-1, 0)[...])
    shifted(pl.ds(SIDE + 8, 8), got(1, 0)[...])

    for n, (dx, dy) in enumerate(AROUND):
        pl.when(there(dx, dy))(lambda n=n: far_copy(7 - n).wait_recv())
    for n, (dx, dy) in enumerate(AROUND):

        @pl.when(there(dx, dy))
        def _(n=n):
            far_copy(n).wait_send()
            edge_copy(n).wait_send()


def front(far, pillar):
    nx, ny = lax.axis_size("tx"), lax.axis_size("ty")
    return pl.pallas_call(
        functools.partial(front_kernel, (nx, ny)),
        out_shape=[
            jax.ShapeDtypeStruct((EXT, EXT // 4, 16, 128), bf16),
            jax.ShapeDtypeStruct((3, SIDE + 16, SIDE), f32),
        ],
        in_specs=[pl.BlockSpec(memory_space=pltpu.VMEM)] * 2,
        out_specs=[pl.BlockSpec(memory_space=pltpu.VMEM)] * 2,
        scratch_shapes=[
            pltpu.VMEM((2, 4, SIDE, 128), f32),
            pltpu.VMEM((NB * NB * 4, 128), f32),
            pltpu.VMEM((1024, 1024), bf16),
            pltpu.VMEM((512, 1024), bf16),
            pltpu.VMEM((512, 1024), f32),
            pltpu.VMEM((8, 8, SIDE), f32),
            pltpu.VMEM((2, 8, SIDE), f32),
            pltpu.VMEM((2, SIDE + 16, 128), f32),
            pltpu.SemaphoreType.DMA((16,)),
            pltpu.SemaphoreType.DMA((16,)),
        ],
        compiler_params=pltpu.CompilerParams(
            vmem_limit_bytes=VMEM_BYTES, collective_id=1, has_side_effects=True
        ),
        name="front",
    )(far, pillar)


def rounded(value):
    return lax.reduce_precision(value, 8, 7)


def first_weights(w_in, b_in):
    w = w_in.reshape(HIDDEN, 3, 3)
    w1 = rounded(w)
    w2 = rounded(w - w1)
    b1 = rounded(b_in)
    b2 = rounded(b_in - b1)
    b3 = b_in - b1 - b2
    cells = jnp.stack([w1, w2, w1, w2, w1], 3).reshape(HIDDEN, 3, 15)
    bias = jnp.stack([b1, b2, b3], 1)[:, :, None]
    one = jnp.concatenate([cells, bias], 2).reshape(HIDDEN, 48)
    return jnp.concatenate(
        [jnp.pad(one, ((0, 0), (16 * r, 48 - 16 * r))) for r in range(4)], 0
    ).astype(bf16)


def back_weights(w_in, w_out):
    v = (w_in.T[None] * w_out[:, None, :]).reshape(18, HIDDEN)
    v1 = rounded(v)
    v2 = v - v1
    wide = jnp.concatenate(
        [
            jnp.pad(jnp.concatenate([v1, v1], 1), ((0, 6), (0, 0))),
            jnp.pad(v2, ((0, 6), (0, HIDDEN))),
        ],
        0,
    )
    upper = jnp.pad(wide, ((0, 0), (0, 2 * HIDDEN)))
    lower = jnp.pad(wide, ((0, 0), (2 * HIDDEN, 0)))
    return jnp.concatenate([upper, lower], 0).astype(bf16)


def local(far_adjoint, pillar, green_blocks, pair_src, pair_dst, group_end, w_in, b_in, w_out):
    ext, p3 = front(far_adjoint, pillar)
    near = sparse_near(
        pair_dst.reshape(-1),
        group_end.reshape(-1),
        pair_src.reshape(-1),
        ext.reshape(EXT * EXT * 4, 128),
        green_blocks,
    )
    grad, sums = cell_model(
        p3,
        near,
        first_weights(w_in, b_in),
        back_weights(w_in, w_out),
        w_out,
    )
    grad, grad_in, grad_bias, grad_out = hand_out(grad, sums)
    return grad, grad_in.T, grad_bias.reshape(HIDDEN), grad_out


def hand_out_kernel(grad_ref, sums_ref, out_ref, first_ref, bias_ref, second_ref):
    out_ref[...] = grad_ref[...]
    value = sums_ref[...]
    first_ref[...] = value[0:9, 0:HIDDEN]
    bias_ref[...] = value[9:10, 0:HIDDEN]
    second_ref[0:1, :] = value[10:11, 0:HIDDEN]
    second_ref[1:2, :] = pltpu.roll(value, HIDDEN, 1)[10:11, 0:HIDDEN]


def hand_out(grad, sums):
    return pl.pallas_call(
        hand_out_kernel,
        out_shape=[
            jax.ShapeDtypeStruct((SIDE, SIDE), f32),
            jax.ShapeDtypeStruct((9, HIDDEN), f32),
            jax.ShapeDtypeStruct((1, HIDDEN), f32),
            jax.ShapeDtypeStruct((2, HIDDEN), f32),
        ],
        in_specs=[pl.BlockSpec(memory_space=pltpu.VMEM)] * 2,
        out_specs=[pl.BlockSpec(memory_space=pltpu.VMEM)] * 4,
        compiler_params=pltpu.CompilerParams(vmem_limit_bytes=VMEM_BYTES),
        name="hand_out",
    )(grad, sums)


def solution(mesh):
    return jax.shard_map(
        local,
        mesh=mesh,
        in_specs=(
            P(None, "tx", "ty"),
            P("tx", "ty"),
            P(),
            P("tx", "ty", None),
            P("tx", "ty", None),
            P("tx", "ty", None),
            P(),
            P(),
            P(),
        ),
        out_specs=(P("tx", "ty"), P(), P(), P()),
        check_vma=False,
    )
```

```python
import functools

import jax
import jax.numpy as jnp
from jax import lax
from jax.experimental import pallas as pl
from jax.experimental.pallas import tpu as pltpu
from jax.sharding import PartitionSpec as P

BLK = 16
CONE = 12
SIDE = 512
NB = SIDE // BLK
EXT = NB + 2 * CONE
GROUPS = 8
CHUNK = 512
HIDDEN = 64
PADROWS = 16
SROWS = 24
VMEM_BYTES = 60 * 1024 * 1024

f32 = jnp.float32
bf16 = jnp.bfloat16
MESH = pl.DeviceIdType.MESH


def swap_pieces(vectors):
    lane = lax.broadcasted_iota(jnp.int32, (8, 128), 1) // 16
    for d in (1, 2, 4):
        mixed = []
        for x in range(8):
            if x & d:
                moved = pltpu.roll(vectors[x ^ d], 128 - 16 * d, 1)
                mixed.append(jnp.where((lane & d) == 0, moved, vectors[x]))
            else:
                moved = pltpu.roll(vectors[x ^ d], 16 * d, 1)
                mixed.append(jnp.where((lane & d) == 0, vectors[x], moved))
        vectors = mixed
    return vectors


def sparse_kernel(
    dst_ref, ends_ref, src_ref, ext_ref, green_ref, near_ref, table, rows, even, odd, stack, seg, acc
):
    chunks = dst_ref.shape[0] // CHUNK

    def widen(i, carry):
        at = pl.ds(pl.multiple_of(i * 128, 128), 128)
        table[at, :] = ext_ref[at, :].astype(f32)
        return carry

    lax.fori_loop(0, EXT * EXT * 4 // 128, widen, 0)
    acc[...] = jnp.zeros_like(acc)
    seg[...] = jnp.zeros_like(seg)

    def gather(base, first, count):
        for q in range(first, first + count):
            d = dst_ref[base + q] * 4
            rows[4 * q : 4 * q + 4, :] = table[pl.ds(pl.multiple_of(d, 4), 4), :]

    def narrow(into):
        for j in range(4):
            into[:, 128 * j : 128 * j + 128] = rows[
                pl.ds(j, CHUNK, stride=4), :
            ].astype(bf16)

    gather(0, 0, CHUNK)
    narrow(even)

    def group(k, parity):
        start = jnp.where(k == 0, 0, ends_ref[jnp.maximum(k - 1, 0)])
        stop = ends_ref[k]

        def visit(c, held, into):
            slot = c * CHUNK + lax.broadcasted_iota(jnp.int32, (1, CHUNK), 1)
            live = (slot >= start) & (slot < stop)
            source = jnp.where(live, src_ref[c], -1)
            ids = lax.broadcasted_iota(jnp.int32, (NB * NB, CHUNK), 0)
            hot = jnp.where(ids == source, 1.0, 0.0).astype(bf16)
            gather(jnp.minimum(c + 1, chunks - 1) * CHUNK, 0, CHUNK)
            seg[...] += jnp.dot(hot, held[...], preferred_element_type=f32)
            narrow(into)

        def chunk(c, parity):
            pl.when(parity == 0)(lambda: visit(c, even, odd))
            pl.when(parity == 1)(lambda: visit(c, odd, even))
            return jnp.where((c + 1) * CHUNK <= stop, 1 - parity, parity)

        parity = lax.fori_loop(start // CHUNK, (stop + CHUNK - 1) // CHUNK, chunk, parity)

        half = BLK * BLK
        real = green_ref[k, 0]
        imag = green_ref[k, 1]
        stack[0:half, 0:half] = real
        stack[0:half, half : 2 * half] = -imag
        stack[half : 2 * half, 0:half] = imag
        stack[half : 2 * half, half : 2 * half] = real

        value = seg[...]
        seg[...] = jnp.zeros_like(seg)
        high = value.astype(bf16)
        low = (value - high.astype(f32)).astype(bf16)
        near = jnp.dot(high, stack[...], preferred_element_type=f32) + jnp.dot(
            low, stack[...], preferred_element_type=f32
        )
        for j in range(4):
            acc[j] += near[:, 128 * j : 128 * j + 128]
        return parity

    lax.fori_loop(0, GROUPS, group, 0)

    def lay(i, carry):
        for j in range(4):
            for t in range(SIDE // 128):
                vectors = [
                    acc[j, pl.ds(i * 256 + 8 * t + b, 8, stride=NB), :] for b in range(8)
                ]
                for x, v in enumerate(swap_pieces(vectors)):
                    at = pl.ds(PADROWS + i * 128 + 8 * (j % 2) + x, 8, stride=BLK)
                    near_ref[j // 2, t, at, :] = v
        return carry

    lax.fori_loop(0, NB // 8, lay, 0)
    for c in range(2):
        for t in range(4):
            near_ref[c, t, 0:PADROWS, :] = jnp.zeros((PADROWS, 128), f32)
            near_ref[c, t, PADROWS + SIDE : 2 * PADROWS + SIDE, :] = jnp.zeros(
                (PADROWS, 128), f32
            )


def sparse_near(targets, ends, sources, ext, green):
    slots = targets.shape[0]
    return pl.pallas_call(
        sparse_kernel,
        out_shape=jax.ShapeDtypeStruct((2, 4, SIDE + 2 * PADROWS, 128), f32),
        in_specs=[
            pl.BlockSpec(memory_space=pltpu.SMEM),
            pl.BlockSpec(memory_space=pltpu.SMEM),
            pl.BlockSpec(memory_space=pltpu.VMEM),
            pl.BlockSpec(memory_space=pltpu.VMEM),
            pl.BlockSpec(memory_space=pltpu.VMEM),
        ],
        out_specs=pl.BlockSpec(memory_space=pltpu.VMEM),
        scratch_shapes=[
            pltpu.VMEM((EXT * EXT * 4, 128), f32),
            pltpu.VMEM((CHUNK * 4, 128), f32),
            pltpu.VMEM((CHUNK, 512), bf16),
            pltpu.VMEM((CHUNK, 512), bf16),
            pltpu.VMEM((512, 512), bf16),
            pltpu.VMEM((NB * NB, 512), f32),
            pltpu.VMEM((4, NB * NB, 128), f32),
        ],
        compiler_params=pltpu.CompilerParams(vmem_limit_bytes=VMEM_BYTES),
        name="sparse_near",
    )(
        targets,
        ends,
        sources.reshape(slots // CHUNK, 1, CHUNK),
        ext,
        green,
    )


def split2(value):
    high = value.astype(bf16).astype(f32)
    return high, value - high


def put(ref, start, stride, value):
    for t in range(SIDE // 128):
        ref[t, pl.ds(start, 8, stride=stride), :] = value[:, 128 * t : 128 * t + 128]


def take(ref, start, stride):
    tiles = [ref[t, pl.ds(start, 8, stride=stride), :] for t in range(SIDE // 128)]
    return jnp.concatenate(tiles, 1)


def greet(nx, ny, tx, ty):
    barrier = pltpu.get_barrier_semaphore()
    for d in range(1, nx):
        pl.semaphore_signal(
            barrier, inc=1, device_id=(lax.rem(tx + d, nx), ty), device_id_type=MESH
        )
    for d in range(1, ny):
        pl.semaphore_signal(
            barrier, inc=1, device_id=(tx, lax.rem(ty + d, ny)), device_id_type=MESH
        )


def finish(
    shape,
    grad_ref,
    west_ref,
    east_ref,
    message,
    out_ref,
    sums_ref,
    row_out,
    row_in,
    col_out,
    col_in,
    cols,
    buf_a,
    buf_b,
    row_send,
    row_recv,
    col_send,
    col_recv,
    send_a,
    recv_a,
    send_b,
    recv_b,
):
    nx, ny = shape
    tx = lax.axis_index("tx")
    ty = lax.axis_index("ty")

    pl.semaphore_wait(pltpu.get_barrier_semaphore(), nx + ny - 2)

    def line(side, which):
        out, into, send, recv, axis = which
        at = (tx, ty)[axis] + 2 * side - 1
        device = (at, ty) if axis == 0 else (tx, at)
        return pltpu.make_async_remote_copy(
            src_ref=out.at[side],
            dst_ref=into.at[side],
            send_sem=send.at[side],
            recv_sem=recv.at[side],
            device_id=device,
            device_id_type=MESH,
        )

    rows = (row_out, row_in, row_send, row_recv, 0)
    columns = (col_out, col_in, col_send, col_recv, 1)

    def has(side, index, count):
        return index > 0 if side == 0 else index < count - 1

    def sums_copy(d, buf, send, recv, index, count, axis):
        other = lax.rem(index + d, count)
        return pltpu.make_async_remote_copy(
            src_ref=buf.at[index],
            dst_ref=buf.at[index],
            send_sem=send.at[d],
            recv_sem=recv.at[index],
            device_id=(other, ty) if axis == 0 else (tx, other),
            device_id_type=MESH,
        )

    def sums_wait(d, buf, send, recv, index, count, axis):
        sender = lax.rem(index + d, count)
        pltpu.make_async_remote_copy(
            src_ref=buf.at[sender],
            dst_ref=buf.at[sender],
            send_sem=send.at[d],
            recv_sem=recv.at[sender],
            device_id=(sender, ty) if axis == 0 else (tx, sender),
            device_id_type=MESH,
        ).wait_recv()

    along_x = (buf_a, send_a, recv_a, tx, nx, 0)
    along_y = (buf_b, send_b, recv_b, ty, ny, 1)
    buf_a[tx] = message
    for d in range(1, nx):
        sums_copy(d, *along_x).start()

    row_out[0, :, 0:128] = west_ref[0:8, :]
    row_out[0, :, 128 : 128 + SIDE] = grad_ref[0:8, :]
    row_out[0, :, 128 + SIDE : 256 + SIDE] = east_ref[0:8, :]
    row_out[1, :, 0:128] = west_ref[SIDE + 8 : SIDE + 16, :]
    row_out[1, :, 128 : 128 + SIDE] = grad_ref[SIDE + 8 : SIDE + 16, :]
    row_out[1, :, 128 + SIDE : 256 + SIDE] = east_ref[SIDE + 8 : SIDE + 16, :]
    for side in range(2):
        pl.when(has(side, tx, nx))(lambda side=side: line(side, rows).start())

    def copy(i, carry):
        at = pl.multiple_of(i * 8, 8)
        out_ref[pl.ds(at, 8), :] = grad_ref[pl.ds(at + 8, 8), :]
        cols[0, pl.ds(at, 8), :] = west_ref[pl.ds(at + 8, 8), :]
        cols[1, pl.ds(at, 8), :] = east_ref[pl.ds(at + 8, 8), :]
        return carry

    lax.fori_loop(0, SIDE // 8, copy, 0)
    for d in range(1, nx):
        sums_wait(d, *along_x)
    value = buf_a[0]
    for d in range(1, nx):
        value = value + buf_a[d]
    buf_b[ty] = value
    for d in range(1, ny):
        sums_copy(d, *along_y).start()

    for side, row, first in ((0, 7, SIDE - 8), (1, 0, 0)):

        @pl.when(has(1 - side, tx, nx))
        def _(side=side, row=row, first=first):
            line(side, rows).wait_recv()
            got = row_in[side]
            got = jnp.where(
                lax.broadcasted_iota(jnp.int32, got.shape, 0) == row, got, 0.0
            )
            out_ref[first : first + 8, :] += got[:, 128 : 128 + SIDE]
            cols[0, first : first + 8, :] += got[:, 0:128]
            cols[1, first : first + 8, :] += got[:, 128 + SIDE : 256 + SIDE]

    for q in range(4):
        tile = slice(128 * q, 128 * q + 128)
        col_out[0, :, tile] = cols[0, tile, :].T[0:8]
        col_out[1, :, tile] = cols[1, tile, :].T[120:128]
    for side in range(2):
        pl.when(has(side, ty, ny))(lambda side=side: line(side, columns).start())

    lane = lax.broadcasted_iota(jnp.int32, (128, 128), 1)
    for side, row, first, spot in ((0, 0, SIDE - 128, 127), (1, 7, 0, 0)):

        @pl.when(has(1 - side, ty, ny))
        def _(side=side, row=row, first=first, spot=spot):
            line(side, columns).wait_recv()
            for q in range(4):
                tile = slice(128 * q, 128 * q + 128)
                got = jnp.broadcast_to(col_in[side, row : row + 1, tile], (128, 128)).T
                out_ref[tile, first : first + 128] += jnp.where(lane == spot, got, 0.0)

    for d in range(1, ny):
        sums_wait(d, *along_y)
    value = buf_b[0]
    for d in range(1, ny):
        value = value + buf_b[d]
    value = value * (float(SIDE * SIDE * nx * ny) ** (-0.5))
    sums_ref[...] = value
    for side in range(2):
        pl.when(has(side, tx, nx))(lambda side=side: line(side, rows).wait_send())
        pl.when(has(side, ty, ny))(lambda side=side: line(side, columns).wait_send())
    for d in range(1, nx):
        sums_copy(d, *along_x).wait_send()
    for d in range(1, ny):
        sums_copy(d, *along_y).wait_send()


def cell_kernel(
    shape,
    p3_ref,
    near_ref,
    w1_ref,
    v_ref,
    wout_ref,
    out_ref,
    sums_ref,
    grad_ref,
    west_ref,
    east_ref,
    q32,
    qs,
    gs,
    ps,
    total,
    nh,
    first_buf,
    second_buf,
    *exchange,
):
    width = SIDE
    nx, ny = shape
    greet(nx, ny, lax.axis_index("tx"), lax.axis_index("ty"))

    def near_rows(c, first, count):
        at = pl.ds(pl.multiple_of(first, 8), count)
        return jnp.concatenate([near_ref[c, t, at, :] for t in range(4)], 1)

    def build(i, carry):
        r0 = pl.multiple_of(i * 8, 8)
        for b in range(3):
            x = p3_ref[b, pl.ds(r0, 8), :]
            x1, rest = split2(x)
            x2, x3 = split2(rest)
            for n, piece in enumerate((x1, x1, x2, x2, x3)):
                put(q32, b * 5 + n, 16, piece)
        put(q32, 15, 16, jnp.ones((8, width), f32))
        for t in range(4):
            qs[pl.ds(r0, 8), :, 128 * t : 128 * t + 128] = (
                q32[t].astype(bf16).reshape(8, 16, 128)
            )
        return carry

    lax.fori_loop(0, 3, build, 0)
    total[...] = jnp.zeros_like(total)
    nh[...] = jnp.zeros_like(nh)
    gs[...] = jnp.zeros_like(gs)
    zero_rows = jnp.zeros((PADROWS * SROWS, 128), f32)
    for t in range(4):
        ps[t, 0 : PADROWS * SROWS, :] = zero_rows
        ps[t, (PADROWS + SIDE) * SROWS : (2 * PADROWS + SIDE) * SROWS, :] = zero_rows

    lane = lax.broadcasted_iota(jnp.int32, (8, width), 1)

    def combine(i, carry):
        parts = []
        deep = [near_rows(c, i * 8, 24) for c in range(2)]
        for b in range(3):
            acc = None
            for a in range(3):
                x0 = i * 8 + 9 - a
                for c in range(2):
                    term = deep[c][9 - a : 17 - a] * take(
                        ps, x0 * SROWS + 9 * c + 3 * a + b, SROWS
                    )
                    acc = term if acc is None else acc + term
            parts.append(acc)
        low = jnp.where(lane == width - 1, 0.0, pltpu.roll(parts[0], width - 1, 1))
        high = jnp.where(lane == 0, 0.0, pltpu.roll(parts[2], 1, 1))
        at = pl.ds(pl.multiple_of(i * 8, 8), 8)
        grad_ref[at, :] = parts[1] + low + high
        west_ref[at, :] = parts[0][:, 0:128]
        east_ref[at, :] = parts[2][:, width - 128 : width]
        return carry

    def strip(i, carry):
        r0 = pl.multiple_of(i * 8, 8)
        n = [near_rows(c, r0 + PADROWS, 8) for c in range(2)]
        deep = [p3_ref[b, pl.ds(r0, 24), :] for b in range(3)]
        for a in range(3):
            for b in range(3):
                feat = deep[b][7 + a : 15 + a]
                for c in range(2):
                    put(gs, 10 * c + 3 * a + b, SROWS, n[c] * feat)
        for c in range(2):
            put(gs, 10 * c + 9, SROWS, n[c])

        def make_next():
            build(jnp.minimum(i + 3, SIDE // 8 + 1), 0)

        def finish_last():
            combine(jnp.maximum(i - 1, 0), 0)

        after = [near_rows(c, r0 + PADROWS + 8, 8)[0:4] for c in range(2)]
        step(r0, 0, r0 + 4, [n[c][4:8] for c in range(2)], first_buf, second_buf, make_next)
        step(r0, 4, r0 + 8, after, second_buf, first_buf, finish_last)
        return carry

    def hidden(x0):
        feats = qs[pl.ds(x0 + 7, 6)].reshape(96, width)
        return jnp.dot(w1_ref[...], feats, preferred_element_type=f32)

    def activate(z, r, n, into, partial):
        hr = jnp.tanh(z[HIDDEN * r : HIDDEN * r + HIDDEN])
        u = 1.0 - hr * hr
        u1 = u.astype(bf16)
        into[2 * HIDDEN * r : 2 * HIDDEN * r + HIDDEN, :] = u1
        into[2 * HIDDEN * r + HIDDEN : 2 * HIDDEN * r + 2 * HIDDEN, :] = (
            u - u1.astype(f32)
        ).astype(bf16)
        for c in range(2):
            for t in range(4):
                tile = slice(128 * t, 128 * t + 128)
                term = n[c][r : r + 1, tile] * hr[:, tile]
                partial[c] = term if partial[c] is None else partial[c] + term

    def back(r0, j, pair, held):
        slope = jnp.dot(
            v_ref[...],
            held[4 * HIDDEN * pair : 4 * HIDDEN * pair + 4 * HIDDEN, :],
            preferred_element_type=f32,
        )
        for r in range(2):
            one = (
                slope[2 * SROWS * r : 2 * SROWS * r + SROWS]
                + slope[2 * SROWS * r + SROWS : 2 * SROWS * r + 2 * SROWS]
            )
            at = pl.ds(pl.multiple_of((r0 + PADROWS + j + 2 * pair + r) * SROWS, 8), SROWS)
            for t in range(4):
                ps[t, at, :] = one[:, 128 * t : 128 * t + 128]

    def sums(j, pair, held):
        left, right = [], []
        for r in range(2 * pair, 2 * pair + 2):
            first = SROWS * (j + r)
            g = jnp.concatenate([gs[t, first : first + SROWS, :] for t in range(4)], 1)
            left.append(held[2 * HIDDEN * r : 2 * HIDDEN * r + 2 * HIDDEN, :])
            right.append(jnp.concatenate(split2(g), 0).astype(bf16))
        return lax.dot_general(
            jnp.concatenate(left, 1),
            jnp.concatenate(right, 1),
            (((1,), (1,)), ((), ())),
            preferred_element_type=f32,
        )

    def step(r0, j, x0, n, held, into, extra):
        partial = [None, None]
        z = hidden(x0)
        activate(z, 0, n, into, partial)
        back(r0, j, 0, held)
        activate(z, 1, n, into, partial)
        one = sums(j, 0, held)
        activate(z, 2, n, into, partial)
        back(r0, j, 1, held)
        activate(z, 3, n, into, partial)
        extra()
        two = sums(j, 1, held)
        total[:, 0 : 2 * SROWS] += one + two
        for c in range(2):
            nh[HIDDEN * c : HIDDEN * c + HIDDEN, :] += partial[c]

    partial = [None, None]
    z = hidden(0)
    for r in range(4):
        activate(z, r, [near_rows(c, PADROWS, 8) for c in range(2)], first_buf, partial)
    for c in range(2):
        nh[HIDDEN * c : HIDDEN * c + HIDDEN, :] += partial[c]
    lax.fori_loop(0, SIDE // 8, strip, 0)
    lax.fori_loop(SIDE // 8 - 1, SIDE // 8 + 2, combine, 0)
    turned = total[...].T
    turned = turned + pltpu.roll(turned, HIDDEN, 1)
    pulled = turned[0:SROWS] + turned[SROWS : 2 * SROWS]
    first = (
        wout_ref[0:1, :] * pulled[0:10, 0:HIDDEN] + wout_ref[1:2, :] * pulled[10:20, 0:HIDDEN]
    )
    first = jnp.concatenate([first, jnp.zeros((10, 128 - HIDDEN), f32)], 1)
    second = jnp.sum(nh[...].T, axis=0, keepdims=True)
    message = jnp.concatenate([first, second, jnp.zeros((5, 128), f32)], 0)
    finish(
        shape,
        grad_ref,
        west_ref,
        east_ref,
        message,
        out_ref,
        sums_ref,
        *exchange,
    )


def cell_model(p3, near, first, back, out_weights):
    nx, ny = lax.axis_size("tx"), lax.axis_size("ty")
    dma = pltpu.SemaphoreType.DMA
    rows = SIDE + 16
    return pl.pallas_call(
        functools.partial(cell_kernel, (nx, ny)),
        out_shape=[
            jax.ShapeDtypeStruct((SIDE, SIDE), f32),
            jax.ShapeDtypeStruct((16, 128), f32),
        ],
        in_specs=[pl.BlockSpec(memory_space=pltpu.VMEM)] * 5,
        out_specs=[pl.BlockSpec(memory_space=pltpu.VMEM)] * 2,
        scratch_shapes=[
            pltpu.VMEM((rows, SIDE), f32),
            pltpu.VMEM((rows, 128), f32),
            pltpu.VMEM((rows, 128), f32),
            pltpu.VMEM((4, 128, 128), f32),
            pltpu.VMEM((rows, 16, SIDE), bf16),
            pltpu.VMEM((4, 8 * SROWS, 128), f32),
            pltpu.VMEM((4, (SIDE + 2 * PADROWS) * SROWS, 128), f32),
            pltpu.VMEM((128, 128), f32),
            pltpu.VMEM((128, 128), f32),
            pltpu.VMEM((8 * HIDDEN, SIDE), bf16),
            pltpu.VMEM((8 * HIDDEN, SIDE), bf16),
            pltpu.VMEM((2, 8, SIDE + 256), f32),
            pltpu.VMEM((2, 8, SIDE + 256), f32),
            pltpu.VMEM((2, 8, SIDE), f32),
            pltpu.VMEM((2, 8, SIDE), f32),
            pltpu.VMEM((2, SIDE, 128), f32),
            pltpu.VMEM((nx, 16, 128), f32),
            pltpu.VMEM((ny, 16, 128), f32),
            dma((2,)),
            dma((2,)),
            dma((2,)),
            dma((2,)),
            dma((nx,)),
            dma((nx,)),
            dma((ny,)),
            dma((ny,)),
        ],
        compiler_params=pltpu.CompilerParams(
            vmem_limit_bytes=VMEM_BYTES, collective_id=0, has_side_effects=True
        ),
        name="cell_model",
    )(p3, near, first, back, out_weights)


AROUND = [(dx, dy) for dx in (-1, 0, 1) for dy in (-1, 0, 1) if (dx, dy) != (0, 0)]


def front_kernel(
    shape,
    far_ref,
    pillar_ref,
    ext_ref,
    p3_ref,
    field,
    flat,
    order,
    pieces,
    placed,
    edge_in,
    turned,
    side,
    sends,
    recvs,
):
    nx, ny = shape
    tx = lax.axis_index("tx")
    ty = lax.axis_index("ty")
    barrier = pltpu.get_barrier_semaphore()
    for dx, dy in AROUND:
        pl.semaphore_signal(
            barrier,
            inc=1,
            device_id=(lax.rem(tx + dx + nx, nx), lax.rem(ty + dy + ny, ny)),
            device_id_type=MESH,
        )

    for q in range(4):
        tile = slice(128 * q, 128 * q + 128)
        turned[0, :, tile] = pillar_ref[tile, 0:128].T[0:8]
        turned[1, :, tile] = pillar_ref[tile, SIDE - 128 : SIDE].T[120:128]

    def mark(x, carry):
        r = lax.broadcasted_iota(jnp.int32, (128, 128), 0)
        spot = (r // 16) * 128 + x * 16 + r % 16
        lane = lax.broadcasted_iota(jnp.int32, (128, 128), 1)
        at = pl.ds(pl.multiple_of(x * 128, 128), 128)
        for b in range(8):
            order[at, 128 * b : 128 * b + 128] = jnp.where(
                spot == lane + 128 * b, 1.0, 0.0
            ).astype(bf16)
        return carry

    lax.fori_loop(0, 8, mark, 0)

    def there(dx, dy):
        fits = None
        for delta, index, count in ((dx, tx, nx), (dy, ty, ny)):
            if delta:
                one = index > 0 if delta < 0 else index < count - 1
                fits = one if fits is None else jnp.logical_and(fits, one)
        return fits

    def rim(delta, length, reach):
        if delta < 0:
            return (0, reach), (length, reach)
        if delta > 0:
            return (length - reach, reach), (-reach, reach)
        return (0, length), (0, length)

    def far_copy(n):
        dx, dy = AROUND[n]
        (x, wx), (ox, _) = rim(dx, NB, CONE)
        (y, wy), (oy, _) = rim(dy, NB // 4, CONE // 4)
        return pltpu.make_async_remote_copy(
            src_ref=ext_ref.at[pl.ds(CONE + x, wx), pl.ds(CONE // 4 + y, wy)],
            dst_ref=ext_ref.at[pl.ds(CONE + ox, wx), pl.ds(CONE // 4 + oy, wy)],
            send_sem=sends.at[n],
            recv_sem=recvs.at[n],
            device_id=(tx + dx, ty + dy),
            device_id_type=MESH,
        )

    def edge_copy(n):
        dx, dy = AROUND[n]
        if dy == 0:
            source = pillar_ref.at[pl.ds(0 if dx < 0 else SIDE - 8, 8), :]
        elif dx == 0:
            source = turned.at[0 if dy < 0 else 1]
        else:
            source = pillar_ref.at[
                pl.ds(0 if dx < 0 else SIDE - 8, 8), pl.ds(0 if dy < 0 else SIDE - 128, 128)
            ]
        wide = SIDE if dx == 0 or dy == 0 else 128
        return pltpu.make_async_remote_copy(
            src_ref=source,
            dst_ref=edge_in.at[n, :, pl.ds(0, wide)],
            send_sem=sends.at[8 + n],
            recv_sem=recvs.at[8 + n],
            device_id=(tx + dx, ty + dy),
            device_id_type=MESH,
        )


    def spread(i, carry):
        at = pl.ds(pl.multiple_of(i * BLK, BLK), BLK)
        for c in range(2):
            strip = far_ref[c, at, :].astype(f32)
            for t in range(4):
                field[c, t, at, :] = strip[:, 128 * t : 128 * t + 128]
        return carry

    lax.fori_loop(0, SIDE // BLK, spread, 0)

    def collect(i, carry):
        for j in range(4):
            for t in range(0, 4, 2):
                at = pl.ds(pl.multiple_of(i * 128 + 32 * j + 8 * t, 16), 16)
                for x in range(8):
                    first = i * 128 + 8 * (j % 2) + x
                    two = [field[j // 2, t + s, pl.ds(first, 8, stride=BLK), :] for s in (0, 1)]
                    pieces[at, 128 * x : 128 * x + 128] = jnp.concatenate(two, 0).astype(bf16)
        return carry

    lax.fori_loop(0, NB // 8, collect, 0)
    placed[...] = jnp.dot(pieces[...], order[...], preferred_element_type=f32)

    def turn(i, carry):
        for j in range(4):
            for t in range(4):
                at = pl.ds(pl.multiple_of(i * 128 + 32 * j + 8 * t, 8), 8)
                for b in range(8):
                    flat[pl.ds(i * 1024 + (8 * t + b) * 4 + j, 8, stride=128), :] = placed[
                        at, 128 * b : 128 * b + 128
                    ]
        return carry

    lax.fori_loop(0, NB // 8, turn, 0)

    def pack(r, carry):
        value = flat[pl.ds(pl.multiple_of(r * 128, 128), 128), :].astype(bf16)
        ext_ref[CONE + r, CONE // 4 : CONE // 4 + NB // 4] = value.reshape(NB // 4, 16, 128)
        return carry

    lax.fori_loop(0, NB, pack, 0)
    pl.semaphore_wait(barrier, len(AROUND))
    for n, (dx, dy) in enumerate(AROUND):
        pl.when(there(dx, dy))(lambda n=n: edge_copy(n).start())
    for n, (dx, dy) in enumerate(AROUND):
        pl.when(there(dx, dy))(lambda n=n: far_copy(n).start())

    for n, (dx, dy) in enumerate(AROUND):

        @pl.when(jnp.logical_not(there(dx, dy)))
        def _(n=n, dx=dx, dy=dy):
            edge_in[7 - n] = jnp.zeros((8, SIDE), f32)
            x = {-1: 0, 0: CONE, 1: CONE + NB}[dx]
            y = {-1: 0, 0: CONE // 4, 1: (CONE + NB) // 4}[dy]
            wy = CONE // 4 if dy else NB // 4

            def clear(i, carry):
                ext_ref[x + i, y : y + wy] = jnp.zeros((wy, 16, 128), bf16)
                return carry

            lax.fori_loop(0, CONE if dx else NB, clear, 0)

    for n, (dx, dy) in enumerate(AROUND):
        pl.when(there(dx, dy))(lambda n=n: edge_copy(7 - n).wait_recv())
    at_of = {place: n for n, place in enumerate(AROUND)}

    def got(dx, dy):
        return edge_in.at[7 - at_of[(dx, dy)]]

    for s, dy in ((0, -1), (1, 1)):
        lane = 127 if s == 0 else 0
        side[s, 0:8, :] = jnp.broadcast_to(got(-1, dy)[:, lane : lane + 1], (8, 128))
        side[s, SIDE + 8 : SIDE + 16, :] = jnp.broadcast_to(
            got(1, dy)[:, lane : lane + 1], (8, 128)
        )
        row = 7 if s == 0 else 0
        for q in range(4):
            tile = slice(128 * q, 128 * q + 128)
            side[s, 8 + 128 * q : 136 + 128 * q, :] = jnp.broadcast_to(
                got(0, dy)[row : row + 1, tile], (128, 128)
            ).T

    lanes = lax.broadcasted_iota(jnp.int32, (8, SIDE), 1)

    def shifted(at, value):
        p3_ref[1, at, :] = value
        west = jnp.concatenate([side[0, at, :]] * 4, 1)
        east = jnp.concatenate([side[1, at, :]] * 4, 1)
        p3_ref[0, at, :] = jnp.where(lanes == 0, west, pltpu.roll(value, 1, 1))
        p3_ref[2, at, :] = jnp.where(lanes == SIDE - 1, east, pltpu.roll(value, SIDE - 1, 1))

    def interior(i, carry):
        r0 = pl.multiple_of(i * 8, 8)
        shifted(pl.ds(r0 + 8, 8), pillar_ref[pl.ds(r0, 8), :])
        return carry

    lax.fori_loop(0, SIDE // 8, interior, 0)
    shifted(pl.ds(0, 8), got(-1, 0)[...])
    shifted(pl.ds(SIDE + 8, 8), got(1, 0)[...])

    for n, (dx, dy) in enumerate(AROUND):
        pl.when(there(dx, dy))(lambda n=n: far_copy(7 - n).wait_recv())
    for n, (dx, dy) in enumerate(AROUND):

        @pl.when(there(dx, dy))
        def _(n=n):
            far_copy(n).wait_send()
            edge_copy(n).wait_send()


def front(far, pillar):
    nx, ny = lax.axis_size("tx"), lax.axis_size("ty")
    return pl.pallas_call(
        functools.partial(front_kernel, (nx, ny)),
        out_shape=[
            jax.ShapeDtypeStruct((EXT, EXT // 4, 16, 128), bf16),
            jax.ShapeDtypeStruct((3, SIDE + 16, SIDE), f32),
        ],
        in_specs=[pl.BlockSpec(memory_space=pltpu.VMEM)] * 2,
        out_specs=[pl.BlockSpec(memory_space=pltpu.VMEM)] * 2,
        scratch_shapes=[
            pltpu.VMEM((2, 4, SIDE, 128), f32),
            pltpu.VMEM((NB * NB * 4, 128), f32),
            pltpu.VMEM((1024, 1024), bf16),
            pltpu.VMEM((512, 1024), bf16),
            pltpu.VMEM((512, 1024), f32),
            pltpu.VMEM((8, 8, SIDE), f32),
            pltpu.VMEM((2, 8, SIDE), f32),
            pltpu.VMEM((2, SIDE + 16, 128), f32),
            pltpu.SemaphoreType.DMA((16,)),
            pltpu.SemaphoreType.DMA((16,)),
        ],
        compiler_params=pltpu.CompilerParams(
            vmem_limit_bytes=VMEM_BYTES, collective_id=1, has_side_effects=True
        ),
        name="front",
    )(far, pillar)


def rounded(value):
    return lax.reduce_precision(value, 8, 7)


def first_weights(w_in, b_in):
    w = w_in.reshape(HIDDEN, 3, 3)
    w1 = rounded(w)
    w2 = rounded(w - w1)
    b1 = rounded(b_in)
    b2 = rounded(b_in - b1)
    b3 = b_in - b1 - b2
    cells = jnp.stack([w1, w2, w1, w2, w1], 3).reshape(HIDDEN, 3, 15)
    bias = jnp.stack([b1, b2, b3], 1)[:, :, None]
    one = jnp.concatenate([cells, bias], 2).reshape(HIDDEN, 48)
    return jnp.concatenate(
        [jnp.pad(one, ((0, 0), (16 * r, 48 - 16 * r))) for r in range(4)], 0
    ).astype(bf16)


def back_weights(w_in, w_out):
    v = (w_in.T[None] * w_out[:, None, :]).reshape(18, HIDDEN)
    v1 = rounded(v)
    v2 = v - v1
    wide = jnp.concatenate(
        [
            jnp.pad(jnp.concatenate([v1, v1], 1), ((0, 6), (0, 0))),
            jnp.pad(v2, ((0, 6), (0, HIDDEN))),
        ],
        0,
    )
    upper = jnp.pad(wide, ((0, 0), (0, 2 * HIDDEN)))
    lower = jnp.pad(wide, ((0, 0), (2 * HIDDEN, 0)))
    return jnp.concatenate([upper, lower], 0).astype(bf16)


def local(far_adjoint, pillar, green_blocks, pair_src, pair_dst, group_end, w_in, b_in, w_out):
    ext, p3 = front(far_adjoint, pillar)
    near = sparse_near(
        pair_dst.reshape(-1),
        group_end.reshape(-1),
        pair_src.reshape(-1),
        ext.reshape(EXT * EXT * 4, 128),
        green_blocks,
    )
    grad, sums = cell_model(
        p3,
        near,
        first_weights(w_in, b_in),
        back_weights(w_in, w_out),
        w_out,
    )
    grad, grad_in, grad_bias, grad_out = hand_out(grad, sums)
    return grad, grad_in.T, grad_bias.reshape(HIDDEN), grad_out


def hand_out_kernel(grad_ref, sums_ref, out_ref, first_ref, bias_ref, second_ref):
    out_ref[...] = grad_ref[...]
    value = sums_ref[...]
    first_ref[...] = value[0:9, 0:HIDDEN]
    bias_ref[...] = value[9:10, 0:HIDDEN]
    second_ref[0:1, :] = value[10:11, 0:HIDDEN]
    second_ref[1:2, :] = pltpu.roll(value, HIDDEN, 1)[10:11, 0:HIDDEN]


def hand_out(grad, sums):
    return pl.pallas_call(
        hand_out_kernel,
        out_shape=[
            jax.ShapeDtypeStruct((SIDE, SIDE), f32),
            jax.ShapeDtypeStruct((9, HIDDEN), f32),
            jax.ShapeDtypeStruct((1, HIDDEN), f32),
            jax.ShapeDtypeStruct((2, HIDDEN), f32),
        ],
        in_specs=[pl.BlockSpec(memory_space=pltpu.VMEM)] * 2,
        out_specs=[pl.BlockSpec(memory_space=pltpu.VMEM)] * 4,
        compiler_params=pltpu.CompilerParams(vmem_limit_bytes=VMEM_BYTES),
        name="hand_out",
    )(grad, sums)


def solution(mesh):
    return jax.shard_map(
        local,
        mesh=mesh,
        in_specs=(
            P(None, "tx", "ty"),
            P("tx", "ty"),
            P(),
            P("tx", "ty", None),
            P("tx", "ty", None),
            P("tx", "ty", None),
            P(),
            P(),
            P(),
        ),
        out_specs=(P("tx", "ty"), P(), P(), P()),
        check_vma=False,
    )
```
